32 devices in a mesh: expert: 8 (over z, y), group: 4 (over x, core).
Axes of the slice: x: 2, y: 2, z: 4, core: 2. Of those that a mesh axis runs over, the one named last changes fastest.
Arguments:
- tokens: bfloat16 [4096, 1024], P(('expert', 'group')), may hold values from -6 to 6
- out_grad: bfloat16 [4096, 1024], P(('expert', 'group')), may hold values from -6 to 6
- w_router: bfloat16 [1024, 256], P('group', 'expert'), may hold values from -0.1875 to 0.1875
- w_in: bfloat16 [8, 1024, 2048], P('expert', None, 'group'), may hold values from -0.1875 to 0.1875
- w_out: bfloat16 [8, 2048, 1024], P('expert', 'group'), may hold values from -0.09375 to 0.09375
- expert_ids: int32 [4096, 2], P(('expert', 'group')), may hold values from 0 to 255, as said below
- slot_ids: int32 [4096, 2], P(('expert', 'group')), may hold values from 0 to 1, as said below
- keep_mask: int32 [4096, 2], P(('expert', 'group')), may hold values 0 or 1
Outputs:
- in_grad: bfloat16 [4096, 1024], P(('expert', 'group'))
- w_in_grad: bfloat16 [8, 1024, 2048], P('expert', None, 'group')
- w_out_grad: bfloat16 [8, 2048, 1024], P('expert', 'group')
- router_grad: float32 [1024, 256], P('group', 'expert')
The draws below stay inside these ranges and needn't reach their ends.
Inputs may be any that keep to these rules, and one draw needn't show every extreme that they name: `expert_ids`: the two ids of a token differ. Among the tokens of one device no expert is named more than 2 times, and in every draw some expert below 4 is named 2 times by the tokens of every device. slot_ids[t, 0] is 0; slot_ids[t, 1] is 1 exactly when the second expert of token t is also the first expert of another token of the same device, else 0; so on one device no two choices share both expert and slot.
All inputs are finite; a program needn't handle non-finite values. No bound on the sum of `keep_mask` on one device may be relied on, other than what follows from the above.
Results may differ from the reference program's by a relative error of at most 0.015.
Values may be sent and summed in bfloat16 or wider, within the bound.
A program may use at most 64 MiB of HBM per device.

```python
import jax
import jax.numpy as jnp
from jax import lax

D = 1024
HID = 4096
CANDIDATE_SPECS = 256
TOP = 2
CAP = 2
SPLIT = 2
TOK = 128
RESIDENT_SPECS = 4
HS = 512
TOKENS = 4096
N_GROUP = 4


def route_table(key):
    block_count = TOKENS // TOK
    shared = jax.random.fold_in(key, 7)
    favoured_specialist = jax.random.randint(jax.random.fold_in(shared, 1), (), 0, RESIDENT_SPECS)
    entropy_integers = jax.random.randint(jax.random.fold_in(shared, 2), (CANDIDATE_SPECS,), 0, 8)
    uniform_samples = jnp.arange(CANDIDATE_SPECS, dtype=jnp.int32)
    favour_increment = jnp.where(uniform_samples == favoured_specialist, 2, jnp.where((entropy_integers == 0) & (uniform_samples < RESIDENT_SPECS), 1, 0))
    ordering_perturbation = jax.random.randint(jax.random.fold_in(key, 8), (block_count, CANDIDATE_SPECS), 0, 65536)
    specialist_logit = (favour_increment[None, :] * 65536 + ordering_perturbation) * CANDIDATE_SPECS + uniform_samples[None, :]
    ranking = jnp.argsort(-specialist_logit, axis=1).astype(jnp.int32)
    offsets = jax.random.randint(jax.random.fold_in(key, 9), (block_count, 1), 1, TOK // 2 + 1)
    places = jnp.arange(TOK, dtype=jnp.int32)[None, :]
    first_rank = jnp.broadcast_to(places, (block_count, TOK))
    second_rank = (places - offsets) % CANDIDATE_SPECS
    first_ids = jnp.take_along_axis(ranking, first_rank, axis=1)
    second_ids = jnp.take_along_axis(ranking, second_rank, axis=1)
    second_slot = jnp.broadcast_to((places >= offsets).astype(jnp.int32), (block_count, TOK))
    order_noise = jax.random.randint(jax.random.fold_in(key, 10), (block_count, TOK), 0, 65536) * TOK + places
    shuffle = jnp.argsort(order_noise, axis=1).astype(jnp.int32)
    first_ids = jnp.take_along_axis(first_ids, shuffle, axis=1)
    second_ids = jnp.take_along_axis(second_ids, shuffle, axis=1)
    second_slot = jnp.take_along_axis(second_slot, shuffle, axis=1)
    id_table = jnp.stack([first_ids, second_ids], axis=2).reshape(TOKENS, 2).astype(jnp.int32)
    slot_table = jnp.stack([jnp.zeros_like(second_slot), second_slot], axis=2).reshape(TOKENS, 2).astype(jnp.int32)
    return (id_table, slot_table)


def draw_expert_ids(key, part):
    id_table, slot_table = route_table(key)
    return id_table


def draw_slot_ids(key, part):
    id_table, slot_table = route_table(key)
    return slot_table


def plant(drawn, stream_key, least, high):
    longest = drawn.shape.index(max(drawn.shape))
    spots = []
    for shift in (0, 1):
        where = [jax.random.randint(jax.random.fold_in(stream_key, axis), (), 0, length) for axis, length in enumerate(drawn.shape)]
        where[longest] = (where[longest] + shift) % drawn.shape[longest]
        spots.append(tuple(where))
    return drawn.at[spots[0]].set(least).at[spots[1]].set(high)


def shard_levels(own_key, dims, shards, least, top_value):
    loudness, own = 1.0, jax.random.fold_in(own_key, 6)
    for position, blocks in shards:
        steps = jnp.exp(jax.random.uniform(jax.random.fold_in(own, position), (blocks,), jnp.float32, least / len(shards), top_value / len(shards)))
        loudness = loudness * jnp.repeat(steps, dims[position] // blocks).reshape([-1 if axis == position else 1 for axis in range(len(dims))])
    return loudness


def noise(key, dims, width, limit, pieces=(), kind=jnp.bfloat16):
    gain = shard_levels(key, dims, pieces, -0.22, 0.18) if pieces else 1.0
    drawn = jax.random.normal(key, dims, jnp.float32) * width * gain
    return jnp.minimum(jnp.maximum(drawn, -limit), limit).astype(kind)


def setup_inputs(seed: int = 0) -> dict:
    streams_of = jax.random.split(jax.random.key(seed), 9)
    tokens = noise(streams_of[0], (TOKENS, D), 1.0, 6.0, ((0, 32),))
    out_grad = noise(streams_of[1], (TOKENS, D), 1.0, 6.0, ((0, 32),))
    w_router = noise(streams_of[2], (D, CANDIDATE_SPECS), D ** -0.5, 0.1875, ((0, 4), (1, 8)))
    w_in = noise(streams_of[3], (RESIDENT_SPECS * SPLIT, D, HID // SPLIT), D ** -0.5, 0.1875, ((0, 8), (2, 4)))
    w_out = noise(streams_of[4], (RESIDENT_SPECS * SPLIT, HID // SPLIT, D), HID ** -0.5, 0.09375, ((0, 8), (1, 4)))
    expert_ids = draw_expert_ids(jax.random.fold_in(streams_of[8], 71), 0)
    slot_ids = draw_slot_ids(jax.random.fold_in(streams_of[8], 71), 0)
    keep_mask = plant((jax.random.randint(streams_of[7], (TOKENS, TOP), 0, 5) < 4).astype(jnp.int32), jax.random.fold_in(streams_of[7], 1), 0, 1)
    return dict(tokens=tokens, out_grad=out_grad, w_router=w_router, w_in=w_in, w_out=w_out, expert_ids=expert_ids, slot_ids=slot_ids, keep_mask=keep_mask)


def gelu_parts(pre_act):
    cubic_term = 0.044715 * pre_act * pre_act * pre_act
    tanh_value = jnp.tanh(0.7978845608028654 * (pre_act + cubic_term))
    gelu_value = 0.5 * pre_act * (1.0 + tanh_value)
    gelu_slope = 0.5 * (1.0 + tanh_value) + 0.5 * pre_act * (1.0 - tanh_value * tanh_value) * 0.7978845608028654 * (1.0 + 3.0 * 0.044715 * pre_act * pre_act)
    return gelu_value, gelu_slope


def expert_backward(inputs):
    x_rows, dy_rows, gate_rows, in_blocks, out_blocks = inputs
    x_wide = x_rows.astype(jnp.float32)
    dy_wide = dy_rows.astype(jnp.float32)
    in_wide = in_blocks.astype(jnp.float32)
    out_wide = out_blocks.astype(jnp.float32)
    gate_wide = gate_rows.astype(jnp.float32)
    pre_act = jnp.einsum("rd,bdh->brh", x_wide, in_wide, precision=lax.Precision.HIGHEST)
    gelu_value, gelu_slope = gelu_parts(pre_act)
    back_up = jnp.einsum("rd,bhd->brh", dy_wide, out_wide, precision=lax.Precision.HIGHEST)
    gate_grad = jnp.sum(jnp.sum(back_up * gelu_value, axis=2), axis=0)
    pre_grad = lax.optimization_barrier((gate_wide[None, :, None] * back_up * gelu_slope).astype(jnp.bfloat16))
    scaled_grad = lax.optimization_barrier((gate_wide[:, None] * dy_wide).astype(jnp.bfloat16))
    hidden_round = lax.optimization_barrier(gelu_value.astype(jnp.bfloat16))
    grad_in = jnp.einsum("rd,brh->bdh", x_wide, pre_grad.astype(jnp.float32), precision=lax.Precision.HIGHEST).astype(jnp.bfloat16)
    grad_out = jnp.einsum("brh,rd->bhd", hidden_round.astype(jnp.float32), scaled_grad.astype(jnp.float32), precision=lax.Precision.HIGHEST).astype(jnp.bfloat16)
    row_parts = lax.optimization_barrier(jnp.einsum("brh,bdh->brd", pre_grad.astype(jnp.float32), in_wide, precision=lax.Precision.HIGHEST).astype(jnp.bfloat16))
    row_grad = jnp.sum(row_parts.astype(jnp.float32), axis=0)
    return row_grad, gate_grad, grad_in, grad_out


def reference(tokens, out_grad, w_router, w_in, w_out, expert_ids, slot_ids, keep_mask):
    total_rows = tokens.shape[0]
    block_count = total_rows // TOK
    row_count = block_count * CAP
    logits = jnp.dot(tokens, w_router, preferred_element_type=jnp.float32)
    chosen = jnp.take_along_axis(logits, expert_ids, axis=1)
    logit_gap = chosen[:, 0] - chosen[:, 1]
    combine = jnp.stack([jax.nn.sigmoid(logit_gap), jax.nn.sigmoid(-logit_gap)], axis=1)
    active = (keep_mask == 1) & (expert_ids < RESIDENT_SPECS)
    rows_index = ((jnp.arange(total_rows, dtype=jnp.int32) // TOK)[:, None] * CAP + slot_ids).astype(jnp.int32)
    target = jnp.where(active, expert_ids, RESIDENT_SPECS).astype(jnp.int32)
    x_buf = jnp.zeros((RESIDENT_SPECS, row_count, D), jnp.bfloat16).at[target, rows_index].set(jnp.broadcast_to(tokens[:, None, :], (total_rows, TOP, D)), mode="drop")
    dy_buf = jnp.zeros((RESIDENT_SPECS, row_count, D), jnp.bfloat16).at[target, rows_index].set(jnp.broadcast_to(out_grad[:, None, :], (total_rows, TOP, D)), mode="drop")
    gate_buf = jnp.zeros((RESIDENT_SPECS, row_count), jnp.bfloat16).at[target, rows_index].set(combine.astype(jnp.bfloat16), mode="drop")
    in_blocks = w_in.reshape(RESIDENT_SPECS, SPLIT, D, N_GROUP, HS).transpose(0, 1, 3, 2, 4).reshape(RESIDENT_SPECS, SPLIT * N_GROUP, D, HS)
    out_blocks = w_out.reshape(RESIDENT_SPECS, SPLIT * N_GROUP, HS, D)
    row_grad, gate_grad, grad_in, grad_out = lax.map(expert_backward, (x_buf, dy_buf, gate_buf, in_blocks, out_blocks))
    w_in_grad = grad_in.reshape(RESIDENT_SPECS, SPLIT, N_GROUP, D, HS).transpose(0, 1, 3, 2, 4).reshape(RESIDENT_SPECS * SPLIT, D, HID // SPLIT)
    w_out_grad = grad_out.reshape(RESIDENT_SPECS * SPLIT, HID // SPLIT, D)
    safe_target = jnp.minimum(target, RESIDENT_SPECS - 1).astype(jnp.int32)
    picked_rows = row_grad[safe_target, rows_index]
    expert_part = jnp.sum(jnp.where(active[:, :, None], picked_rows, jnp.float32(0.0)), axis=1)
    gate_back = jnp.where(active, gate_grad[safe_target, rows_index], jnp.float32(0.0))
    gate_slope = combine[:, 0] * combine[:, 1] * (gate_back[:, 0] - gate_back[:, 1])
    uniform_samples = jnp.arange(CANDIDATE_SPECS, dtype=jnp.int32)
    first_hot = (expert_ids[:, 0:1] == uniform_samples[None, :]).astype(jnp.float32)
    second_hot = (expert_ids[:, 1:2] == uniform_samples[None, :]).astype(jnp.float32)
    logit_grad = first_hot * gate_slope[:, None] - second_hot * gate_slope[:, None]
    router_part = jnp.dot(logit_grad, w_router.astype(jnp.float32).T, precision=lax.Precision.HIGHEST)
    in_grad = (expert_part + router_part).astype(jnp.bfloat16)
    router_grad = jnp.dot(tokens.astype(jnp.float32).T, logit_grad, precision=lax.Precision.HIGHEST)
    return (in_grad, w_in_grad, w_out_grad, router_grad)
```

```python
import functools

import jax
import jax.numpy as jnp
from jax import lax
from jax.experimental import pallas as pl
from jax.experimental.pallas import tpu as pltpu
from jax.sharding import PartitionSpec as P

CAP = 2
SPLIT = 2
LANES = 128
F32 = jnp.float32
BF16 = jnp.bfloat16
MESH = pl.DeviceIdType.MESH


def gelu_parts(pre_act):
    cubic_term = 0.044715 * pre_act * pre_act * pre_act
    tanh_value = jnp.tanh(0.7978845608028654 * (pre_act + cubic_term))
    gelu_value = 0.5 * pre_act * (1.0 + tanh_value)
    gelu_slope = 0.5 * (1.0 + tanh_value) + 0.5 * pre_act * (
        1.0 - tanh_value * tanh_value
    ) * 0.7978845608028654 * (1.0 + 3.0 * 0.044715 * pre_act * pre_act)
    return (gelu_value, gelu_slope)


def expert_rows(w_in_local, w_out_local, pieces):
    x_piece, dy_piece, gate_piece = pieces
    gate_col = gate_piece.astype(jnp.float32)[:, None]
    pre_act = jnp.dot(x_piece, w_in_local, preferred_element_type=jnp.float32)
    gelu_value, gelu_slope = gelu_parts(pre_act)
    back_up = jnp.einsum("rd,hd->rh", dy_piece, w_out_local, preferred_element_type=jnp.float32)
    gate_piece_sum = jnp.sum(back_up * gelu_value, axis=1)
    pre_grad = (gate_col * back_up * gelu_slope).astype(jnp.bfloat16)
    scaled_grad = (gate_col * dy_piece.astype(jnp.float32)).astype(jnp.bfloat16)
    sum_in = jnp.einsum("rd,rh->dh", x_piece, pre_grad, preferred_element_type=jnp.float32)
    sum_out = jnp.einsum(
        "rh,rd->hd",
        gelu_value.astype(jnp.bfloat16),
        scaled_grad,
        preferred_element_type=jnp.float32,
    )
    part_rows = jnp.einsum("rh,dh->rd", pre_grad, w_in_local, preferred_element_type=jnp.float32)
    return (sum_in, sum_out, part_rows, gate_piece_sum)


def gathered_body(tokens, out_grad, w_router, w_in, w_out, expert_ids, slot_ids, keep_mask):
    expert_count = lax.axis_size("expert")
    window = expert_count // SPLIT
    slot_count = window * CAP
    model_width = tokens.shape[1]
    router_full = lax.all_gather(
        lax.all_gather(w_router, "expert", axis=1, tiled=True), "group", axis=0, tiled=True
    )
    logits = jnp.dot(tokens, router_full, preferred_element_type=jnp.float32)
    uniform_samples = jnp.arange(router_full.shape[1], dtype=jnp.int32)
    first_hot = (expert_ids[:, 0:1] == uniform_samples[None, :]).astype(jnp.float32)
    second_hot = (expert_ids[:, 1:2] == uniform_samples[None, :]).astype(jnp.float32)
    logit_gap = jnp.sum(logits * first_hot, axis=1) - jnp.sum(logits * second_hot, axis=1)
    combine = jnp.stack([jax.nn.sigmoid(logit_gap), jax.nn.sigmoid(-logit_gap)], axis=1)
    active = (keep_mask == 1) & (expert_ids < window)
    slot_code = jnp.where(active, expert_ids * CAP + slot_ids, -1)
    slot_axis = jnp.arange(slot_count, dtype=jnp.int32)
    place_first = (slot_code[:, 0:1] == slot_axis[None, :]).astype(jnp.float32)
    place_second = (slot_code[:, 1:2] == slot_axis[None, :]).astype(jnp.float32)
    placement = place_first + place_second
    place_round = placement.astype(jnp.bfloat16)
    token_slots = jnp.einsum(
        "ts,td->sd", place_round, tokens, preferred_element_type=jnp.float32
    ).astype(jnp.bfloat16)
    grad_slots = jnp.einsum(
        "ts,td->sd", place_round, out_grad, preferred_element_type=jnp.float32
    ).astype(jnp.bfloat16)
    gate_slots = jnp.sum(
        place_first * combine[:, 0:1] + place_second * combine[:, 1:2], axis=0
    ).astype(jnp.bfloat16)
    token_send = jnp.repeat(token_slots.reshape(window, CAP, model_width), SPLIT, axis=0)
    grad_send = jnp.repeat(grad_slots.reshape(window, CAP, model_width), SPLIT, axis=0)
    gate_send = jnp.repeat(gate_slots.reshape(window, CAP), SPLIT, axis=0)
    token_recv, grad_recv, gate_recv = (
        lax.all_to_all(token_send, "expert", split_axis=0, concat_axis=0, tiled=True),
        lax.all_to_all(grad_send, "expert", split_axis=0, concat_axis=0, tiled=True),
        lax.all_to_all(gate_send, "expert", split_axis=0, concat_axis=0, tiled=True),
    )
    row_count = expert_count * CAP
    token_rows = token_recv.reshape(row_count, model_width)
    grad_rows = grad_recv.reshape(row_count, model_width)
    gate_rows = gate_recv.reshape(row_count)
    w_in_local = w_in[0]
    w_out_local = w_out[0]
    sum_in, sum_out, row_parts, gate_parts = expert_rows(
        w_in_local,
        w_out_local,
        (
            lax.all_gather(token_rows, "group", axis=0, tiled=True),
            lax.all_gather(grad_rows, "group", axis=0, tiled=True),
            lax.all_gather(gate_rows, "group", axis=0, tiled=True),
        ),
    )
    w_in_grad = sum_in.astype(jnp.bfloat16)[None]
    w_out_grad = sum_out.astype(jnp.bfloat16)[None]
    row_sums = lax.psum_scatter(
        row_parts.astype(jnp.bfloat16), "group", scatter_dimension=0, tiled=True
    ).astype(jnp.float32)
    gate_sums = lax.psum_scatter(gate_parts, "group", scatter_dimension=0, tiled=True)
    rows_back, gates_back = (
        lax.all_to_all(
            row_sums.reshape(expert_count, CAP, model_width).astype(jnp.bfloat16),
            "expert",
            split_axis=0,
            concat_axis=0,
            tiled=True,
        ).astype(jnp.float32),
        lax.all_to_all(
            gate_sums.reshape(expert_count, CAP).astype(jnp.bfloat16),
            "expert",
            split_axis=0,
            concat_axis=0,
            tiled=True,
        ).astype(jnp.float32),
    )
    rows_back = jnp.sum(rows_back.reshape(window, SPLIT, CAP, model_width), axis=1).reshape(
        slot_count, model_width
    )
    gates_back = jnp.sum(gates_back.reshape(window, SPLIT, CAP), axis=1).reshape(slot_count)
    expert_part = jnp.dot(placement, rows_back, precision=lax.Precision.HIGHEST)
    gate_first = jnp.sum(place_first * gates_back[None, :], axis=1)
    gate_second = jnp.sum(place_second * gates_back[None, :], axis=1)
    gate_slope = combine[:, 0] * combine[:, 1] * (gate_first - gate_second)
    logit_grad = first_hot * gate_slope[:, None] - second_hot * gate_slope[:, None]
    router_part = jnp.dot(
        logit_grad, router_full.astype(jnp.float32).T, precision=lax.Precision.HIGHEST
    )
    in_grad = (expert_part + router_part).astype(jnp.bfloat16)
    router_sum = jnp.dot(tokens.astype(jnp.float32).T, logit_grad, precision=lax.Precision.HIGHEST)
    router_grad = lax.psum_scatter(
        lax.psum_scatter(router_sum, "expert", scatter_dimension=1, tiled=True),
        "group",
        scatter_dimension=0,
        tiled=True,
    )
    return (in_grad, w_in_grad, w_out_grad, router_grad)


def iota(shape, axis):
    return lax.broadcasted_iota(jnp.int32, shape, axis)


def one_hot(mask):
    return jnp.where(mask, 1.0, 0.0).astype(F32)


def contract(left, right, left_axis, right_axis):
    return lax.dot_general(
        left, right, (((left_axis,), (right_axis,)), ((), ())), preferred_element_type=F32
    )


def fused_kernel(
    window,
    groups,
    tokens_hbm,
    out_grad_hbm,
    router_ref,
    w_in_hbm,
    w_out_hbm,
    ids_ref,
    slots_ref,
    keep_ref,
    in_grad_ref,
    w_in_grad_hbm,
    w_out_grad_hbm,
    router_grad_ref,
    tok,
    outg,
    w1,
    w2,
    g1,
    g2,
    z_send,
    z_recv,
    w_recv,
    pack,
    xs,
    gv_send,
    gv_recv,
    gg,
    rp_send,
    rp_recv,
    coef_ref,
    rg_send,
    rg_recv,
    ret_send,
    ret_recv,
    load_sems,
    store_sems,
    zs,
    zr,
    ws,
    wr,
    pks,
    pkr,
    gvs,
    gvr,
    ggs,
    ggr,
    rps,
    rpr,
    rgs,
    rgr,
    rts,
    rtr,
):
    plane = SPLIT * groups
    width = tok.shape[1]
    chunks = width // LANES
    rows = window * CAP
    message = z_send.shape[1]
    used = CAP * (2 * chunks + 1)
    columns, depth = router_ref.shape
    ix = lax.axis_index("expert")
    g = lax.axis_index("group")
    z = ix // SPLIT
    y = lax.rem(ix, SPLIT)
    q = y * groups + g

    def z_up(d):
        return (lax.rem(z + d, window) * SPLIT + y, g)

    def z_down(d):
        return (lax.rem(z + window - d, window) * SPLIT + y, g)

    def in_plane(p):
        return (z * SPLIT + p // groups, lax.rem(p, groups))

    def q_up(d):
        return lax.rem(q + d, plane)

    def q_down(d):
        return lax.rem(q + plane - d, plane)

    def remote(src, dst, send_sems, recv_sems, d, target):
        return pltpu.make_async_remote_copy(
            src_ref=src,
            dst_ref=dst,
            send_sem=send_sems.at[d],
            recv_sem=recv_sems.at[d],
            device_id=target,
            device_id_type=MESH,
        )

    loads = [
        pltpu.make_async_copy(src, dst, load_sems.at[i])
        for i, (src, dst) in enumerate(
            [
                (tokens_hbm, tok),
                (out_grad_hbm, outg),
                (w_in_hbm.at[0], w1),
                (w_out_hbm.at[0], w2),
            ]
        )
    ]
    for load in loads:
        load.start()

    barrier = pltpu.get_barrier_semaphore()
    for d in range(1, window):
        pl.semaphore_signal(barrier, inc=1, device_id=z_up(d), device_id_type=MESH)
    for d in range(1, plane):
        pl.semaphore_signal(barrier, inc=1, device_id=in_plane(q_up(d)), device_id_type=MESH)

    places = []
    for k in range(2):
        ids = ids_ref[k : k + 1, :]
        relative = jnp.where(ids < z, ids - z + window, ids - z)
        active = (keep_ref[k : k + 1, :] == 1) & (ids < window)
        code = jnp.where(active, relative * CAP + slots_ref[k : k + 1, :], -1)
        places.append(one_hot(iota((LANES, LANES), 0) == code))
    place = places[0] + places[1]
    place_rows = place[:16].astype(BF16)
    short = place[:rows]
    first_id = jnp.sum(short * ids_ref[0:1, :].astype(F32), axis=1, keepdims=True)
    second_id = jnp.sum(short * ids_ref[1:2, :].astype(F32), axis=1, keepdims=True)
    which = jnp.sum(places[0][:rows] - places[1][:rows], axis=1, keepdims=True)
    lane = iota((rows, LANES), 1)
    meta = jnp.where(
        lane == 0, first_id, jnp.where(lane == 1, second_id, jnp.where(lane == 2, which, 0.0))
    )

    loads[0].wait()
    loads[1].wait()
    x_slots = contract(place_rows, tok[...], 1, 0)[:rows]
    dy_slots = contract(place_rows, outg[...], 1, 0)[:rows]
    pieces = [x_slots[:, c * LANES : (c + 1) * LANES] for c in range(chunks)]
    pieces += [dy_slots[:, c * LANES : (c + 1) * LANES] for c in range(chunks)]
    pieces += [meta, jnp.zeros((rows, LANES), F32)]
    folded = jnp.concatenate(pieces, axis=0).astype(BF16)
    depth_f = folded.shape[0]
    spread = []
    for d in range(window):
        row = iota((message, depth_f), 0)
        source = (row >> 1) * rows + d * CAP + (row & 1)
        spread.append(one_hot((iota((message, depth_f), 1) == source) & (row < used)))
    messages = contract(jnp.concatenate(spread, axis=0).astype(BF16), folded, 1, 0).astype(BF16)
    z_recv[0] = messages[:message]
    for d in range(1, window):
        z_send[d] = messages[d * message : (d + 1) * message]
    w_recv[0] = router_ref[...]

    pl.semaphore_wait(barrier, window - 1 + plane - 1)

    z_copies, w_copies = [], []
    for d in range(1, window):
        z_copies.append(remote(z_send.at[d], z_recv.at[d], zs, zr, d, z_up(d)))
        z_copies[-1].start()
    for d in range(1, window):
        w_copies.append(remote(router_ref, w_recv.at[d], ws, wr, d, z_up(d)))
        w_copies[-1].start()

    wide = (chunks + 1) * 16
    row = iota((wide, window * message), 0)
    inner = row & 15
    chunk = row >> 4
    block = jnp.where((inner < rows) & (chunk < chunks), chunk, chunk + chunks)
    source = ((inner & (rows - 1)) >> 1) * message + block * CAP + (inner & 1)
    gather = one_hot(iota((wide, window * message), 1) == source).astype(BF16)
    for copy in z_copies:
        copy.wait_recv()
    gathered = contract(
        gather, z_recv[...].reshape(window * message, LANES), 1, 0
    ).astype(BF16)
    for c in range(chunks + 1):
        pack[q, :, c * LANES : (c + 1) * LANES] = gathered[c * 16 : (c + 1) * 16]

    def all_plane(src, dst_of, send_sems, recv_sems):
        copies = []
        for d in range(1, plane):
            target = q_up(d)
            copies.append(
                remote(src(target), dst_of(q), send_sems, recv_sems, d, in_plane(target))
            )
            copies[-1].start()
        arrivals = [
            remote(src(q_up(d)), dst_of(q_down(d)), send_sems, recv_sems, d, in_plane(q_up(d)))
            for d in range(1, plane)
        ]
        return copies, arrivals

    pk_copies, pk_arrivals = all_plane(lambda p: pack.at[q], lambda p: pack.at[p], pks, pkr)

    for copy in w_copies:
        copy.wait_recv()
    router = w_recv[...].reshape(window * columns, depth)
    for copy in pk_arrivals:
        copy.wait_recv()

    total = plane * rows
    everything = pack[...].astype(F32)
    x_rows = everything[:, :rows, :width].reshape(total, width).astype(BF16)
    dy_rows = everything[:, rows:, :width].reshape(total, width).astype(BF16)
    info = everything[:, :rows, width:].reshape(total, LANES)
    xs[...] = x_rows
    x_part = xs[:, pl.ds(pl.multiple_of(g * depth, LANES), depth)]

    column = iota((total, window * columns), 1)
    owner = lax.rem(z + window - column // columns, window)
    column_id = ((owner * SPLIT + y) * columns + lax.rem(column, columns)).astype(F32)
    hot = one_hot(info[:, 0:1] == column_id) - one_hot(info[:, 1:2] == column_id)
    sign = info[:, 2:3]
    gap_part = jnp.sum(contract(x_part, router, 1, 1) * hot, axis=1, keepdims=True)
    row_diff = contract(hot.astype(BF16), router, 1, 0)
    eye = iota((total, LANES), 0) == iota((total, LANES), 1)
    gap_row = jnp.sum(jnp.where(eye, gap_part, 0.0), axis=0, keepdims=True)
    gv_send[:, :, :depth] = row_diff.reshape(plane, rows, depth)
    gv_send[:, :, depth:] = jnp.broadcast_to(gap_row[None], (plane, rows, LANES))
    gv_recv[q] = gv_send[q]
    gv_copies, gv_arrivals = all_plane(
        lambda p: gv_send.at[p], lambda p: gv_recv.at[p], gvs, gvr
    )

    loads[3].wait()
    back_up = contract(dy_rows, w2[...], 1, 1)
    loads[2].wait()
    pre_act = contract(x_rows, w1[...], 1, 0)
    gelu_value, gelu_slope = gelu_parts(pre_act)
    gate_part = jnp.sum(back_up * gelu_value, axis=1, keepdims=True)
    gate_row = jnp.sum(jnp.where(eye, gate_part, 0.0), axis=0, keepdims=True)
    gg[q] = jnp.broadcast_to(gate_row, (rows, LANES))
    gg_copies, gg_arrivals = all_plane(lambda p: gg.at[q], lambda p: gg.at[p], ggs, ggr)

    for copy in gv_arrivals:
        copy.wait_recv()
    gap_sum = jnp.sum(gv_recv[:, 0:1, depth:], axis=0)
    gap = jnp.sum(jnp.where(eye, gap_sum, 0.0), axis=1, keepdims=True)
    combine_first = jax.nn.sigmoid(gap)
    combine_second = jax.nn.sigmoid(-gap)
    gate = jnp.where(sign > 0.5, combine_first, jnp.where(sign < -0.5, combine_second, 0.0))
    gate = gate.astype(BF16).astype(F32)
    pre_grad = (gate * back_up * gelu_slope).astype(BF16)
    part_rows = contract(pre_grad, w1[...], 1, 1).reshape(plane, rows, width)
    half = width // 2
    rp_send[...] = jnp.concatenate(
        [part_rows[:, :, :half], part_rows[:, :, half:]], axis=1
    ).astype(BF16)
    rp_recv[q] = rp_send[q]
    rp_copies, rp_arrivals = all_plane(
        lambda p: rp_send.at[p], lambda p: rp_recv.at[p], rps, rpr
    )

    for copy in gg_arrivals:
        copy.wait_recv()
    grad_sum = jnp.sum(gg[:, 0:1, :], axis=0)
    gate_grad = jnp.sum(jnp.where(eye, grad_sum, 0.0), axis=1, keepdims=True)
    coef = sign * combine_first * combine_second * gate_grad
    coef_ref[...] = jnp.broadcast_to(coef, (total, LANES))
    logit_grad = coef * hot
    high = logit_grad.astype(BF16)
    low = (logit_grad - high.astype(F32)).astype(BF16)
    router_part = contract(
        jnp.concatenate([high, low], axis=0), jnp.concatenate([x_part, x_part], axis=0), 0, 0
    )
    for d in range(1, window):
        rg_send[d] = router_part[d * columns : (d + 1) * columns].astype(BF16)
    rg_copies = []
    for d in range(1, window):
        rg_copies.append(remote(rg_send.at[d], rg_recv.at[d], rgs, rgr, d, z_down(d)))
        rg_copies[-1].start()

    g1[...] = contract(x_rows, pre_grad, 0, 0).astype(BF16)
    stores = [pltpu.make_async_copy(g1, w_in_grad_hbm.at[0], store_sems.at[0])]
    stores[0].start()
    scaled_grad = (gate * dy_rows.astype(F32)).astype(BF16)
    g2[...] = contract(gelu_value.astype(BF16), scaled_grad, 0, 0).astype(BF16)
    stores.append(pltpu.make_async_copy(g2, w_out_grad_hbm.at[0], store_sems.at[1]))
    stores[1].start()

    for copy in rp_arrivals:
        copy.wait_recv()
    summed = jnp.sum(rp_recv[...].astype(F32), axis=0)
    row_grad = jnp.concatenate([summed[:rows], summed[rows:]], axis=1)
    diffs = []
    for part in range(groups):
        diff = gv_recv[part, :, :depth]
        for other in range(1, SPLIT):
            diff = diff + gv_recv[other * groups + part, :, :depth]
        diffs.append(diff)
    own_coef = coef_ref[pl.ds(pl.multiple_of(q * rows, rows), rows), 0:1]
    row_grad = row_grad + own_coef * jnp.concatenate(diffs, axis=1)
    folded = jnp.concatenate(
        [row_grad[:, c * LANES : (c + 1) * LANES] for c in range(chunks)], axis=0
    ).astype(BF16)
    back = chunks * rows
    row = iota((back, back), 0)
    source = ((row >> 1) & (chunks - 1)) * rows + (row >> 4) * CAP + (row & 1)
    fold = one_hot(iota((back, back), 1) == source).astype(BF16)
    ret_send[...] = contract(fold, folded, 1, 0).astype(BF16).reshape(ret_send.shape)
    ret_recv[0] = ret_send[0]
    ret_copies = []
    for d in range(1, window):
        ret_copies.append(remote(ret_send.at[d], ret_recv.at[d], rts, rtr, d, z_down(d)))
        ret_copies[-1].start()

    spread_back = jnp.transpose(place).astype(BF16)
    for copy in rg_copies:
        copy.wait_recv()
    router_grad_ref[...] = router_part[:columns] + jnp.sum(
        rg_recv[1:].astype(F32), axis=0
    )

    source = ((row >> 1) & (window - 1)) * 16 + (row >> 3) * CAP + (row & 1)
    unfold = one_hot(iota((back, back), 1) == source).astype(BF16)
    for copy in ret_copies:
        copy.wait_recv()
    flat = contract(unfold, ret_recv[...].reshape(back, LANES), 1, 0)
    returned = jnp.concatenate(
        [flat[c * rows : (c + 1) * rows] for c in range(chunks)], axis=1
    )
    returned = jnp.concatenate([returned, jnp.zeros((LANES - rows, width), F32)], axis=0)
    in_grad_ref[...] = contract(spread_back, returned.astype(BF16), 1, 0).astype(BF16)

    for group in (z_copies, w_copies, pk_copies, gv_copies, gg_copies, rp_copies, rg_copies, ret_copies):
        for copy in group:
            copy.wait_send()
    for store in stores:
        store.wait()


def fused(tokens, out_grad, w_router, w_in, w_out, expert_ids, slot_ids, keep_mask):
    window = lax.axis_size("expert") // SPLIT
    groups = lax.axis_size("group")
    plane = SPLIT * groups
    count, width = tokens.shape
    hidden = w_in.shape[2]
    depth, columns = w_router.shape
    rows = window * CAP
    message = -(-CAP * (2 * width // LANES + 1) // 16) * 16
    vmem = pl.BlockSpec(memory_space=pltpu.VMEM)
    hbm = pl.BlockSpec(memory_space=pl.ANY)
    dma = pltpu.SemaphoreType.DMA
    in_grad, w_in_grad, w_out_grad, router_grad = pl.pallas_call(
        functools.partial(fused_kernel, window, groups),
        out_shape=(
            jax.ShapeDtypeStruct((count, width), BF16),
            jax.ShapeDtypeStruct(w_in.shape, BF16),
            jax.ShapeDtypeStruct(w_out.shape, BF16),
            jax.ShapeDtypeStruct((columns, depth), F32),
        ),
        in_specs=[hbm, hbm, vmem, hbm, hbm, vmem, vmem, vmem],
        out_specs=(vmem, hbm, hbm, vmem),
        scratch_shapes=[
            pltpu.VMEM((count, width), BF16),
            pltpu.VMEM((count, width), BF16),
            pltpu.VMEM((width, hidden), BF16),
            pltpu.VMEM((hidden, width), BF16),
            pltpu.VMEM((width, hidden), BF16),
            pltpu.VMEM((hidden, width), BF16),
            pltpu.VMEM((window, message, LANES), BF16),
            pltpu.VMEM((window, message, LANES), BF16),
            pltpu.VMEM((window, columns, depth), BF16),
            pltpu.VMEM((plane, 16, width + LANES), BF16),
            pltpu.VMEM((plane * rows, width), BF16),
            pltpu.VMEM((plane, rows, depth + LANES), F32),
            pltpu.VMEM((plane, rows, depth + LANES), F32),
            pltpu.VMEM((plane, rows, LANES), F32),
            pltpu.VMEM((plane, 16, width // 2), BF16),
            pltpu.VMEM((plane, 16, width // 2), BF16),
            pltpu.VMEM((plane * rows, LANES), F32),
            pltpu.VMEM((window, columns, depth), BF16),
            pltpu.VMEM((window, columns, depth), BF16),
            pltpu.VMEM((window, 16, LANES), BF16),
            pltpu.VMEM((window, 16, LANES), BF16),
            dma((4,)),
            dma((2,)),
        ]
        + [dma((window,))] * 4
        + [dma((plane,))] * 8
        + [dma((window,))] * 4,
        compiler_params=pltpu.CompilerParams(
            collective_id=0, has_side_effects=True, vmem_limit_bytes=40 * 1024 * 1024
        ),
    )(
        tokens,
        out_grad,
        w_router.T,
        w_in,
        w_out,
        expert_ids.T,
        slot_ids.T,
        keep_mask.T,
    )
    return (in_grad, w_in_grad, w_out_grad, router_grad.T)


def body(*args):
    tokens, _, w_router = args[:3]
    window = lax.axis_size("expert") // SPLIT
    fits = (
        window * CAP == 8
        and w_router.shape[1] % 16 == 0
        and w_router.shape[0] % LANES == 0
        and window * w_router.shape[1] == LANES
        and SPLIT * lax.axis_size("group") * window * CAP <= LANES
        and tokens.shape == (LANES, 8 * LANES)
    )
    return fused(*args) if fits else gathered_body(*args)


def solution(mesh):
    return jax.shard_map(
        body,
        mesh=mesh,
        in_specs=(
            P(("expert", "group"), None),
            P(("expert", "group"), None),
            P("group", "expert"),
            P("expert", None, "group"),
            P("expert", "group", None),
            P(("expert", "group"), None),
            P(("expert", "group"), None),
            P(("expert", "group"), None),
        ),
        out_specs=(
            P(("expert", "group"), None),
            P("expert", None, "group"),
            P("expert", "group", None),
            P("group", "expert"),
        ),
        check_vma=False,
    )
```

```python
import functools

import jax
import jax.numpy as jnp
from jax import lax
from jax.experimental import pallas as pl
from jax.experimental.pallas import tpu as pltpu
from jax.sharding import PartitionSpec as P

CAP = 2
SPLIT = 2
LANES = 128
F32 = jnp.float32
BF16 = jnp.bfloat16
MESH = pl.DeviceIdType.MESH


def gelu_parts(pre_act):
    cubic_term = 0.044715 * pre_act * pre_act * pre_act
    tanh_value = jnp.tanh(0.7978845608028654 * (pre_act + cubic_term))
    gelu_value = 0.5 * pre_act * (1.0 + tanh_value)
    gelu_slope = 0.5 * (1.0 + tanh_value) + 0.5 * pre_act * (
        1.0 - tanh_value * tanh_value
    ) * 0.7978845608028654 * (1.0 + 3.0 * 0.044715 * pre_act * pre_act)
    return (gelu_value, gelu_slope)


def expert_rows(w_in_local, w_out_local, pieces):
    x_piece, dy_piece, gate_piece = pieces
    gate_col = gate_piece.astype(jnp.float32)[:, None]
    pre_act = jnp.dot(x_piece, w_in_local, preferred_element_type=jnp.float32)
    gelu_value, gelu_slope = gelu_parts(pre_act)
    back_up = jnp.einsum("rd,hd->rh", dy_piece, w_out_local, preferred_element_type=jnp.float32)
    gate_piece_sum = jnp.sum(back_up * gelu_value, axis=1)
    pre_grad = (gate_col * back_up * gelu_slope).astype(jnp.bfloat16)
    scaled_grad = (gate_col * dy_piece.astype(jnp.float32)).astype(jnp.bfloat16)
    sum_in = jnp.einsum("rd,rh->dh", x_piece, pre_grad, preferred_element_type=jnp.float32)
    sum_out = jnp.einsum(
        "rh,rd->hd",
        gelu_value.astype(jnp.bfloat16),
        scaled_grad,
        preferred_element_type=jnp.float32,
    )
    part_rows = jnp.einsum("rh,dh->rd", pre_grad, w_in_local, preferred_element_type=jnp.float32)
    return (sum_in, sum_out, part_rows, gate_piece_sum)


def gathered_body(tokens, out_grad, w_router, w_in, w_out, expert_ids, slot_ids, keep_mask):
    expert_count = lax.axis_size("expert")
    window = expert_count // SPLIT
    slot_count = window * CAP
    model_width = tokens.shape[1]
    router_full = lax.all_gather(
        lax.all_gather(w_router, "expert", axis=1, tiled=True), "group", axis=0, tiled=True
    )
    logits = jnp.dot(tokens, router_full, preferred_element_type=jnp.float32)
    uniform_samples = jnp.arange(router_full.shape[1], dtype=jnp.int32)
    first_hot = (expert_ids[:, 0:1] == uniform_samples[None, :]).astype(jnp.float32)
    second_hot = (expert_ids[:, 1:2] == uniform_samples[None, :]).astype(jnp.float32)
    logit_gap = jnp.sum(logits * first_hot, axis=1) - jnp.sum(logits * second_hot, axis=1)
    combine = jnp.stack([jax.nn.sigmoid(logit_gap), jax.nn.sigmoid(-logit_gap)], axis=1)
    active = (keep_mask == 1) & (expert_ids < window)
    slot_code = jnp.where(active, expert_ids * CAP + slot_ids, -1)
    slot_axis = jnp.arange(slot_count, dtype=jnp.int32)
    place_first = (slot_code[:, 0:1] == slot_axis[None, :]).astype(jnp.float32)
    place_second = (slot_code[:, 1:2] == slot_axis[None, :]).astype(jnp.float32)
    placement = place_first + place_second
    place_round = placement.astype(jnp.bfloat16)
    token_slots = jnp.einsum(
        "ts,td->sd", place_round, tokens, preferred_element_type=jnp.float32
    ).astype(jnp.bfloat16)
    grad_slots = jnp.einsum(
        "ts,td->sd", place_round, out_grad, preferred_element_type=jnp.float32
    ).astype(jnp.bfloat16)
    gate_slots = jnp.sum(
        place_first * combine[:, 0:1] + place_second * combine[:, 1:2], axis=0
    ).astype(jnp.bfloat16)
    token_send = jnp.repeat(token_slots.reshape(window, CAP, model_width), SPLIT, axis=0)
    grad_send = jnp.repeat(grad_slots.reshape(window, CAP, model_width), SPLIT, axis=0)
    gate_send = jnp.repeat(gate_slots.reshape(window, CAP), SPLIT, axis=0)
    token_recv, grad_recv, gate_recv = (
        lax.all_to_all(token_send, "expert", split_axis=0, concat_axis=0, tiled=True),
        lax.all_to_all(grad_send, "expert", split_axis=0, concat_axis=0, tiled=True),
        lax.all_to_all(gate_send, "expert", split_axis=0, concat_axis=0, tiled=True),
    )
    row_count = expert_count * CAP
    token_rows = token_recv.reshape(row_count, model_width)
    grad_rows = grad_recv.reshape(row_count, model_width)
    gate_rows = gate_recv.reshape(row_count)
    w_in_local = w_in[0]
    w_out_local = w_out[0]
    sum_in, sum_out, row_parts, gate_parts = expert_rows(
        w_in_local,
        w_out_local,
        (
            lax.all_gather(token_rows, "group", axis=0, tiled=True),
            lax.all_gather(grad_rows, "group", axis=0, tiled=True),
            lax.all_gather(gate_rows, "group", axis=0, tiled=True),
        ),
    )
    w_in_grad = sum_in.astype(jnp.bfloat16)[None]
    w_out_grad = sum_out.astype(jnp.bfloat16)[None]
    row_sums = lax.psum_scatter(
        row_parts.astype(jnp.bfloat16), "group", scatter_dimension=0, tiled=True
    ).astype(jnp.float32)
    gate_sums = lax.psum_scatter(gate_parts, "group", scatter_dimension=0, tiled=True)
    rows_back, gates_back = (
        lax.all_to_all(
            row_sums.reshape(expert_count, CAP, model_width).astype(jnp.bfloat16),
            "expert",
            split_axis=0,
            concat_axis=0,
            tiled=True,
        ).astype(jnp.float32),
        lax.all_to_all(
            gate_sums.reshape(expert_count, CAP).astype(jnp.bfloat16),
            "expert",
            split_axis=0,
            concat_axis=0,
            tiled=True,
        ).astype(jnp.float32),
    )
    rows_back = jnp.sum(rows_back.reshape(window, SPLIT, CAP, model_width), axis=1).reshape(
        slot_count, model_width
    )
    gates_back = jnp.sum(gates_back.reshape(window, SPLIT, CAP), axis=1).reshape(slot_count)
    expert_part = jnp.dot(placement, rows_back, precision=lax.Precision.HIGHEST)
    gate_first = jnp.sum(place_first * gates_back[None, :], axis=1)
    gate_second = jnp.sum(place_second * gates_back[None, :], axis=1)
    gate_slope = combine[:, 0] * combine[:, 1] * (gate_first - gate_second)
    logit_grad = first_hot * gate_slope[:, None] - second_hot * gate_slope[:, None]
    router_part = jnp.dot(
        logit_grad, router_full.astype(jnp.float32).T, precision=lax.Precision.HIGHEST
    )
    in_grad = (expert_part + router_part).astype(jnp.bfloat16)
    router_sum = jnp.dot(tokens.astype(jnp.float32).T, logit_grad, precision=lax.Precision.HIGHEST)
    router_grad = lax.psum_scatter(
        lax.psum_scatter(router_sum, "expert", scatter_dimension=1, tiled=True),
        "group",
        scatter_dimension=0,
        tiled=True,
    )
    return (in_grad, w_in_grad, w_out_grad, router_grad)


def iota(shape, axis):
    return lax.broadcasted_iota(jnp.int32, shape, axis)


def one_hot(mask):
    return jnp.where(mask, 1.0, 0.0).astype(F32)


def contract(left, right, left_axis, right_axis):
    return lax.dot_general(
        left, right, (((left_axis,), (right_axis,)), ((), ())), preferred_element_type=F32
    )


def choice_places(z, window, ids_ref, slots_ref, keep_ref):
    places = []
    for k in range(2):
        ids = ids_ref[k : k + 1, :]
        relative = jnp.where(ids < z, ids - z + window, ids - z)
        active = (keep_ref[k : k + 1, :] == 1) & (ids < window)
        code = jnp.where(active, relative * CAP + slots_ref[k : k + 1, :], -1)
        places.append(one_hot(iota((LANES, LANES), 0) == code))
    return places


def finish_kernel(
    window,
    g1_ref,
    g2_ref,
    returned_hbm,
    router_ref,
    ids_hbm,
    slots_hbm,
    keep_hbm,
    in_grad_hbm,
    w_in_grad_hbm,
    w_out_grad_hbm,
    router_grad_hbm,
    in_grad,
    returned_ref,
    ids_ref,
    slots_ref,
    keep_ref,
    sems,
    load_sems,
):
    loads = [
        pltpu.make_async_copy(src, dst, load_sems.at[i])
        for i, (src, dst) in enumerate(
            [
                (ids_hbm, ids_ref),
                (slots_hbm, slots_ref),
                (keep_hbm, keep_ref),
                (returned_hbm, returned_ref),
            ]
        )
    ]
    for load in loads:
        load.start()
    parts = 4
    copies = []
    for src, dst in ((g1_ref, w_in_grad_hbm.at[0]), (g2_ref, w_out_grad_hbm.at[0])):
        step = src.shape[0] // parts
        for p in range(parts):
            span = pl.ds(p * step, step)
            copies.append(pltpu.make_async_copy(src.at[span], dst.at[span], sems.at[len(copies)]))
    copies.append(pltpu.make_async_copy(router_ref, router_grad_hbm, sems.at[2 * parts]))
    for copy in copies:
        copy.start()
    for load in loads:
        load.wait()
    z = lax.axis_index("expert") // SPLIT
    places = choice_places(z, window, ids_ref, slots_ref, keep_ref)
    spread_back = jnp.transpose(places[0] + places[1]).astype(BF16)
    rows = window * CAP
    chunks = in_grad.shape[1] // LANES
    back = chunks * rows
    row = iota((back, back), 0)
    source = ((row >> 1) & (window - 1)) * 16 + (row >> 3) * CAP + (row & 1)
    unfold = one_hot(iota((back, back), 1) == source).astype(BF16)
    flat = contract(unfold, returned_ref[...].reshape(back, LANES), 1, 0)
    returned = jnp.concatenate(
        [flat[c * rows : (c + 1) * rows] for c in range(chunks)], axis=1
    )
    returned = jnp.concatenate(
        [returned, jnp.zeros((LANES - rows, chunks * LANES), F32)], axis=0
    )
    in_grad[...] = contract(spread_back, returned.astype(BF16), 1, 0).astype(BF16)
    last = pltpu.make_async_copy(in_grad, in_grad_hbm, sems.at[2 * parts + 1])
    last.start()
    for copy in copies:
        copy.wait()
    last.wait()


def fused_kernel(
    window,
    groups,
    tokens_hbm,
    out_grad_hbm,
    router_hbm,
    w_in_hbm,
    w_out_hbm,
    ids_hbm,
    slots_hbm,
    keep_hbm,
    g1_out,
    g2_out,
    returned_ref,
    router_grad_ref,
    ids_ref,
    slots_ref,
    keep_ref,
    tok,
    outg,
    w1,
    w2,
    g1,
    g2,
    z_send,
    z_recv,
    w_recv,
    pack,
    xs,
    gv_send,
    gv_recv,
    gg,
    rp_send,
    rp_recv,
    coef_ref,
    rg_send,
    rg_recv,
    ret_send,
    ret_recv,
    load_sems,
    store_sems,
    zs,
    zr,
    ws,
    wr,
    pks,
    pkr,
    gvs,
    gvr,
    ggs,
    ggr,
    rps,
    rpr,
    rgs,
    rgr,
    rts,
    rtr,
):
    plane = SPLIT * groups
    width = tok.shape[1]
    chunks = width // LANES
    rows = window * CAP
    message = z_send.shape[1]
    used = CAP * (2 * chunks + 1)
    columns, depth = router_hbm.shape
    ix = lax.axis_index("expert")
    g = lax.axis_index("group")
    z = ix // SPLIT
    y = lax.rem(ix, SPLIT)
    q = y * groups + g

    def z_up(d):
        return (lax.rem(z + d, window) * SPLIT + y, g)

    def z_down(d):
        return (lax.rem(z + window - d, window) * SPLIT + y, g)

    def in_plane(p):
        return (z * SPLIT + p // groups, lax.rem(p, groups))

    def q_up(d):
        return lax.rem(q + d, plane)

    def q_down(d):
        return lax.rem(q + plane - d, plane)

    def remote(src, dst, send_sems, recv_sems, d, target):
        return pltpu.make_async_remote_copy(
            src_ref=src,
            dst_ref=dst,
            send_sem=send_sems.at[d],
            recv_sem=recv_sems.at[d],
            device_id=target,
            device_id_type=MESH,
        )

    loads = [
        pltpu.make_async_copy(src, dst, load_sems.at[i])
        for i, (src, dst) in enumerate(
            [
                (ids_hbm, ids_ref),
                (slots_hbm, slots_ref),
                (keep_hbm, keep_ref),
                (tokens_hbm, tok),
                (out_grad_hbm, outg),
                (router_hbm, w_recv.at[0]),
                (w_in_hbm.at[0], w1),
                (w_out_hbm.at[0], w2),
            ]
        )
    ]
    for load in loads:
        load.start()

    barrier = pltpu.get_barrier_semaphore()
    for d in range(1, window):
        pl.semaphore_signal(barrier, inc=1, device_id=z_up(d), device_id_type=MESH)
    for d in range(1, plane):
        pl.semaphore_signal(barrier, inc=1, device_id=in_plane(q_up(d)), device_id_type=MESH)

    for load in loads[:3]:
        load.wait()
    places = choice_places(z, window, ids_ref, slots_ref, keep_ref)
    place = places[0] + places[1]
    place_rows = place[:16].astype(BF16)
    short = place[:rows]
    first_id = jnp.sum(short * ids_ref[0:1, :].astype(F32), axis=1, keepdims=True)
    second_id = jnp.sum(short * ids_ref[1:2, :].astype(F32), axis=1, keepdims=True)
    which = jnp.sum(places[0][:rows] - places[1][:rows], axis=1, keepdims=True)
    lane = iota((rows, LANES), 1)
    meta = jnp.where(
        lane == 0, first_id, jnp.where(lane == 1, second_id, jnp.where(lane == 2, which, 0.0))
    )

    loads[3].wait()
    loads[4].wait()
    x_slots = contract(place_rows, tok[...], 1, 0)[:rows]
    dy_slots = contract(place_rows, outg[...], 1, 0)[:rows]
    pieces = [x_slots[:, c * LANES : (c + 1) * LANES] for c in range(chunks)]
    pieces += [dy_slots[:, c * LANES : (c + 1) * LANES] for c in range(chunks)]
    pieces += [meta, jnp.zeros((rows, LANES), F32)]
    folded = jnp.concatenate(pieces, axis=0).astype(BF16)
    depth_f = folded.shape[0]
    spread = []
    for d in range(window):
        row = iota((message, depth_f), 0)
        source = (row >> 1) * rows + d * CAP + (row & 1)
        spread.append(one_hot((iota((message, depth_f), 1) == source) & (row < used)))
    messages = contract(jnp.concatenate(spread, axis=0).astype(BF16), folded, 1, 0).astype(BF16)
    z_recv[0] = messages[:message]
    for d in range(1, window):
        z_send[d] = messages[d * message : (d + 1) * message]
    pl.semaphore_wait(barrier, window - 1 + plane - 1)

    z_copies, w_copies = [], []
    for d in range(1, window):
        z_copies.append(remote(z_send.at[d], z_recv.at[d], zs, zr, d, z_up(d)))
        z_copies[-1].start()
    loads[5].wait()
    for d in range(1, window):
        w_copies.append(remote(w_recv.at[0], w_recv.at[d], ws, wr, d, z_up(d)))
        w_copies[-1].start()

    wide = (chunks + 1) * 16
    row = iota((wide, window * message), 0)
    inner = row & 15
    chunk = row >> 4
    block = jnp.where((inner < rows) & (chunk < chunks), chunk, chunk + chunks)
    source = ((inner & (rows - 1)) >> 1) * message + block * CAP + (inner & 1)
    gather = one_hot(iota((wide, window * message), 1) == source).astype(BF16)
    for copy in z_copies:
        copy.wait_recv()
    gathered = contract(
        gather, z_recv[...].reshape(window * message, LANES), 1, 0
    ).astype(BF16)
    for c in range(chunks + 1):
        pack[q, :, c * LANES : (c + 1) * LANES] = gathered[c * 16 : (c + 1) * 16]

    def all_plane(src, dst_of, send_sems, recv_sems):
        copies = []
        for d in range(1, plane):
            target = q_up(d)
            copies.append(
                remote(src(target), dst_of(q), send_sems, recv_sems, d, in_plane(target))
            )
            copies[-1].start()
        arrivals = [
            remote(src(q_up(d)), dst_of(q_down(d)), send_sems, recv_sems, d, in_plane(q_up(d)))
            for d in range(1, plane)
        ]
        return copies, arrivals

    pk_copies, pk_arrivals = all_plane(lambda p: pack.at[q], lambda p: pack.at[p], pks, pkr)

    for copy in w_copies:
        copy.wait_recv()
    router = w_recv[...].reshape(window * columns, depth)
    for copy in pk_arrivals:
        copy.wait_recv()

    total = plane * rows
    everything = pack[...].astype(F32)
    x_rows = everything[:, :rows, :width].reshape(total, width).astype(BF16)
    dy_rows = everything[:, rows:, :width].reshape(total, width).astype(BF16)
    info = everything[:, :rows, width:].reshape(total, LANES)
    xs[...] = x_rows
    x_part = xs[:, pl.ds(pl.multiple_of(g * depth, LANES), depth)]

    column = iota((total, window * columns), 1)
    owner = lax.rem(z + window - column // columns, window)
    column_id = ((owner * SPLIT + y) * columns + lax.rem(column, columns)).astype(F32)
    hot = one_hot(info[:, 0:1] == column_id) - one_hot(info[:, 1:2] == column_id)
    sign = info[:, 2:3]
    gap_part = jnp.sum(contract(x_part, router, 1, 1) * hot, axis=1, keepdims=True)
    row_diff = contract(hot.astype(BF16), router, 1, 0)
    eye = iota((total, LANES), 0) == iota((total, LANES), 1)
    gap_row = jnp.sum(jnp.where(eye, gap_part, 0.0), axis=0, keepdims=True)
    gv_send[:, :, :depth] = row_diff.reshape(plane, rows, depth)
    gv_send[:, :, depth:] = jnp.broadcast_to(gap_row[None], (plane, rows, LANES))
    gv_recv[q] = gv_send[q]
    gv_copies, gv_arrivals = all_plane(
        lambda p: gv_send.at[p], lambda p: gv_recv.at[p], gvs, gvr
    )

    loads[7].wait()
    back_up = contract(dy_rows, w2[...], 1, 1)
    loads[6].wait()
    pre_act = contract(x_rows, w1[...], 1, 0)
    gelu_value, gelu_slope = gelu_parts(pre_act)
    gate_part = jnp.sum(back_up * gelu_value, axis=1, keepdims=True)
    gate_row = jnp.sum(jnp.where(eye, gate_part, 0.0), axis=0, keepdims=True)
    gg[q] = jnp.broadcast_to(gate_row, (rows, LANES))
    gg_copies, gg_arrivals = all_plane(lambda p: gg.at[q], lambda p: gg.at[p], ggs, ggr)

    for copy in gv_arrivals:
        copy.wait_recv()
    gap_sum = jnp.sum(gv_recv[:, 0:1, depth:], axis=0)
    gap = jnp.sum(jnp.where(eye, gap_sum, 0.0), axis=1, keepdims=True)
    combine_first = jax.nn.sigmoid(gap)
    combine_second = jax.nn.sigmoid(-gap)
    gate = jnp.where(sign > 0.5, combine_first, jnp.where(sign < -0.5, combine_second, 0.0))
    gate = gate.astype(BF16).astype(F32)
    pre_grad = (gate * back_up * gelu_slope).astype(BF16)
    part_rows = contract(pre_grad, w1[...], 1, 1).reshape(plane, rows, width)
    half = width // 2
    rp_send[...] = jnp.concatenate(
        [part_rows[:, :, :half], part_rows[:, :, half:]], axis=1
    ).astype(BF16)
    rp_recv[q] = rp_send[q]
    rp_copies, rp_arrivals = all_plane(
        lambda p: rp_send.at[p], lambda p: rp_recv.at[p], rps, rpr
    )

    for copy in gg_arrivals:
        copy.wait_recv()
    grad_sum = jnp.sum(gg[:, 0:1, :], axis=0)
    gate_grad = jnp.sum(jnp.where(eye, grad_sum, 0.0), axis=1, keepdims=True)
    coef = sign * combine_first * combine_second * gate_grad
    coef_ref[...] = jnp.broadcast_to(coef, (total, LANES))
    logit_grad = coef * hot
    high = logit_grad.astype(BF16)
    low = (logit_grad - high.astype(F32)).astype(BF16)
    router_part = contract(
        jnp.concatenate([high, low], axis=0), jnp.concatenate([x_part, x_part], axis=0), 0, 0
    )
    for d in range(1, window):
        rg_send[d] = router_part[d * columns : (d + 1) * columns].astype(BF16)
    rg_copies = []
    for d in range(1, window):
        rg_copies.append(remote(rg_send.at[d], rg_recv.at[d], rgs, rgr, d, z_down(d)))
        rg_copies[-1].start()

    g1[...] = contract(x_rows, pre_grad, 0, 0).astype(BF16)
    stores = [pltpu.make_async_copy(g1, g1_out, store_sems.at[0])]
    stores[0].start()
    scaled_grad = (gate * dy_rows.astype(F32)).astype(BF16)
    g2[...] = contract(gelu_value.astype(BF16), scaled_grad, 0, 0).astype(BF16)
    stores.append(pltpu.make_async_copy(g2, g2_out, store_sems.at[1]))
    stores[1].start()

    for copy in rp_arrivals:
        copy.wait_recv()
    summed = jnp.sum(rp_recv[...].astype(F32), axis=0)
    row_grad = jnp.concatenate([summed[:rows], summed[rows:]], axis=1)
    diffs = []
    for part in range(groups):
        diff = gv_recv[part, :, :depth]
        for other in range(1, SPLIT):
            diff = diff + gv_recv[other * groups + part, :, :depth]
        diffs.append(diff)
    own_coef = coef_ref[pl.ds(pl.multiple_of(q * rows, rows), rows), 0:1]
    row_grad = row_grad + own_coef * jnp.concatenate(diffs, axis=1)
    folded = jnp.concatenate(
        [row_grad[:, c * LANES : (c + 1) * LANES] for c in range(chunks)], axis=0
    ).astype(BF16)
    back = chunks * rows
    row = iota((back, back), 0)
    source = ((row >> 1) & (chunks - 1)) * rows + (row >> 4) * CAP + (row & 1)
    fold = one_hot(iota((back, back), 1) == source).astype(BF16)
    ret_send[...] = contract(fold, folded, 1, 0).astype(BF16).reshape(ret_send.shape)
    ret_recv[0] = ret_send[0]
    ret_copies = []
    for d in range(1, window):
        ret_copies.append(remote(ret_send.at[d], ret_recv.at[d], rts, rtr, d, z_down(d)))
        ret_copies[-1].start()

    for copy in rg_copies:
        copy.wait_recv()
    router_grad_ref[...] = router_part[:columns] + jnp.sum(
        rg_recv[1:].astype(F32), axis=0
    )

    for copy in ret_copies:
        copy.wait_recv()
    returned_ref[...] = ret_recv[...]

    for group in (z_copies, w_copies, pk_copies, gv_copies, gg_copies, rp_copies, rg_copies, ret_copies):
        for copy in group:
            copy.wait_send()
    for store in stores:
        store.wait()


def fused(tokens, out_grad, w_router, w_in, w_out, expert_ids, slot_ids, keep_mask):
    window = lax.axis_size("expert") // SPLIT
    groups = lax.axis_size("group")
    plane = SPLIT * groups
    count, width = tokens.shape
    hidden = w_in.shape[2]
    depth, columns = w_router.shape
    rows = window * CAP
    message = -(-CAP * (2 * width // LANES + 1) // 16) * 16
    vmem = pl.BlockSpec(memory_space=pltpu.VMEM)
    free = pl.BlockSpec(memory_space=pl.ANY)
    hbm = pl.BlockSpec(memory_space=pltpu.HBM)
    dma = pltpu.SemaphoreType.DMA
    routing = (expert_ids.T, slot_ids.T, keep_mask.T)
    g1, g2, returned, router_part = pl.pallas_call(
        functools.partial(fused_kernel, window, groups),
        out_shape=(
            jax.ShapeDtypeStruct((width, hidden), BF16),
            jax.ShapeDtypeStruct((hidden, width), BF16),
            jax.ShapeDtypeStruct((window, 16, LANES), BF16),
            jax.ShapeDtypeStruct((columns, depth), F32),
        ),
        in_specs=[hbm] * 8,
        out_specs=(free, free, vmem, vmem),
        scratch_shapes=[
            pltpu.VMEM(expert_ids.shape[::-1], jnp.int32),
            pltpu.VMEM(slot_ids.shape[::-1], jnp.int32),
            pltpu.VMEM(keep_mask.shape[::-1], jnp.int32),
            pltpu.VMEM((count, width), BF16),
            pltpu.VMEM((count, width), BF16),
            pltpu.VMEM((width, hidden), BF16),
            pltpu.VMEM((hidden, width), BF16),
            pltpu.VMEM((width, hidden), BF16),
            pltpu.VMEM((hidden, width), BF16),
            pltpu.VMEM((window, message, LANES), BF16),
            pltpu.VMEM((window, message, LANES), BF16),
            pltpu.VMEM((window, columns, depth), BF16),
            pltpu.VMEM((plane, 16, width + LANES), BF16),
            pltpu.VMEM((plane * rows, width), BF16),
            pltpu.VMEM((plane, rows, depth + LANES), F32),
            pltpu.VMEM((plane, rows, depth + LANES), F32),
            pltpu.VMEM((plane, rows, LANES), F32),
            pltpu.VMEM((plane, 16, width // 2), BF16),
            pltpu.VMEM((plane, 16, width // 2), BF16),
            pltpu.VMEM((plane * rows, LANES), F32),
            pltpu.VMEM((window, columns, depth), BF16),
            pltpu.VMEM((window, columns, depth), BF16),
            pltpu.VMEM((window, 16, LANES), BF16),
            pltpu.VMEM((window, 16, LANES), BF16),
            dma((8,)),
            dma((2,)),
        ]
        + [dma((window,))] * 4
        + [dma((plane,))] * 8
        + [dma((window,))] * 4,
        compiler_params=pltpu.CompilerParams(
            collective_id=0, has_side_effects=True, vmem_limit_bytes=60 * 1024 * 1024
        ),
    )(
        tokens,
        out_grad,
        w_router.T,
        w_in,
        w_out,
        *routing,
    )
    in_grad, w_in_grad, w_out_grad, router_grad = pl.pallas_call(
        functools.partial(finish_kernel, window),
        out_shape=(
            jax.ShapeDtypeStruct((count, width), BF16),
            jax.ShapeDtypeStruct(w_in.shape, BF16),
            jax.ShapeDtypeStruct(w_out.shape, BF16),
            jax.ShapeDtypeStruct((columns, depth), F32),
        ),
        in_specs=[hbm] * 7,
        out_specs=(hbm, hbm, hbm, hbm),
        scratch_shapes=[
            pltpu.VMEM((count, width), BF16),
            pltpu.VMEM((window, 16, LANES), BF16),
            pltpu.VMEM(expert_ids.shape[::-1], jnp.int32),
            pltpu.VMEM(slot_ids.shape[::-1], jnp.int32),
            pltpu.VMEM(keep_mask.shape[::-1], jnp.int32),
            dma((10,)),
            dma((4,)),
        ],
        compiler_params=pltpu.CompilerParams(vmem_limit_bytes=60 * 1024 * 1024),
    )(g1, g2, returned, router_part, *routing)
    return (in_grad, w_in_grad, w_out_grad, router_grad.T)


def body(*args):
    tokens, _, w_router = args[:3]
    window = lax.axis_size("expert") // SPLIT
    fits = (
        window * CAP == 8
        and w_router.shape[1] % 16 == 0
        and w_router.shape[0] % LANES == 0
        and window * w_router.shape[1] == LANES
        and SPLIT * lax.axis_size("group") * window * CAP <= LANES
        and tokens.shape == (LANES, 8 * LANES)
    )
    return fused(*args) if fits else gathered_body(*args)


def solution(mesh):
    return jax.shard_map(
        body,
        mesh=mesh,
        in_specs=(
            P(("expert", "group"), None),
            P(("expert", "group"), None),
            P("group", "expert"),
            P("expert", None, "group"),
            P("expert", "group", None),
            P(("expert", "group"), None),
            P(("expert", "group"), None),
            P(("expert", "group"), None),
        ),
        out_specs=(
            P(("expert", "group"), None),
            P("expert", None, "group"),
            P("expert", "group", None),
            P("group", "expert"),
        ),
        check_vma=False,
    )
```

```python
import functools

import jax
import jax.numpy as jnp
from jax import lax
from jax.experimental import pallas as pl
from jax.experimental.pallas import tpu as pltpu
from jax.sharding import PartitionSpec as P

CAP = 2
SPLIT = 2
LANES = 128
F32 = jnp.float32
BF16 = jnp.bfloat16
MESH = pl.DeviceIdType.MESH


def gelu_parts(pre_act):
    cubic_term = 0.044715 * pre_act * pre_act * pre_act
    tanh_value = jnp.tanh(0.7978845608028654 * (pre_act + cubic_term))
    gelu_value = 0.5 * pre_act * (1.0 + tanh_value)
    gelu_slope = 0.5 * (1.0 + tanh_value) + 0.5 * pre_act * (
        1.0 - tanh_value * tanh_value
    ) * 0.7978845608028654 * (1.0 + 3.0 * 0.044715 * pre_act * pre_act)
    return (gelu_value, gelu_slope)


def expert_rows(w_in_local, w_out_local, pieces):
    x_piece, dy_piece, gate_piece = pieces
    gate_col = gate_piece.astype(jnp.float32)[:, None]
    pre_act = jnp.dot(x_piece, w_in_local, preferred_element_type=jnp.float32)
    gelu_value, gelu_slope = gelu_parts(pre_act)
    back_up = jnp.einsum("rd,hd->rh", dy_piece, w_out_local, preferred_element_type=jnp.float32)
    gate_piece_sum = jnp.sum(back_up * gelu_value, axis=1)
    pre_grad = (gate_col * back_up * gelu_slope).astype(jnp.bfloat16)
    scaled_grad = (gate_col * dy_piece.astype(jnp.float32)).astype(jnp.bfloat16)
    sum_in = jnp.einsum("rd,rh->dh", x_piece, pre_grad, preferred_element_type=jnp.float32)
    sum_out = jnp.einsum(
        "rh,rd->hd",
        gelu_value.astype(jnp.bfloat16),
        scaled_grad,
        preferred_element_type=jnp.float32,
    )
    part_rows = jnp.einsum("rh,dh->rd", pre_grad, w_in_local, preferred_element_type=jnp.float32)
    return (sum_in, sum_out, part_rows, gate_piece_sum)


def gathered_body(tokens, out_grad, w_router, w_in, w_out, expert_ids, slot_ids, keep_mask):
    expert_count = lax.axis_size("expert")
    window = expert_count // SPLIT
    slot_count = window * CAP
    model_width = tokens.shape[1]
    router_full = lax.all_gather(
        lax.all_gather(w_router, "expert", axis=1, tiled=True), "group", axis=0, tiled=True
    )
    logits = jnp.dot(tokens, router_full, preferred_element_type=jnp.float32)
    uniform_samples = jnp.arange(router_full.shape[1], dtype=jnp.int32)
    first_hot = (expert_ids[:, 0:1] == uniform_samples[None, :]).astype(jnp.float32)
    second_hot = (expert_ids[:, 1:2] == uniform_samples[None, :]).astype(jnp.float32)
    logit_gap = jnp.sum(logits * first_hot, axis=1) - jnp.sum(logits * second_hot, axis=1)
    combine = jnp.stack([jax.nn.sigmoid(logit_gap), jax.nn.sigmoid(-logit_gap)], axis=1)
    active = (keep_mask == 1) & (expert_ids < window)
    slot_code = jnp.where(active, expert_ids * CAP + slot_ids, -1)
    slot_axis = jnp.arange(slot_count, dtype=jnp.int32)
    place_first = (slot_code[:, 0:1] == slot_axis[None, :]).astype(jnp.float32)
    place_second = (slot_code[:, 1:2] == slot_axis[None, :]).astype(jnp.float32)
    placement = place_first + place_second
    place_round = placement.astype(jnp.bfloat16)
    token_slots = jnp.einsum(
        "ts,td->sd", place_round, tokens, preferred_element_type=jnp.float32
    ).astype(jnp.bfloat16)
    grad_slots = jnp.einsum(
        "ts,td->sd", place_round, out_grad, preferred_element_type=jnp.float32
    ).astype(jnp.bfloat16)
    gate_slots = jnp.sum(
        place_first * combine[:, 0:1] + place_second * combine[:, 1:2], axis=0
    ).astype(jnp.bfloat16)
    token_send = jnp.repeat(token_slots.reshape(window, CAP, model_width), SPLIT, axis=0)
    grad_send = jnp.repeat(grad_slots.reshape(window, CAP, model_width), SPLIT, axis=0)
    gate_send = jnp.repeat(gate_slots.reshape(window, CAP), SPLIT, axis=0)
    token_recv, grad_recv, gate_recv = (
        lax.all_to_all(token_send, "expert", split_axis=0, concat_axis=0, tiled=True),
        lax.all_to_all(grad_send, "expert", split_axis=0, concat_axis=0, tiled=True),
        lax.all_to_all(gate_send, "expert", split_axis=0, concat_axis=0, tiled=True),
    )
    row_count = expert_count * CAP
    token_rows = token_recv.reshape(row_count, model_width)
    grad_rows = grad_recv.reshape(row_count, model_width)
    gate_rows = gate_recv.reshape(row_count)
    w_in_local = w_in[0]
    w_out_local = w_out[0]
    sum_in, sum_out, row_parts, gate_parts = expert_rows(
        w_in_local,
        w_out_local,
        (
            lax.all_gather(token_rows, "group", axis=0, tiled=True),
            lax.all_gather(grad_rows, "group", axis=0, tiled=True),
            lax.all_gather(gate_rows, "group", axis=0, tiled=True),
        ),
    )
    w_in_grad = sum_in.astype(jnp.bfloat16)[None]
    w_out_grad = sum_out.astype(jnp.bfloat16)[None]
    row_sums = lax.psum_scatter(
        row_parts.astype(jnp.bfloat16), "group", scatter_dimension=0, tiled=True
    ).astype(jnp.float32)
    gate_sums = lax.psum_scatter(gate_parts, "group", scatter_dimension=0, tiled=True)
    rows_back, gates_back = (
        lax.all_to_all(
            row_sums.reshape(expert_count, CAP, model_width).astype(jnp.bfloat16),
            "expert",
            split_axis=0,
            concat_axis=0,
            tiled=True,
        ).astype(jnp.float32),
        lax.all_to_all(
            gate_sums.reshape(expert_count, CAP).astype(jnp.bfloat16),
            "expert",
            split_axis=0,
            concat_axis=0,
            tiled=True,
        ).astype(jnp.float32),
    )
    rows_back = jnp.sum(rows_back.reshape(window, SPLIT, CAP, model_width), axis=1).reshape(
        slot_count, model_width
    )
    gates_back = jnp.sum(gates_back.reshape(window, SPLIT, CAP), axis=1).reshape(slot_count)
    expert_part = jnp.dot(placement, rows_back, precision=lax.Precision.HIGHEST)
    gate_first = jnp.sum(place_first * gates_back[None, :], axis=1)
    gate_second = jnp.sum(place_second * gates_back[None, :], axis=1)
    gate_slope = combine[:, 0] * combine[:, 1] * (gate_first - gate_second)
    logit_grad = first_hot * gate_slope[:, None] - second_hot * gate_slope[:, None]
    router_part = jnp.dot(
        logit_grad, router_full.astype(jnp.float32).T, precision=lax.Precision.HIGHEST
    )
    in_grad = (expert_part + router_part).astype(jnp.bfloat16)
    router_sum = jnp.dot(tokens.astype(jnp.float32).T, logit_grad, precision=lax.Precision.HIGHEST)
    router_grad = lax.psum_scatter(
        lax.psum_scatter(router_sum, "expert", scatter_dimension=1, tiled=True),
        "group",
        scatter_dimension=0,
        tiled=True,
    )
    return (in_grad, w_in_grad, w_out_grad, router_grad)


def iota(shape, axis):
    return lax.broadcasted_iota(jnp.int32, shape, axis)


def one_hot(mask):
    return jnp.where(mask, 1.0, 0.0).astype(F32)


def contract(left, right, left_axis, right_axis):
    return lax.dot_general(
        left, right, (((left_axis,), (right_axis,)), ((), ())), preferred_element_type=F32
    )


def choice_places(z, window, ids_ref, slots_ref, keep_ref):
    places = []
    for k in range(2):
        ids = ids_ref[k : k + 1, :]
        relative = jnp.where(ids < z, ids - z + window, ids - z)
        active = (keep_ref[k : k + 1, :] == 1) & (ids < window)
        code = jnp.where(active, relative * CAP + slots_ref[k : k + 1, :], -1)
        places.append(one_hot(iota((LANES, LANES), 0) == code))
    return places


def finish_kernel(
    window,
    x_hbm,
    pre_grad_hbm,
    hidden_hbm,
    scaled_hbm,
    returned_hbm,
    router_ref,
    ids_hbm,
    slots_hbm,
    keep_hbm,
    in_grad_hbm,
    w_in_grad_hbm,
    w_out_grad_hbm,
    router_grad_hbm,
    x_rows,
    pre_grad,
    hidden,
    scaled,
    router_grad,
    g1,
    g2,
    in_grad,
    returned_ref,
    ids_ref,
    slots_ref,
    keep_ref,
    sems,
    load_sems,
):
    loads = [
        pltpu.make_async_copy(src, dst, load_sems.at[i])
        for i, (src, dst) in enumerate(
            [
                (x_hbm, x_rows),
                (pre_grad_hbm, pre_grad),
                (hidden_hbm, hidden),
                (scaled_hbm, scaled),
                (returned_hbm, returned_ref),
                (router_ref, router_grad),
                (ids_hbm, ids_ref),
                (slots_hbm, slots_ref),
                (keep_hbm, keep_ref),
            ]
        )
    ]
    for load in loads:
        load.start()
    parts = 4
    copies = []

    def weight_grad(left, right, staged, target):
        step = staged.shape[0] // parts
        for p in range(parts):
            span = pl.ds(p * step, step)
            staged[span] = contract(left[:, span], right[...], 0, 0).astype(BF16)
            copies.append(
                pltpu.make_async_copy(staged.at[span], target.at[span], sems.at[len(copies)])
            )
            copies[-1].start()

    loads[0].wait()
    loads[1].wait()
    weight_grad(x_rows, pre_grad, g1, w_in_grad_hbm.at[0])
    loads[2].wait()
    loads[3].wait()
    weight_grad(hidden, scaled, g2, w_out_grad_hbm.at[0])
    for load in loads[4:]:
        load.wait()
    copies.append(pltpu.make_async_copy(router_grad, router_grad_hbm, sems.at[2 * parts]))
    copies[-1].start()
    z = lax.axis_index("expert") // SPLIT
    places = choice_places(z, window, ids_ref, slots_ref, keep_ref)
    spread_back = jnp.transpose(places[0] + places[1]).astype(BF16)
    rows = window * CAP
    chunks = in_grad.shape[1] // LANES
    back = chunks * rows
    row = iota((back, back), 0)
    source = ((row >> 1) & (window - 1)) * 16 + (row >> 3) * CAP + (row & 1)
    unfold = one_hot(iota((back, back), 1) == source).astype(BF16)
    flat = contract(unfold, returned_ref[...].reshape(back, LANES), 1, 0)
    returned = jnp.concatenate(
        [flat[c * rows : (c + 1) * rows] for c in range(chunks)], axis=1
    )
    returned = jnp.concatenate(
        [returned, jnp.zeros((LANES - rows, chunks * LANES), F32)], axis=0
    )
    in_grad[...] = contract(spread_back, returned.astype(BF16), 1, 0).astype(BF16)
    copies.append(pltpu.make_async_copy(in_grad, in_grad_hbm, sems.at[2 * parts + 1]))
    copies[-1].start()
    for copy in copies:
        copy.wait()


def fused_kernel(
    window,
    groups,
    tokens_hbm,
    out_grad_hbm,
    router_hbm,
    w_in_hbm,
    w_out_hbm,
    ids_hbm,
    slots_hbm,
    keep_hbm,
    x_out,
    pre_grad_out,
    hidden_out,
    scaled_out,
    returned_ref,
    router_grad_ref,
    ids_ref,
    slots_ref,
    keep_ref,
    tok,
    outg,
    w1,
    w2,
    pre_grad_ref,
    hidden_ref,
    scaled_ref,
    z_send,
    z_recv,
    w_recv,
    x_pack,
    dy_pack,
    xs,
    gv_send,
    gv_recv,
    gg,
    rp_send,
    rp_recv,
    coef_ref,
    rg_send,
    rg_recv,
    ret_send,
    ret_recv,
    load_sems,
    store_sems,
    zs,
    zr,
    ws,
    wr,
    xps,
    xpr,
    dps,
    dpr,
    gvs,
    gvr,
    ggs,
    ggr,
    rps,
    rpr,
    rgs,
    rgr,
    rts,
    rtr,
):
    plane = SPLIT * groups
    width = tok.shape[1]
    chunks = width // LANES
    rows = window * CAP
    message = z_send.shape[1]
    used = CAP * (2 * chunks + 1)
    columns, depth = router_hbm.shape
    ix = lax.axis_index("expert")
    g = lax.axis_index("group")
    z = ix // SPLIT
    y = lax.rem(ix, SPLIT)
    q = y * groups + g

    def z_up(d):
        return (lax.rem(z + d, window) * SPLIT + y, g)

    def z_down(d):
        return (lax.rem(z + window - d, window) * SPLIT + y, g)

    def in_plane(p):
        return (z * SPLIT + p // groups, lax.rem(p, groups))

    def q_up(d):
        return lax.rem(q + d, plane)

    def q_down(d):
        return lax.rem(q + plane - d, plane)

    def remote(src, dst, send_sems, recv_sems, d, target):
        return pltpu.make_async_remote_copy(
            src_ref=src,
            dst_ref=dst,
            send_sem=send_sems.at[d],
            recv_sem=recv_sems.at[d],
            device_id=target,
            device_id_type=MESH,
        )

    loads = [
        pltpu.make_async_copy(src, dst, load_sems.at[i])
        for i, (src, dst) in enumerate(
            [
                (ids_hbm, ids_ref),
                (slots_hbm, slots_ref),
                (keep_hbm, keep_ref),
                (tokens_hbm, tok),
                (out_grad_hbm, outg),
                (router_hbm, w_recv.at[0]),
                (w_in_hbm.at[0], w1),
                (w_out_hbm.at[0], w2),
            ]
        )
    ]
    for load in loads:
        load.start()

    barrier = pltpu.get_barrier_semaphore()
    for d in range(1, window):
        pl.semaphore_signal(barrier, inc=1, device_id=z_up(d), device_id_type=MESH)
    for d in range(1, plane):
        pl.semaphore_signal(barrier, inc=1, device_id=in_plane(q_up(d)), device_id_type=MESH)

    for load in loads[:3]:
        load.wait()
    places = choice_places(z, window, ids_ref, slots_ref, keep_ref)
    place = places[0] + places[1]
    place_rows = place[:16].astype(BF16)
    short = place[:rows]
    first_id = jnp.sum(short * ids_ref[0:1, :].astype(F32), axis=1, keepdims=True)
    second_id = jnp.sum(short * ids_ref[1:2, :].astype(F32), axis=1, keepdims=True)
    which = jnp.sum(places[0][:rows] - places[1][:rows], axis=1, keepdims=True)
    lane = iota((rows, LANES), 1)
    meta = jnp.where(
        lane == 0, first_id, jnp.where(lane == 1, second_id, jnp.where(lane == 2, which, 0.0))
    )

    loads[3].wait()
    loads[4].wait()
    x_slots = contract(place_rows, tok[...], 1, 0)[:rows]
    dy_slots = contract(place_rows, outg[...], 1, 0)[:rows]
    pieces = [x_slots[:, c * LANES : (c + 1) * LANES] for c in range(chunks)]
    pieces += [dy_slots[:, c * LANES : (c + 1) * LANES] for c in range(chunks)]
    pieces += [meta, jnp.zeros((rows, LANES), F32)]
    folded = jnp.concatenate(pieces, axis=0).astype(BF16)
    depth_f = folded.shape[0]
    spread = []
    for d in range(window):
        row = iota((message, depth_f), 0)
        source = (row >> 1) * rows + d * CAP + (row & 1)
        spread.append(one_hot((iota((message, depth_f), 1) == source) & (row < used)))
    messages = contract(jnp.concatenate(spread, axis=0).astype(BF16), folded, 1, 0).astype(BF16)
    z_recv[0] = messages[:message]
    for d in range(1, window):
        z_send[d] = messages[d * message : (d + 1) * message]
    pl.semaphore_wait(barrier, window - 1 + plane - 1)

    z_copies, w_copies = [], []
    for d in range(1, window):
        z_copies.append(remote(z_send.at[d], z_recv.at[d], zs, zr, d, z_up(d)))
        z_copies[-1].start()
    loads[5].wait()
    for d in range(1, window):
        w_copies.append(remote(w_recv.at[0], w_recv.at[d], ws, wr, d, z_up(d)))
        w_copies[-1].start()

    half = width // 2
    side = chunks // 2
    wide = (chunks + 1) * 16
    row = iota((wide, window * message), 0)
    inner = row & 15
    column = row >> 4
    upper = jnp.where(inner < rows, 0, side)
    block = jnp.where(
        column < side,
        column + upper,
        jnp.where(column == side, 2 * chunks, chunks + column - side - 1 + upper),
    )
    source = ((inner & (rows - 1)) >> 1) * message + block * CAP + (inner & 1)
    gather = one_hot(iota((wide, window * message), 1) == source).astype(BF16)
    for copy in z_copies:
        copy.wait_recv()
    gathered = contract(
        gather, z_recv[...].reshape(window * message, LANES), 1, 0
    ).astype(BF16)
    for c in range(side + 1):
        x_pack[q, :, c * LANES : (c + 1) * LANES] = gathered[c * 16 : (c + 1) * 16]
    for c in range(side):
        first = (side + 1 + c) * 16
        dy_pack[q, :, c * LANES : (c + 1) * LANES] = gathered[first : first + 16]

    def all_plane(src, dst_of, send_sems, recv_sems, base=0):
        copies = []
        for d in range(1, plane):
            target = q_up(d)
            copies.append(
                remote(
                    src(target), dst_of(q), send_sems, recv_sems, base + d, in_plane(target)
                )
            )
            copies[-1].start()
        arrivals = [
            remote(
                src(q_up(d)), dst_of(q_down(d)), send_sems, recv_sems, base + d, in_plane(q_up(d))
            )
            for d in range(1, plane)
        ]
        return copies, arrivals

    def unfolded(block):
        return jnp.concatenate(
            [block[:, :rows, :half], block[:, rows:, :half]], axis=2
        ).reshape(plane * rows, width)

    xp_copies, xp_arrivals = all_plane(
        lambda p: x_pack.at[q], lambda p: x_pack.at[p], xps, xpr
    )
    dp_copies, dp_arrivals = all_plane(
        lambda p: dy_pack.at[q], lambda p: dy_pack.at[p], dps, dpr
    )

    for copy in w_copies:
        copy.wait_recv()
    router = w_recv[...].reshape(window * columns, depth)
    for copy in xp_arrivals:
        copy.wait_recv()

    total = plane * rows
    packed = x_pack[...].astype(F32)
    x_rows = unfolded(packed).astype(BF16)
    info = packed[:, :rows, half:].reshape(total, LANES)
    xs[...] = x_rows
    x_part = xs[:, pl.ds(pl.multiple_of(g * depth, LANES), depth)]

    column = iota((total, window * columns), 1)
    owner = lax.rem(z + window - column // columns, window)
    column_id = ((owner * SPLIT + y) * columns + lax.rem(column, columns)).astype(F32)
    hot = one_hot(info[:, 0:1] == column_id) - one_hot(info[:, 1:2] == column_id)
    sign = info[:, 2:3]
    gap_part = jnp.sum(contract(x_part, router, 1, 1) * hot, axis=1, keepdims=True)
    row_diff = contract(hot.astype(BF16), router, 1, 0)
    eye = iota((total, LANES), 0) == iota((total, LANES), 1)
    gap_row = jnp.sum(jnp.where(eye, gap_part, 0.0), axis=0, keepdims=True)
    gv_send[:, :, :depth] = row_diff.reshape(plane, rows, depth)
    gv_send[:, :, depth:] = jnp.broadcast_to(gap_row[None], (plane, rows, LANES))
    gv_recv[q] = gv_send[q]
    gv_copies, gv_arrivals = all_plane(
        lambda p: gv_send.at[p], lambda p: gv_recv.at[p], gvs, gvr
    )

    loads[6].wait()
    pre_act = contract(x_rows, w1[...], 1, 0)
    loads[7].wait()
    for copy in dp_arrivals:
        copy.wait_recv()
    dy_rows = unfolded(dy_pack[...].astype(F32)).astype(BF16)
    back_up = contract(dy_rows, w2[...], 1, 1)
    gelu_value, gelu_slope = gelu_parts(pre_act)
    gate_part = jnp.sum(back_up * gelu_value, axis=1, keepdims=True)
    gate_row = jnp.sum(jnp.where(eye, gate_part, 0.0), axis=0, keepdims=True)
    gg[q] = jnp.broadcast_to(gate_row, (rows, LANES))
    gg_copies, gg_arrivals = all_plane(lambda p: gg.at[q], lambda p: gg.at[p], ggs, ggr)

    for copy in gv_arrivals:
        copy.wait_recv()
    gap_sum = jnp.sum(gv_recv[:, 0:1, depth:], axis=0)
    gap = jnp.sum(jnp.where(eye, gap_sum, 0.0), axis=1, keepdims=True)
    combine_first = jax.nn.sigmoid(gap)
    combine_second = jax.nn.sigmoid(-gap)
    gate = jnp.where(sign > 0.5, combine_first, jnp.where(sign < -0.5, combine_second, 0.0))
    gate = gate.astype(BF16).astype(F32)
    pre_grad = (gate * back_up * gelu_slope).astype(BF16)
    rp_copies, rp_arrivals = [], []
    for h in range(2):
        part = contract(pre_grad, w1[h * half : (h + 1) * half, :], 1, 1)
        part = part.reshape(plane, rows, half)
        rp_send[h] = jnp.concatenate(
            [part[:, :, : half // 2], part[:, :, half // 2 :]], axis=1
        ).astype(BF16)
        rp_recv[h, q] = rp_send[h, q]
        started, arriving = all_plane(
            lambda p, h=h: rp_send.at[h, p],
            lambda p, h=h: rp_recv.at[h, p],
            rps,
            rpr,
            h * plane,
        )
        rp_copies += started
        rp_arrivals.append(arriving)

    for copy in gg_arrivals:
        copy.wait_recv()
    grad_sum = jnp.sum(gg[:, 0:1, :], axis=0)
    gate_grad = jnp.sum(jnp.where(eye, grad_sum, 0.0), axis=1, keepdims=True)
    coef = sign * combine_first * combine_second * gate_grad
    coef_ref[...] = jnp.broadcast_to(coef, (total, LANES))
    logit_grad = coef * hot
    high = logit_grad.astype(BF16)
    low = (logit_grad - high.astype(F32)).astype(BF16)
    router_part = contract(
        jnp.concatenate([high, low], axis=0), jnp.concatenate([x_part, x_part], axis=0), 0, 0
    )
    for d in range(1, window):
        rg_send[d] = router_part[d * columns : (d + 1) * columns].astype(BF16)
    rg_copies = []
    for d in range(1, window):
        rg_copies.append(remote(rg_send.at[d], rg_recv.at[d], rgs, rgr, d, z_down(d)))
        rg_copies[-1].start()

    pre_grad_ref[...] = pre_grad
    hidden_ref[...] = gelu_value.astype(BF16)
    scaled_ref[...] = (gate * dy_rows.astype(F32)).astype(BF16)
    stores = [
        pltpu.make_async_copy(src, dst, store_sems.at[i])
        for i, (src, dst) in enumerate(
            [
                (xs, x_out),
                (pre_grad_ref, pre_grad_out),
                (hidden_ref, hidden_out),
                (scaled_ref, scaled_out),
            ]
        )
    ]
    for store in stores:
        store.start()

    halves = []
    for h in range(2):
        for copy in rp_arrivals[h]:
            copy.wait_recv()
        summed = jnp.sum(rp_recv[h].astype(F32), axis=0)
        halves += [summed[:rows], summed[rows:]]
    row_grad = jnp.concatenate(halves, axis=1)
    diffs = []
    for part in range(groups):
        diff = gv_recv[part, :, :depth]
        for other in range(1, SPLIT):
            diff = diff + gv_recv[other * groups + part, :, :depth]
        diffs.append(diff)
    own_coef = coef_ref[pl.ds(pl.multiple_of(q * rows, rows), rows), 0:1]
    row_grad = row_grad + own_coef * jnp.concatenate(diffs, axis=1)
    folded = jnp.concatenate(
        [row_grad[:, c * LANES : (c + 1) * LANES] for c in range(chunks)], axis=0
    ).astype(BF16)
    back = chunks * rows
    row = iota((back, back), 0)
    source = ((row >> 1) & (chunks - 1)) * rows + (row >> 4) * CAP + (row & 1)
    fold = one_hot(iota((back, back), 1) == source).astype(BF16)
    ret_send[...] = contract(fold, folded, 1, 0).astype(BF16).reshape(ret_send.shape)
    ret_recv[0] = ret_send[0]
    ret_copies = []
    for d in range(1, window):
        ret_copies.append(remote(ret_send.at[d], ret_recv.at[d], rts, rtr, d, z_down(d)))
        ret_copies[-1].start()

    for copy in rg_copies:
        copy.wait_recv()
    router_grad_ref[...] = router_part[:columns] + jnp.sum(
        rg_recv[1:].astype(F32), axis=0
    )

    for copy in ret_copies:
        copy.wait_recv()
    returned_ref[...] = ret_recv[...]

    for group in (
        z_copies,
        w_copies,
        xp_copies,
        dp_copies,
        gv_copies,
        gg_copies,
        rp_copies,
        rg_copies,
        ret_copies,
    ):
        for copy in group:
            copy.wait_send()
    for store in stores:
        store.wait()


def fused(tokens, out_grad, w_router, w_in, w_out, expert_ids, slot_ids, keep_mask):
    window = lax.axis_size("expert") // SPLIT
    groups = lax.axis_size("group")
    plane = SPLIT * groups
    count, width = tokens.shape
    hidden = w_in.shape[2]
    depth, columns = w_router.shape
    rows = window * CAP
    message = -(-CAP * (2 * width // LANES + 1) // 16) * 16
    vmem = pl.BlockSpec(memory_space=pltpu.VMEM)
    hbm = pl.BlockSpec(memory_space=pltpu.HBM)
    dma = pltpu.SemaphoreType.DMA
    routing = (expert_ids.T, slot_ids.T, keep_mask.T)
    total = plane * rows
    *handed, returned, router_part = pl.pallas_call(
        functools.partial(fused_kernel, window, groups),
        out_shape=(
            jax.ShapeDtypeStruct((total, width), BF16),
            jax.ShapeDtypeStruct((total, hidden), BF16),
            jax.ShapeDtypeStruct((total, hidden), BF16),
            jax.ShapeDtypeStruct((total, width), BF16),
            jax.ShapeDtypeStruct((window, 16, LANES), BF16),
            jax.ShapeDtypeStruct((columns, depth), F32),
        ),
        in_specs=[hbm] * 8,
        out_specs=(hbm, hbm, hbm, hbm, vmem, vmem),
        scratch_shapes=[
            pltpu.VMEM(expert_ids.shape[::-1], jnp.int32),
            pltpu.VMEM(slot_ids.shape[::-1], jnp.int32),
            pltpu.VMEM(keep_mask.shape[::-1], jnp.int32),
            pltpu.VMEM((count, width), BF16),
            pltpu.VMEM((count, width), BF16),
            pltpu.VMEM((width, hidden), BF16),
            pltpu.VMEM((hidden, width), BF16),
            pltpu.VMEM((total, hidden), BF16),
            pltpu.VMEM((total, hidden), BF16),
            pltpu.VMEM((total, width), BF16),
            pltpu.VMEM((window, message, LANES), BF16),
            pltpu.VMEM((window, message, LANES), BF16),
            pltpu.VMEM((window, columns, depth), BF16),
            pltpu.VMEM((plane, 16, width // 2 + LANES), BF16),
            pltpu.VMEM((plane, 16, width // 2), BF16),
            pltpu.VMEM((plane * rows, width), BF16),
            pltpu.VMEM((plane, rows, depth + LANES), F32),
            pltpu.VMEM((plane, rows, depth + LANES), F32),
            pltpu.VMEM((plane, rows, LANES), F32),
            pltpu.VMEM((2, plane, 16, width // 4), BF16),
            pltpu.VMEM((2, plane, 16, width // 4), BF16),
            pltpu.VMEM((plane * rows, LANES), F32),
            pltpu.VMEM((window, columns, depth), BF16),
            pltpu.VMEM((window, columns, depth), BF16),
            pltpu.VMEM((window, 16, LANES), BF16),
            pltpu.VMEM((window, 16, LANES), BF16),
            dma((8,)),
            dma((4,)),
        ]
        + [dma((window,))] * 4
        + [dma((plane,))] * 8
        + [dma((2 * plane,))] * 2
        + [dma((window,))] * 4,
        compiler_params=pltpu.CompilerParams(
            collective_id=0, has_side_effects=True, vmem_limit_bytes=60 * 1024 * 1024
        ),
    )(
        tokens,
        out_grad,
        w_router.T,
        w_in,
        w_out,
        *routing,
    )
    in_grad, w_in_grad, w_out_grad, router_grad = pl.pallas_call(
        functools.partial(finish_kernel, window),
        out_shape=(
            jax.ShapeDtypeStruct((count, width), BF16),
            jax.ShapeDtypeStruct(w_in.shape, BF16),
            jax.ShapeDtypeStruct(w_out.shape, BF16),
            jax.ShapeDtypeStruct((columns, depth), F32),
        ),
        in_specs=[hbm] * 9,
        out_specs=(hbm, hbm, hbm, hbm),
        scratch_shapes=[
            pltpu.VMEM((total, width), BF16),
            pltpu.VMEM((total, hidden), BF16),
            pltpu.VMEM((total, hidden), BF16),
            pltpu.VMEM((total, width), BF16),
            pltpu.VMEM((columns, depth), F32),
            pltpu.VMEM((width, hidden), BF16),
            pltpu.VMEM((hidden, width), BF16),
            pltpu.VMEM((count, width), BF16),
            pltpu.VMEM((window, 16, LANES), BF16),
            pltpu.VMEM(expert_ids.shape[::-1], jnp.int32),
            pltpu.VMEM(slot_ids.shape[::-1], jnp.int32),
            pltpu.VMEM(keep_mask.shape[::-1], jnp.int32),
            dma((10,)),
            dma((9,)),
        ],
        compiler_params=pltpu.CompilerParams(vmem_limit_bytes=60 * 1024 * 1024),
    )(*handed, returned, router_part, *routing)
    return (in_grad, w_in_grad, w_out_grad, router_grad.T)


def body(*args):
    tokens, _, w_router = args[:3]
    window = lax.axis_size("expert") // SPLIT
    fits = (
        window * CAP == 8
        and w_router.shape[1] % 16 == 0
        and w_router.shape[0] % LANES == 0
        and window * w_router.shape[1] == LANES
        and SPLIT * lax.axis_size("group") * window * CAP <= LANES
        and tokens.shape == (LANES, 8 * LANES)
    )
    return fused(*args) if fits else gathered_body(*args)


def solution(mesh):
    return jax.shard_map(
        body,
        mesh=mesh,
        in_specs=(
            P(("expert", "group"), None),
            P(("expert", "group"), None),
            P("group", "expert"),
            P("expert", None, "group"),
            P("expert", "group", None),
            P(("expert", "group"), None),
            P(("expert", "group"), None),
            P(("expert", "group"), None),
        ),
        out_specs=(
            P(("expert", "group"), None),
            P("expert", None, "group"),
            P("expert", "group", None),
            P("group", "expert"),
        ),
        check_vma=False,
    )
```

```python
import functools

import jax
import jax.numpy as jnp
from jax import lax
from jax.experimental import pallas as pl
from jax.experimental.pallas import tpu as pltpu
from jax.sharding import PartitionSpec as P

CAP = 2
SPLIT = 2
LANES = 128
F32 = jnp.float32
BF16 = jnp.bfloat16
MESH = pl.DeviceIdType.MESH


def gelu_parts(pre_act):
    cubic_term = 0.044715 * pre_act * pre_act * pre_act
    tanh_value = jnp.tanh(0.7978845608028654 * (pre_act + cubic_term))
    gelu_value = 0.5 * pre_act * (1.0 + tanh_value)
    gelu_slope = 0.5 * (1.0 + tanh_value) + 0.5 * pre_act * (
        1.0 - tanh_value * tanh_value
    ) * 0.7978845608028654 * (1.0 + 3.0 * 0.044715 * pre_act * pre_act)
    return (gelu_value, gelu_slope)


def expert_rows(w_in_local, w_out_local, pieces):
    x_piece, dy_piece, gate_piece = pieces
    gate_col = gate_piece.astype(jnp.float32)[:, None]
    pre_act = jnp.dot(x_piece, w_in_local, preferred_element_type=jnp.float32)
    gelu_value, gelu_slope = gelu_parts(pre_act)
    back_up = jnp.einsum("rd,hd->rh", dy_piece, w_out_local, preferred_element_type=jnp.float32)
    gate_piece_sum = jnp.sum(back_up * gelu_value, axis=1)
    pre_grad = (gate_col * back_up * gelu_slope).astype(jnp.bfloat16)
    scaled_grad = (gate_col * dy_piece.astype(jnp.float32)).astype(jnp.bfloat16)
    sum_in = jnp.einsum("rd,rh->dh", x_piece, pre_grad, preferred_element_type=jnp.float32)
    sum_out = jnp.einsum(
        "rh,rd->hd",
        gelu_value.astype(jnp.bfloat16),
        scaled_grad,
        preferred_element_type=jnp.float32,
    )
    part_rows = jnp.einsum("rh,dh->rd", pre_grad, w_in_local, preferred_element_type=jnp.float32)
    return (sum_in, sum_out, part_rows, gate_piece_sum)


def gathered_body(tokens, out_grad, w_router, w_in, w_out, expert_ids, slot_ids, keep_mask):
    expert_count = lax.axis_size("expert")
    window = expert_count // SPLIT
    slot_count = window * CAP
    model_width = tokens.shape[1]
    router_full = lax.all_gather(
        lax.all_gather(w_router, "expert", axis=1, tiled=True), "group", axis=0, tiled=True
    )
    logits = jnp.dot(tokens, router_full, preferred_element_type=jnp.float32)
    uniform_samples = jnp.arange(router_full.shape[1], dtype=jnp.int32)
    first_hot = (expert_ids[:, 0:1] == uniform_samples[None, :]).astype(jnp.float32)
    second_hot = (expert_ids[:, 1:2] == uniform_samples[None, :]).astype(jnp.float32)
    logit_gap = jnp.sum(logits * first_hot, axis=1) - jnp.sum(logits * second_hot, axis=1)
    combine = jnp.stack([jax.nn.sigmoid(logit_gap), jax.nn.sigmoid(-logit_gap)], axis=1)
    active = (keep_mask == 1) & (expert_ids < window)
    slot_code = jnp.where(active, expert_ids * CAP + slot_ids, -1)
    slot_axis = jnp.arange(slot_count, dtype=jnp.int32)
    place_first = (slot_code[:, 0:1] == slot_axis[None, :]).astype(jnp.float32)
    place_second = (slot_code[:, 1:2] == slot_axis[None, :]).astype(jnp.float32)
    placement = place_first + place_second
    place_round = placement.astype(jnp.bfloat16)
    token_slots = jnp.einsum(
        "ts,td->sd", place_round, tokens, preferred_element_type=jnp.float32
    ).astype(jnp.bfloat16)
    grad_slots = jnp.einsum(
        "ts,td->sd", place_round, out_grad, preferred_element_type=jnp.float32
    ).astype(jnp.bfloat16)
    gate_slots = jnp.sum(
        place_first * combine[:, 0:1] + place_second * combine[:, 1:2], axis=0
    ).astype(jnp.bfloat16)
    token_send = jnp.repeat(token_slots.reshape(window, CAP, model_width), SPLIT, axis=0)
    grad_send = jnp.repeat(grad_slots.reshape(window, CAP, model_width), SPLIT, axis=0)
    gate_send = jnp.repeat(gate_slots.reshape(window, CAP), SPLIT, axis=0)
    token_recv, grad_recv, gate_recv = (
        lax.all_to_all(token_send, "expert", split_axis=0, concat_axis=0, tiled=True),
        lax.all_to_all(grad_send, "expert", split_axis=0, concat_axis=0, tiled=True),
        lax.all_to_all(gate_send, "expert", split_axis=0, concat_axis=0, tiled=True),
    )
    row_count = expert_count * CAP
    token_rows = token_recv.reshape(row_count, model_width)
    grad_rows = grad_recv.reshape(row_count, model_width)
    gate_rows = gate_recv.reshape(row_count)
    w_in_local = w_in[0]
    w_out_local = w_out[0]
    sum_in, sum_out, row_parts, gate_parts = expert_rows(
        w_in_local,
        w_out_local,
        (
            lax.all_gather(token_rows, "group", axis=0, tiled=True),
            lax.all_gather(grad_rows, "group", axis=0, tiled=True),
            lax.all_gather(gate_rows, "group", axis=0, tiled=True),
        ),
    )
    w_in_grad = sum_in.astype(jnp.bfloat16)[None]
    w_out_grad = sum_out.astype(jnp.bfloat16)[None]
    row_sums = lax.psum_scatter(
        row_parts.astype(jnp.bfloat16), "group", scatter_dimension=0, tiled=True
    ).astype(jnp.float32)
    gate_sums = lax.psum_scatter(gate_parts, "group", scatter_dimension=0, tiled=True)
    rows_back, gates_back = (
        lax.all_to_all(
            row_sums.reshape(expert_count, CAP, model_width).astype(jnp.bfloat16),
            "expert",
            split_axis=0,
            concat_axis=0,
            tiled=True,
        ).astype(jnp.float32),
        lax.all_to_all(
            gate_sums.reshape(expert_count, CAP).astype(jnp.bfloat16),
            "expert",
            split_axis=0,
            concat_axis=0,
            tiled=True,
        ).astype(jnp.float32),
    )
    rows_back = jnp.sum(rows_back.reshape(window, SPLIT, CAP, model_width), axis=1).reshape(
        slot_count, model_width
    )
    gates_back = jnp.sum(gates_back.reshape(window, SPLIT, CAP), axis=1).reshape(slot_count)
    expert_part = jnp.dot(placement, rows_back, precision=lax.Precision.HIGHEST)
    gate_first = jnp.sum(place_first * gates_back[None, :], axis=1)
    gate_second = jnp.sum(place_second * gates_back[None, :], axis=1)
    gate_slope = combine[:, 0] * combine[:, 1] * (gate_first - gate_second)
    logit_grad = first_hot * gate_slope[:, None] - second_hot * gate_slope[:, None]
    router_part = jnp.dot(
        logit_grad, router_full.astype(jnp.float32).T, precision=lax.Precision.HIGHEST
    )
    in_grad = (expert_part + router_part).astype(jnp.bfloat16)
    router_sum = jnp.dot(tokens.astype(jnp.float32).T, logit_grad, precision=lax.Precision.HIGHEST)
    router_grad = lax.psum_scatter(
        lax.psum_scatter(router_sum, "expert", scatter_dimension=1, tiled=True),
        "group",
        scatter_dimension=0,
        tiled=True,
    )
    return (in_grad, w_in_grad, w_out_grad, router_grad)


def iota(shape, axis):
    return lax.broadcasted_iota(jnp.int32, shape, axis)


def one_hot(mask):
    return jnp.where(mask, 1.0, 0.0).astype(F32)


def contract(left, right, left_axis, right_axis):
    return lax.dot_general(
        left, right, (((left_axis,), (right_axis,)), ((), ())), preferred_element_type=F32
    )


def choice_places(z, window, ids_ref, slots_ref, keep_ref):
    places = []
    for k in range(2):
        ids = ids_ref[k : k + 1, :]
        relative = jnp.where(ids < z, ids - z + window, ids - z)
        active = (keep_ref[k : k + 1, :] == 1) & (ids < window)
        code = jnp.where(active, relative * CAP + slots_ref[k : k + 1, :], -1)
        places.append(one_hot(iota((LANES, LANES), 0) == code))
    return places


def finish_kernel(
    window,
    x_hbm,
    pre_grad_hbm,
    hidden_hbm,
    scaled_hbm,
    returned_hbm,
    router_ref,
    ids_hbm,
    slots_hbm,
    keep_hbm,
    in_grad_hbm,
    w_in_grad_hbm,
    w_out_grad_hbm,
    router_grad_hbm,
    x_rows,
    pre_grad,
    hidden,
    scaled,
    router_grad,
    g1,
    g2,
    in_grad,
    returned_ref,
    ids_ref,
    slots_ref,
    keep_ref,
    sems,
    load_sems,
):
    loads = [
        pltpu.make_async_copy(src, dst, load_sems.at[i])
        for i, (src, dst) in enumerate(
            [
                (x_hbm, x_rows),
                (pre_grad_hbm, pre_grad),
                (hidden_hbm, hidden),
                (scaled_hbm, scaled),
                (returned_hbm, returned_ref),
                (router_ref, router_grad),
                (ids_hbm, ids_ref),
                (slots_hbm, slots_ref),
                (keep_hbm, keep_ref),
            ]
        )
    ]
    for load in loads:
        load.start()
    parts = 4
    copies = []

    def weight_grad(left, right, staged, target):
        step = staged.shape[0] // parts
        for p in range(parts):
            span = pl.ds(p * step, step)
            staged[span] = contract(left[:, span], right[...], 0, 0).astype(BF16)
            copies.append(
                pltpu.make_async_copy(staged.at[span], target.at[span], sems.at[len(copies)])
            )
            copies[-1].start()

    loads[0].wait()
    loads[1].wait()
    weight_grad(x_rows, pre_grad, g1, w_in_grad_hbm.at[0])
    loads[2].wait()
    loads[3].wait()
    weight_grad(hidden, scaled, g2, w_out_grad_hbm.at[0])
    for load in loads[4:]:
        load.wait()
    copies.append(pltpu.make_async_copy(router_grad, router_grad_hbm, sems.at[2 * parts]))
    copies[-1].start()
    z = lax.axis_index("expert") // SPLIT
    places = choice_places(z, window, ids_ref, slots_ref, keep_ref)
    spread_back = jnp.transpose(places[0] + places[1]).astype(BF16)
    rows = window * CAP
    chunks = in_grad.shape[1] // LANES
    back = chunks * rows
    row = iota((back, back), 0)
    source = ((row >> 1) & (window - 1)) * 16 + (row >> 3) * CAP + (row & 1)
    unfold = one_hot(iota((back, back), 1) == source).astype(BF16)
    flat = contract(unfold, returned_ref[...].reshape(back, LANES), 1, 0)
    returned = jnp.concatenate(
        [flat[c * rows : (c + 1) * rows] for c in range(chunks)], axis=1
    )
    returned = jnp.concatenate(
        [returned, jnp.zeros((LANES - rows, chunks * LANES), F32)], axis=0
    )
    in_grad[...] = contract(spread_back, returned.astype(BF16), 1, 0).astype(BF16)
    copies.append(pltpu.make_async_copy(in_grad, in_grad_hbm, sems.at[2 * parts + 1]))
    copies[-1].start()
    for copy in copies:
        copy.wait()


def fused_kernel(
    window,
    groups,
    tokens_hbm,
    out_grad_hbm,
    router_hbm,
    w_in_hbm,
    w_out_hbm,
    ids_hbm,
    slots_hbm,
    keep_hbm,
    x_out,
    pre_grad_out,
    hidden_out,
    scaled_out,
    returned_ref,
    router_grad_ref,
    ids_ref,
    slots_ref,
    keep_ref,
    tok,
    outg,
    w1,
    w2,
    pre_grad_ref,
    hidden_ref,
    scaled_ref,
    z_send,
    z_recv,
    w_recv,
    x_pack,
    dy_pack,
    xs,
    gv_send,
    gv_recv,
    gg,
    rp_send,
    rp_recv,
    coef_ref,
    rg_send,
    rg_recv,
    ret_send,
    ret_recv,
    load_sems,
    store_sems,
    zs,
    ws,
    xps,
    dps,
    gvs,
    ggs,
    rps,
    rgs,
    rts,
):
    plane = SPLIT * groups
    width = tok.shape[1]
    chunks = width // LANES
    rows = window * CAP
    message = z_send.shape[1]
    used = CAP * (2 * chunks + 1)
    columns, depth = router_hbm.shape
    ix = lax.axis_index("expert")
    g = lax.axis_index("group")
    z = ix // SPLIT
    y = lax.rem(ix, SPLIT)
    q = y * groups + g

    def z_up(d):
        return (lax.rem(z + d, window) * SPLIT + y, g)

    def z_down(d):
        return (lax.rem(z + window - d, window) * SPLIT + y, g)

    def in_plane(p):
        return (z * SPLIT + p // groups, lax.rem(p, groups))

    def q_up(d):
        return lax.rem(q + d, plane)

    def q_down(d):
        return lax.rem(q + plane - d, plane)

    def remote(src, dst, sems, target):
        return pltpu.make_async_remote_copy(
            src_ref=src,
            dst_ref=dst,
            send_sem=sems.at[0],
            recv_sem=sems.at[1],
            device_id=target,
            device_id_type=MESH,
        )

    def along_z(src, dst, sems, target_of):
        for d in range(1, window):
            remote(src(d), dst.at[d], sems, target_of(d)).start()
        every = dst.at[pl.ds(1, window - 1)]
        return remote(every, every, sems, target_of(1))

    def all_plane(src, dst, sems):
        for d in range(1, plane):
            target = q_up(d)
            remote(src(target), dst.at[q], sems, in_plane(target)).start()
        every = dst.at[pl.ds(0, plane - 1)]
        return remote(every, every, sems, in_plane(q_up(1)))

    barrier = pltpu.get_barrier_semaphore()
    for d in range(1, window):
        pl.semaphore_signal(barrier, inc=1, device_id=z_up(d), device_id_type=MESH)
    for d in range(1, plane):
        pl.semaphore_signal(barrier, inc=1, device_id=in_plane(q_up(d)), device_id_type=MESH)

    loads = [
        pltpu.make_async_copy(src, dst, load_sems.at[i])
        for i, (src, dst) in enumerate(
            [
                (ids_hbm, ids_ref),
                (slots_hbm, slots_ref),
                (keep_hbm, keep_ref),
                (tokens_hbm, tok),
                (out_grad_hbm, outg),
                (router_hbm, w_recv.at[0]),
                (w_in_hbm.at[0], w1),
                (w_out_hbm.at[0], w2),
            ]
        )
    ]
    for load in loads:
        load.start()

    depth_f = (2 * chunks + 2) * rows
    spread = []
    for d in range(window):
        row = iota((message, depth_f), 0)
        source = (row >> 1) * rows + d * CAP + (row & 1)
        spread.append(one_hot((iota((message, depth_f), 1) == source) & (row < used)))
    spread = jnp.concatenate(spread, axis=0).astype(BF16)
    half = width // 2
    side = chunks // 2
    wide = (chunks + 1) * 16
    row = iota((wide, window * message), 0)
    inner = row & 15
    column = row >> 4
    upper = jnp.where(inner < rows, 0, side)
    block = jnp.where(
        column < side,
        column + upper,
        jnp.where(column == side, 2 * chunks, chunks + column - side - 1 + upper),
    )
    source = ((inner & (rows - 1)) >> 1) * message + block * CAP + (inner & 1)
    gather = one_hot(iota((wide, window * message), 1) == source).astype(BF16)

    for load in loads[:3]:
        load.wait()
    places = choice_places(z, window, ids_ref, slots_ref, keep_ref)
    place = places[0] + places[1]
    place_rows = place[:16].astype(BF16)
    short = place[:rows]
    first_id = jnp.sum(short * ids_ref[0:1, :].astype(F32), axis=1, keepdims=True)
    second_id = jnp.sum(short * ids_ref[1:2, :].astype(F32), axis=1, keepdims=True)
    which = jnp.sum(places[0][:rows] - places[1][:rows], axis=1, keepdims=True)
    lane = iota((rows, LANES), 1)
    meta = jnp.where(
        lane == 0, first_id, jnp.where(lane == 1, second_id, jnp.where(lane == 2, which, 0.0))
    )

    loads[3].wait()
    loads[4].wait()
    x_slots = contract(place_rows, tok[...], 1, 0)[:rows]
    dy_slots = contract(place_rows, outg[...], 1, 0)[:rows]
    pieces = [x_slots[:, c * LANES : (c + 1) * LANES] for c in range(chunks)]
    pieces += [dy_slots[:, c * LANES : (c + 1) * LANES] for c in range(chunks)]
    pieces += [meta, jnp.zeros((rows, LANES), F32)]
    folded = jnp.concatenate(pieces, axis=0).astype(BF16)
    messages = contract(spread, folded, 1, 0).astype(BF16)
    z_recv[0] = messages[:message]
    for d in range(1, window):
        z_send[d] = messages[d * message : (d + 1) * message]
    pl.semaphore_wait(barrier, window - 1 + plane - 1)

    z_all = along_z(lambda d: z_send.at[d], z_recv, zs, z_up)
    loads[5].wait()
    w_all = along_z(lambda d: w_recv.at[0], w_recv, ws, z_up)
    z_all.wait_recv()
    gathered = contract(
        gather, z_recv[...].reshape(window * message, LANES), 1, 0
    ).astype(BF16)
    for c in range(side + 1):
        x_pack[q, :, c * LANES : (c + 1) * LANES] = gathered[c * 16 : (c + 1) * 16]
    for c in range(side):
        first = (side + 1 + c) * 16
        dy_pack[q, :, c * LANES : (c + 1) * LANES] = gathered[first : first + 16]

    def unfolded(block):
        return jnp.concatenate(
            [block[:, :rows, :half], block[:, rows:, :half]], axis=2
        ).reshape(plane * rows, width)

    xp_all = all_plane(lambda p: x_pack.at[q], x_pack, xps)
    dp_all = all_plane(lambda p: dy_pack.at[q], dy_pack, dps)
    z_all.wait_send()
    w_all.wait()
    router = w_recv[...].reshape(window * columns, depth)
    xp_all.wait_recv()

    total = plane * rows
    packed = x_pack[...].astype(F32)
    x_rows = unfolded(packed).astype(BF16)
    info = packed[:, :rows, half:].reshape(total, LANES)
    xs[...] = x_rows
    x_part = xs[:, pl.ds(pl.multiple_of(g * depth, LANES), depth)]

    column = iota((total, window * columns), 1)
    owner = lax.rem(z + window - column // columns, window)
    column_id = ((owner * SPLIT + y) * columns + lax.rem(column, columns)).astype(F32)
    hot = one_hot(info[:, 0:1] == column_id) - one_hot(info[:, 1:2] == column_id)
    sign = info[:, 2:3]
    gap_part = jnp.sum(contract(x_part, router, 1, 1) * hot, axis=1, keepdims=True)
    row_diff = contract(hot.astype(BF16), router, 1, 0)
    eye = iota((total, LANES), 0) == iota((total, LANES), 1)
    gap_row = jnp.sum(jnp.where(eye, gap_part, 0.0), axis=0, keepdims=True)
    gv_send[:, :, :depth] = row_diff.reshape(plane, rows, depth)
    gv_send[:, :, depth:] = jnp.broadcast_to(gap_row[None], (plane, rows, LANES))
    gv_recv[q] = gv_send[q]
    gv_all = all_plane(lambda p: gv_send.at[p], gv_recv, gvs)

    loads[6].wait()
    pre_act = contract(x_rows, w1[...], 1, 0)
    loads[7].wait()
    dp_all.wait_recv()
    dy_rows = unfolded(dy_pack[...].astype(F32)).astype(BF16)
    back_up = contract(dy_rows, w2[...], 1, 1)
    gelu_value, gelu_slope = gelu_parts(pre_act)
    gate_part = jnp.sum(back_up * gelu_value, axis=1, keepdims=True)
    gate_row = jnp.sum(jnp.where(eye, gate_part, 0.0), axis=0, keepdims=True)
    gg[q] = jnp.broadcast_to(gate_row, (rows, LANES))
    gg_all = all_plane(lambda p: gg.at[q], gg, ggs)

    gv_all.wait_recv()
    gap_sum = jnp.sum(gv_recv[:, 0:1, depth:], axis=0)
    gap = jnp.sum(jnp.where(eye, gap_sum, 0.0), axis=1, keepdims=True)
    combine_first = jax.nn.sigmoid(gap)
    combine_second = jax.nn.sigmoid(-gap)
    gate = jnp.where(sign > 0.5, combine_first, jnp.where(sign < -0.5, combine_second, 0.0))
    gate = gate.astype(BF16).astype(F32)
    pre_grad = (gate * back_up * gelu_slope).astype(BF16)
    rp_all = []
    for h in range(2):
        part = contract(pre_grad, w1[h * half : (h + 1) * half, :], 1, 1)
        part = part.reshape(plane, rows, half)
        rp_send[h] = jnp.concatenate(
            [part[:, :, : half // 2], part[:, :, half // 2 :]], axis=1
        ).astype(BF16)
        rp_recv[h, q] = rp_send[h, q]
        rp_all.append(all_plane(lambda p, h=h: rp_send.at[h, p], rp_recv.at[h], rps.at[h]))

    gg_all.wait_recv()
    grad_sum = jnp.sum(gg[:, 0:1, :], axis=0)
    gate_grad = jnp.sum(jnp.where(eye, grad_sum, 0.0), axis=1, keepdims=True)
    coef = sign * combine_first * combine_second * gate_grad
    coef_ref[...] = jnp.broadcast_to(coef, (total, LANES))
    logit_grad = coef * hot
    high = logit_grad.astype(BF16)
    low = (logit_grad - high.astype(F32)).astype(BF16)
    router_part = contract(
        jnp.concatenate([high, low], axis=0), jnp.concatenate([x_part, x_part], axis=0), 0, 0
    )
    for d in range(1, window):
        rg_send[d] = router_part[d * columns : (d + 1) * columns].astype(BF16)
    rg_all = along_z(lambda d: rg_send.at[d], rg_recv, rgs, z_down)

    pre_grad_ref[...] = pre_grad
    hidden_ref[...] = gelu_value.astype(BF16)
    scaled_ref[...] = (gate * dy_rows.astype(F32)).astype(BF16)
    stores = [
        pltpu.make_async_copy(src, dst, store_sems.at[i])
        for i, (src, dst) in enumerate(
            [
                (xs, x_out),
                (pre_grad_ref, pre_grad_out),
                (hidden_ref, hidden_out),
                (scaled_ref, scaled_out),
            ]
        )
    ]
    for store in stores:
        store.start()

    for sent in (xp_all, dp_all, gv_all, gg_all):
        sent.wait_send()
    halves = []
    for h in range(2):
        rp_all[h].wait_recv()
        summed = jnp.sum(rp_recv[h].astype(F32), axis=0)
        halves += [summed[:rows], summed[rows:]]
    row_grad = jnp.concatenate(halves, axis=1)
    diffs = []
    for part in range(groups):
        diff = gv_recv[part, :, :depth]
        for other in range(1, SPLIT):
            diff = diff + gv_recv[other * groups + part, :, :depth]
        diffs.append(diff)
    own_coef = coef_ref[pl.ds(pl.multiple_of(q * rows, rows), rows), 0:1]
    row_grad = row_grad + own_coef * jnp.concatenate(diffs, axis=1)
    folded = jnp.concatenate(
        [row_grad[:, c * LANES : (c + 1) * LANES] for c in range(chunks)], axis=0
    ).astype(BF16)
    back = chunks * rows
    row = iota((back, back), 0)
    source = ((row >> 1) & (chunks - 1)) * rows + (row >> 4) * CAP + (row & 1)
    fold = one_hot(iota((back, back), 1) == source).astype(BF16)
    ret_send[...] = contract(fold, folded, 1, 0).astype(BF16).reshape(ret_send.shape)
    ret_recv[0] = ret_send[0]
    ret_all = along_z(lambda d: ret_send.at[d], ret_recv, rts, z_down)

    for sent in (*rp_all, rg_all):
        sent.wait_send()
    for store in stores:
        store.wait()
    rg_all.wait_recv()
    router_grad_ref[...] = router_part[:columns] + jnp.sum(
        rg_recv[1:].astype(F32), axis=0
    )
    ret_all.wait()
    returned_ref[...] = ret_recv[...]


def fused(tokens, out_grad, w_router, w_in, w_out, expert_ids, slot_ids, keep_mask):
    window = lax.axis_size("expert") // SPLIT
    groups = lax.axis_size("group")
    plane = SPLIT * groups
    count, width = tokens.shape
    hidden = w_in.shape[2]
    depth, columns = w_router.shape
    rows = window * CAP
    message = -(-CAP * (2 * width // LANES + 1) // 16) * 16
    vmem = pl.BlockSpec(memory_space=pltpu.VMEM)
    hbm = pl.BlockSpec(memory_space=pltpu.HBM)
    dma = pltpu.SemaphoreType.DMA
    routing = (expert_ids.T, slot_ids.T, keep_mask.T)
    total = plane * rows
    *handed, returned, router_part = pl.pallas_call(
        functools.partial(fused_kernel, window, groups),
        out_shape=(
            jax.ShapeDtypeStruct((total, width), BF16),
            jax.ShapeDtypeStruct((total, hidden), BF16),
            jax.ShapeDtypeStruct((total, hidden), BF16),
            jax.ShapeDtypeStruct((total, width), BF16),
            jax.ShapeDtypeStruct((window, 16, LANES), BF16),
            jax.ShapeDtypeStruct((columns, depth), F32),
        ),
        in_specs=[hbm] * 8,
        out_specs=(hbm, hbm, hbm, hbm, vmem, vmem),
        scratch_shapes=[
            pltpu.VMEM(expert_ids.shape[::-1], jnp.int32),
            pltpu.VMEM(slot_ids.shape[::-1], jnp.int32),
            pltpu.VMEM(keep_mask.shape[::-1], jnp.int32),
            pltpu.VMEM((count, width), BF16),
            pltpu.VMEM((count, width), BF16),
            pltpu.VMEM((width, hidden), BF16),
            pltpu.VMEM((hidden, width), BF16),
            pltpu.VMEM((total, hidden), BF16),
            pltpu.VMEM((total, hidden), BF16),
            pltpu.VMEM((total, width), BF16),
            pltpu.VMEM((window, message, LANES), BF16),
            pltpu.VMEM((window, message, LANES), BF16),
            pltpu.VMEM((window, columns, depth), BF16),
            pltpu.VMEM((plane, 16, width // 2 + LANES), BF16),
            pltpu.VMEM((plane, 16, width // 2), BF16),
            pltpu.VMEM((plane * rows, width), BF16),
            pltpu.VMEM((plane, rows, depth + LANES), F32),
            pltpu.VMEM((plane, rows, depth + LANES), F32),
            pltpu.VMEM((plane, rows, LANES), F32),
            pltpu.VMEM((2, plane, 16, width // 4), BF16),
            pltpu.VMEM((2, plane, 16, width // 4), BF16),
            pltpu.VMEM((plane * rows, LANES), F32),
            pltpu.VMEM((window, columns, depth), BF16),
            pltpu.VMEM((window, columns, depth), BF16),
            pltpu.VMEM((window, 16, LANES), BF16),
            pltpu.VMEM((window, 16, LANES), BF16),
            dma((8,)),
            dma((4,)),
        ]
        + [dma((2,))] * 6
        + [dma((2, 2))]
        + [dma((2,))] * 2,
        compiler_params=pltpu.CompilerParams(
            collective_id=0, has_side_effects=True, vmem_limit_bytes=60 * 1024 * 1024
        ),
    )(
        tokens,
        out_grad,
        w_router.T,
        w_in,
        w_out,
        *routing,
    )
    in_grad, w_in_grad, w_out_grad, router_grad = pl.pallas_call(
        functools.partial(finish_kernel, window),
        out_shape=(
            jax.ShapeDtypeStruct((count, width), BF16),
            jax.ShapeDtypeStruct(w_in.shape, BF16),
            jax.ShapeDtypeStruct(w_out.shape, BF16),
            jax.ShapeDtypeStruct((columns, depth), F32),
        ),
        in_specs=[hbm] * 9,
        out_specs=(hbm, hbm, hbm, hbm),
        scratch_shapes=[
            pltpu.VMEM((total, width), BF16),
            pltpu.VMEM((total, hidden), BF16),
            pltpu.VMEM((total, hidden), BF16),
            pltpu.VMEM((total, width), BF16),
            pltpu.VMEM((columns, depth), F32),
            pltpu.VMEM((width, hidden), BF16),
            pltpu.VMEM((hidden, width), BF16),
            pltpu.VMEM((count, width), BF16),
            pltpu.VMEM((window, 16, LANES), BF16),
            pltpu.VMEM(expert_ids.shape[::-1], jnp.int32),
            pltpu.VMEM(slot_ids.shape[::-1], jnp.int32),
            pltpu.VMEM(keep_mask.shape[::-1], jnp.int32),
            dma((10,)),
            dma((9,)),
        ],
        compiler_params=pltpu.CompilerParams(vmem_limit_bytes=60 * 1024 * 1024),
    )(*handed, returned, router_part, *routing)
    return (in_grad, w_in_grad, w_out_grad, router_grad.T)


def body(*args):
    tokens, _, w_router = args[:3]
    window = lax.axis_size("expert") // SPLIT
    fits = (
        window * CAP == 8
        and w_router.shape[1] % 16 == 0
        and w_router.shape[0] % LANES == 0
        and window * w_router.shape[1] == LANES
        and SPLIT * lax.axis_size("group") * window * CAP <= LANES
        and tokens.shape == (LANES, 8 * LANES)
    )
    return fused(*args) if fits else gathered_body(*args)


def solution(mesh):
    return jax.shard_map(
        body,
        mesh=mesh,
        in_specs=(
            P(("expert", "group"), None),
            P(("expert", "group"), None),
            P("group", "expert"),
            P("expert", None, "group"),
            P("expert", "group", None),
            P(("expert", "group"), None),
            P(("expert", "group"), None),
            P(("expert", "group"), None),
        ),
        out_specs=(
            P(("expert", "group"), None),
            P("expert", None, "group"),
            P("expert", "group", None),
            P("group", "expert"),
        ),
        check_vma=False,
    )
```

```python
import functools

import jax
import jax.numpy as jnp
from jax import lax
from jax.experimental import pallas as pl
from jax.experimental.pallas import tpu as pltpu
from jax.sharding import PartitionSpec as P

CAP = 2
SPLIT = 2
LANES = 128
F32 = jnp.float32
BF16 = jnp.bfloat16
MESH = pl.DeviceIdType.MESH


def gelu_parts(pre_act):
    cubic_term = 0.044715 * pre_act * pre_act * pre_act
    tanh_value = jnp.tanh(0.7978845608028654 * (pre_act + cubic_term))
    gelu_value = 0.5 * pre_act * (1.0 + tanh_value)
    gelu_slope = 0.5 * (1.0 + tanh_value) + 0.5 * pre_act * (
        1.0 - tanh_value * tanh_value
    ) * 0.7978845608028654 * (1.0 + 3.0 * 0.044715 * pre_act * pre_act)
    return (gelu_value, gelu_slope)


def expert_rows(w_in_local, w_out_local, pieces):
    x_piece, dy_piece, gate_piece = pieces
    gate_col = gate_piece.astype(jnp.float32)[:, None]
    pre_act = jnp.dot(x_piece, w_in_local, preferred_element_type=jnp.float32)
    gelu_value, gelu_slope = gelu_parts(pre_act)
    back_up = jnp.einsum("rd,hd->rh", dy_piece, w_out_local, preferred_element_type=jnp.float32)
    gate_piece_sum = jnp.sum(back_up * gelu_value, axis=1)
    pre_grad = (gate_col * back_up * gelu_slope).astype(jnp.bfloat16)
    scaled_grad = (gate_col * dy_piece.astype(jnp.float32)).astype(jnp.bfloat16)
    sum_in = jnp.einsum("rd,rh->dh", x_piece, pre_grad, preferred_element_type=jnp.float32)
    sum_out = jnp.einsum(
        "rh,rd->hd",
        gelu_value.astype(jnp.bfloat16),
        scaled_grad,
        preferred_element_type=jnp.float32,
    )
    part_rows = jnp.einsum("rh,dh->rd", pre_grad, w_in_local, preferred_element_type=jnp.float32)
    return (sum_in, sum_out, part_rows, gate_piece_sum)


def gathered_body(tokens, out_grad, w_router, w_in, w_out, expert_ids, slot_ids, keep_mask):
    expert_count = lax.axis_size("expert")
    window = expert_count // SPLIT
    slot_count = window * CAP
    model_width = tokens.shape[1]
    router_full = lax.all_gather(
        lax.all_gather(w_router, "expert", axis=1, tiled=True), "group", axis=0, tiled=True
    )
    logits = jnp.dot(tokens, router_full, preferred_element_type=jnp.float32)
    uniform_samples = jnp.arange(router_full.shape[1], dtype=jnp.int32)
    first_hot = (expert_ids[:, 0:1] == uniform_samples[None, :]).astype(jnp.float32)
    second_hot = (expert_ids[:, 1:2] == uniform_samples[None, :]).astype(jnp.float32)
    logit_gap = jnp.sum(logits * first_hot, axis=1) - jnp.sum(logits * second_hot, axis=1)
    combine = jnp.stack([jax.nn.sigmoid(logit_gap), jax.nn.sigmoid(-logit_gap)], axis=1)
    active = (keep_mask == 1) & (expert_ids < window)
    slot_code = jnp.where(active, expert_ids * CAP + slot_ids, -1)
    slot_axis = jnp.arange(slot_count, dtype=jnp.int32)
    place_first = (slot_code[:, 0:1] == slot_axis[None, :]).astype(jnp.float32)
    place_second = (slot_code[:, 1:2] == slot_axis[None, :]).astype(jnp.float32)
    placement = place_first + place_second
    place_round = placement.astype(jnp.bfloat16)
    token_slots = jnp.einsum(
        "ts,td->sd", place_round, tokens, preferred_element_type=jnp.float32
    ).astype(jnp.bfloat16)
    grad_slots = jnp.einsum(
        "ts,td->sd", place_round, out_grad, preferred_element_type=jnp.float32
    ).astype(jnp.bfloat16)
    gate_slots = jnp.sum(
        place_first * combine[:, 0:1] + place_second * combine[:, 1:2], axis=0
    ).astype(jnp.bfloat16)
    token_send = jnp.repeat(token_slots.reshape(window, CAP, model_width), SPLIT, axis=0)
    grad_send = jnp.repeat(grad_slots.reshape(window, CAP, model_width), SPLIT, axis=0)
    gate_send = jnp.repeat(gate_slots.reshape(window, CAP), SPLIT, axis=0)
    token_recv, grad_recv, gate_recv = (
        lax.all_to_all(token_send, "expert", split_axis=0, concat_axis=0, tiled=True),
        lax.all_to_all(grad_send, "expert", split_axis=0, concat_axis=0, tiled=True),
        lax.all_to_all(gate_send, "expert", split_axis=0, concat_axis=0, tiled=True),
    )
    row_count = expert_count * CAP
    token_rows = token_recv.reshape(row_count, model_width)
    grad_rows = grad_recv.reshape(row_count, model_width)
    gate_rows = gate_recv.reshape(row_count)
    w_in_local = w_in[0]
    w_out_local = w_out[0]
    sum_in, sum_out, row_parts, gate_parts = expert_rows(
        w_in_local,
        w_out_local,
        (
            lax.all_gather(token_rows, "group", axis=0, tiled=True),
            lax.all_gather(grad_rows, "group", axis=0, tiled=True),
            lax.all_gather(gate_rows, "group", axis=0, tiled=True),
        ),
    )
    w_in_grad = sum_in.astype(jnp.bfloat16)[None]
    w_out_grad = sum_out.astype(jnp.bfloat16)[None]
    row_sums = lax.psum_scatter(
        row_parts.astype(jnp.bfloat16), "group", scatter_dimension=0, tiled=True
    ).astype(jnp.float32)
    gate_sums = lax.psum_scatter(gate_parts, "group", scatter_dimension=0, tiled=True)
    rows_back, gates_back = (
        lax.all_to_all(
            row_sums.reshape(expert_count, CAP, model_width).astype(jnp.bfloat16),
            "expert",
            split_axis=0,
            concat_axis=0,
            tiled=True,
        ).astype(jnp.float32),
        lax.all_to_all(
            gate_sums.reshape(expert_count, CAP).astype(jnp.bfloat16),
            "expert",
            split_axis=0,
            concat_axis=0,
            tiled=True,
        ).astype(jnp.float32),
    )
    rows_back = jnp.sum(rows_back.reshape(window, SPLIT, CAP, model_width), axis=1).reshape(
        slot_count, model_width
    )
    gates_back = jnp.sum(gates_back.reshape(window, SPLIT, CAP), axis=1).reshape(slot_count)
    expert_part = jnp.dot(placement, rows_back, precision=lax.Precision.HIGHEST)
    gate_first = jnp.sum(place_first * gates_back[None, :], axis=1)
    gate_second = jnp.sum(place_second * gates_back[None, :], axis=1)
    gate_slope = combine[:, 0] * combine[:, 1] * (gate_first - gate_second)
    logit_grad = first_hot * gate_slope[:, None] - second_hot * gate_slope[:, None]
    router_part = jnp.dot(
        logit_grad, router_full.astype(jnp.float32).T, precision=lax.Precision.HIGHEST
    )
    in_grad = (expert_part + router_part).astype(jnp.bfloat16)
    router_sum = jnp.dot(tokens.astype(jnp.float32).T, logit_grad, precision=lax.Precision.HIGHEST)
    router_grad = lax.psum_scatter(
        lax.psum_scatter(router_sum, "expert", scatter_dimension=1, tiled=True),
        "group",
        scatter_dimension=0,
        tiled=True,
    )
    return (in_grad, w_in_grad, w_out_grad, router_grad)


def iota(shape, axis):
    return lax.broadcasted_iota(jnp.int32, shape, axis)


def one_hot(mask):
    return jnp.where(mask, 1.0, 0.0).astype(F32)


def contract(left, right, left_axis, right_axis):
    return lax.dot_general(
        left, right, (((left_axis,), (right_axis,)), ((), ())), preferred_element_type=F32
    )


def choice_places(count, z, window, ids_ref, slots_ref, keep_ref):
    places = []
    for k in range(2):
        ids = ids_ref[k : k + 1, :]
        relative = jnp.where(ids < z, ids - z + window, ids - z)
        active = (keep_ref[k : k + 1, :] == 1) & (ids < window)
        code = jnp.where(active, relative * CAP + slots_ref[k : k + 1, :], -1)
        places.append(one_hot(iota((count, LANES), 0) == code))
    return places


def finish_kernel(
    window,
    g1_hbm,
    g2_hbm,
    returned_hbm,
    router_hbm,
    ids_hbm,
    slots_hbm,
    keep_hbm,
    in_grad_hbm,
    w_in_grad_hbm,
    w_out_grad_hbm,
    router_grad_hbm,
    g1,
    g2,
    router_grad,
    in_grad,
    returned_ref,
    ids_ref,
    slots_ref,
    keep_ref,
    sems,
    load_sems,
):
    parts = 4
    loads, stores = [], []
    for src, staged, dst, pieces in (
        (ids_hbm, ids_ref, None, 1),
        (slots_hbm, slots_ref, None, 1),
        (keep_hbm, keep_ref, None, 1),
        (returned_hbm, returned_ref, None, 1),
        (router_hbm, router_grad, router_grad_hbm, 1),
        (g1_hbm, g1, w_in_grad_hbm.at[0], parts),
        (g2_hbm, g2, w_out_grad_hbm.at[0], parts),
    ):
        step = src.shape[0] // pieces
        for p in range(pieces):
            span = pl.ds(p * step, step)
            whole = pieces == 1
            loads.append(
                pltpu.make_async_copy(
                    src if whole else src.at[span],
                    staged if whole else staged.at[span],
                    load_sems.at[len(loads)],
                )
            )
            if dst is not None:
                stores.append(
                    pltpu.make_async_copy(
                        staged if whole else staged.at[span],
                        dst if whole else dst.at[span],
                        sems.at[len(stores)],
                    )
                )
    for load in loads:
        load.start()
    rows = window * CAP
    chunks = in_grad.shape[1] // LANES
    back = chunks * rows
    row = iota((back, back), 0)
    source = ((row >> 1) & (window - 1)) * 16 + (row >> 3) * CAP + (row & 1)
    unfold = one_hot(iota((back, back), 1) == source).astype(BF16)
    z = lax.axis_index("expert") // SPLIT
    for load in loads[:3]:
        load.wait()
    places = choice_places(LANES, z, window, ids_ref, slots_ref, keep_ref)
    spread_back = jnp.transpose(places[0] + places[1]).astype(BF16)
    loads[3].wait()
    flat = contract(unfold, returned_ref[...].reshape(back, LANES), 1, 0)
    returned = jnp.concatenate(
        [flat[c * rows : (c + 1) * rows] for c in range(chunks)], axis=1
    )
    returned = jnp.concatenate(
        [returned, jnp.zeros((LANES - rows, chunks * LANES), F32)], axis=0
    ).astype(BF16)
    for load, store in zip(loads[4:], stores):
        load.wait()
        store.start()
    in_grad[...] = contract(spread_back, returned, 1, 0).astype(BF16)
    stores.append(pltpu.make_async_copy(in_grad, in_grad_hbm, sems.at[len(stores)]))
    stores[-1].start()
    for store in stores:
        store.wait()


def fused_kernel(
    window,
    groups,
    tokens_hbm,
    out_grad_hbm,
    router_hbm,
    w_in_hbm,
    w_out_hbm,
    ids_hbm,
    slots_hbm,
    keep_hbm,
    g1_out,
    g2_out,
    returned_out,
    router_grad_out,
    ids_ref,
    slots_ref,
    keep_ref,
    tok,
    outg,
    w1,
    w2,
    g1,
    g2,
    router_grad_ref,
    z_send,
    z_recv,
    w_recv,
    x_pack,
    dy_pack,
    xs,
    gv_send,
    gv_recv,
    gg,
    rp_send,
    rp_recv,
    coef_ref,
    rg_send,
    rg_recv,
    ret_send,
    ret_recv,
    load_sems,
    store_sems,
    zs,
    ws,
    xps,
    dps,
    gvs,
    ggs,
    rps,
    rgs,
    rts,
):
    plane = SPLIT * groups
    width = tok.shape[1]
    chunks = width // LANES
    rows = window * CAP
    message = z_send.shape[1]
    used = CAP * (2 * chunks + 1)
    columns, depth = router_hbm.shape
    ix = lax.axis_index("expert")
    g = lax.axis_index("group")
    z = ix // SPLIT
    y = lax.rem(ix, SPLIT)
    q = y * groups + g

    def z_up(d):
        return (lax.rem(z + d, window) * SPLIT + y, g)

    def z_down(d):
        return (lax.rem(z + window - d, window) * SPLIT + y, g)

    def in_plane(p):
        return (z * SPLIT + p // groups, lax.rem(p, groups))

    def q_up(d):
        return lax.rem(q + d, plane)

    def q_down(d):
        return lax.rem(q + plane - d, plane)

    def remote(src, dst, sems, target):
        return pltpu.make_async_remote_copy(
            src_ref=src,
            dst_ref=dst,
            send_sem=sems.at[0],
            recv_sem=sems.at[1],
            device_id=target,
            device_id_type=MESH,
        )

    def along_z(src, dst, sems, target_of):
        for d in range(1, window):
            remote(src(d), dst.at[d], sems, target_of(d)).start()
        every = dst.at[pl.ds(1, window - 1)]
        return remote(every, every, sems, target_of(1))

    def all_plane(src, dst, sems):
        for d in range(1, plane):
            target = q_up(d)
            remote(src(target), dst.at[q], sems, in_plane(target)).start()
        every = dst.at[pl.ds(0, plane - 1)]
        return remote(every, every, sems, in_plane(q_up(1)))

    barrier = pltpu.get_barrier_semaphore()
    for d in range(1, window):
        pl.semaphore_signal(barrier, inc=1, device_id=z_up(d), device_id_type=MESH)
    for d in range(1, plane):
        pl.semaphore_signal(barrier, inc=1, device_id=in_plane(q_up(d)), device_id_type=MESH)

    loads = [
        pltpu.make_async_copy(src, dst, load_sems.at[i])
        for i, (src, dst) in enumerate(
            [
                (ids_hbm, ids_ref),
                (slots_hbm, slots_ref),
                (keep_hbm, keep_ref),
                (tokens_hbm, tok),
                (out_grad_hbm, outg),
                (router_hbm, w_recv.at[0]),
                (w_in_hbm.at[0], w1),
                (w_out_hbm.at[0], w2),
            ]
        )
    ]
    for load in loads:
        load.start()

    depth_f = (2 * chunks + 2) * rows
    spread = []
    for d in range(window):
        row = iota((message, depth_f), 0)
        source = (row >> 1) * rows + d * CAP + (row & 1)
        spread.append(one_hot((iota((message, depth_f), 1) == source) & (row < used)))
    spread = jnp.concatenate(spread, axis=0).astype(BF16)
    half = width // 2
    side = chunks // 2
    wide = (chunks + 1) * 16
    row = iota((wide, window * message), 0)
    inner = row & 15
    column = row >> 4
    upper = jnp.where(inner < rows, 0, side)
    block = jnp.where(
        column < side,
        column + upper,
        jnp.where(column == side, 2 * chunks, chunks + column - side - 1 + upper),
    )
    source = ((inner & (rows - 1)) >> 1) * message + block * CAP + (inner & 1)
    gather = one_hot(iota((wide, window * message), 1) == source).astype(BF16)

    for load in loads[:3]:
        load.wait()
    places = choice_places(16, z, window, ids_ref, slots_ref, keep_ref)
    place = places[0] + places[1]
    place_rows = place.astype(BF16)
    short = place[:rows]
    first_id = jnp.sum(short * ids_ref[0:1, :].astype(F32), axis=1, keepdims=True)
    second_id = jnp.sum(short * ids_ref[1:2, :].astype(F32), axis=1, keepdims=True)
    which = jnp.sum(places[0][:rows] - places[1][:rows], axis=1, keepdims=True)
    lane = iota((rows, LANES), 1)
    meta = jnp.where(
        lane == 0, first_id, jnp.where(lane == 1, second_id, jnp.where(lane == 2, which, 0.0))
    )

    loads[3].wait()
    loads[4].wait()
    x_slots = contract(place_rows, tok[...], 1, 0)[:rows]
    dy_slots = contract(place_rows, outg[...], 1, 0)[:rows]
    pieces = [x_slots[:, c * LANES : (c + 1) * LANES] for c in range(chunks)]
    pieces += [dy_slots[:, c * LANES : (c + 1) * LANES] for c in range(chunks)]
    pieces += [meta, jnp.zeros((rows, LANES), F32)]
    folded = jnp.concatenate(pieces, axis=0).astype(BF16)
    messages = contract(spread, folded, 1, 0).astype(BF16)
    z_recv[0] = messages[:message]
    for d in range(1, window):
        z_send[d] = messages[d * message : (d + 1) * message]
    pl.semaphore_wait(barrier, window - 1 + plane - 1)

    z_all = along_z(lambda d: z_send.at[d], z_recv, zs, z_up)
    total = plane * rows
    eye = iota((total, LANES), 0) == iota((total, LANES), 1)
    column = iota((1, window * columns), 1)
    owner = lax.rem(z + window - column // columns, window)
    column_id = ((owner * SPLIT + y) * columns + lax.rem(column, columns)).astype(F32)
    loads[5].wait()
    w_all = along_z(lambda d: w_recv.at[0], w_recv, ws, z_up)
    z_all.wait_recv()
    gathered = contract(
        gather, z_recv[...].reshape(window * message, LANES), 1, 0
    ).astype(BF16)
    for c in range(side + 1):
        x_pack[q, :, c * LANES : (c + 1) * LANES] = gathered[c * 16 : (c + 1) * 16]
    for c in range(side):
        first = (side + 1 + c) * 16
        dy_pack[q, :, c * LANES : (c + 1) * LANES] = gathered[first : first + 16]

    def unfolded(block):
        return jnp.concatenate(
            [block[:, :rows, :half], block[:, rows:, :half]], axis=2
        ).reshape(plane * rows, width)

    xp_all = all_plane(lambda p: x_pack.at[q], x_pack, xps)
    dp_all = all_plane(lambda p: dy_pack.at[q], dy_pack, dps)
    z_all.wait_send()
    w_all.wait()
    router = w_recv[...].reshape(window * columns, depth)
    xp_all.wait_recv()

    packed = x_pack[...].astype(F32)
    x_rows = unfolded(packed).astype(BF16)
    info = packed[:, :rows, half:].reshape(total, LANES)
    xs[...] = x_rows
    x_part = xs[:, pl.ds(pl.multiple_of(g * depth, LANES), depth)]

    hot = one_hot(info[:, 0:1] == column_id) - one_hot(info[:, 1:2] == column_id)
    sign = info[:, 2:3]
    gap_part = jnp.sum(contract(x_part, router, 1, 1) * hot, axis=1, keepdims=True)
    row_diff = contract(hot.astype(BF16), router, 1, 0)
    gap_row = jnp.sum(jnp.where(eye, gap_part, 0.0), axis=0, keepdims=True)
    gv_send[:, :, :depth] = row_diff.reshape(plane, rows, depth)
    gv_send[:, :, depth:] = jnp.broadcast_to(gap_row[None], (plane, rows, LANES))
    gv_recv[q] = gv_send[q]
    gv_all = all_plane(lambda p: gv_send.at[p], gv_recv, gvs)

    loads[6].wait()
    pre_act = contract(x_rows, w1[...], 1, 0)
    loads[7].wait()
    dp_all.wait_recv()
    dy_rows = unfolded(dy_pack[...].astype(F32)).astype(BF16)
    back_up = contract(dy_rows, w2[...], 1, 1)
    gelu_value, gelu_slope = gelu_parts(pre_act)
    gate_part = jnp.sum(back_up * gelu_value, axis=1, keepdims=True)
    gate_row = jnp.sum(jnp.where(eye, gate_part, 0.0), axis=0, keepdims=True)
    gg[q] = jnp.broadcast_to(gate_row, (rows, LANES))
    gg_all = all_plane(lambda p: gg.at[q], gg, ggs)

    gv_all.wait_recv()
    gap_sum = jnp.sum(gv_recv[:, 0:1, depth:], axis=0)
    gap = jnp.sum(jnp.where(eye, gap_sum, 0.0), axis=1, keepdims=True)
    combine_first = jax.nn.sigmoid(gap)
    combine_second = jax.nn.sigmoid(-gap)
    gate = jnp.where(sign > 0.5, combine_first, jnp.where(sign < -0.5, combine_second, 0.0))
    gate = gate.astype(BF16).astype(F32)
    pre_grad = (gate * back_up * gelu_slope).astype(BF16)
    rp_all = []
    for h in range(2):
        part = contract(pre_grad, w1[h * half : (h + 1) * half, :], 1, 1)
        part = part.reshape(plane, rows, half)
        rp_send[h] = jnp.concatenate(
            [part[:, :, : half // 2], part[:, :, half // 2 :]], axis=1
        ).astype(BF16)
        rp_recv[h, q] = rp_send[h, q]
        rp_all.append(all_plane(lambda p, h=h: rp_send.at[h, p], rp_recv.at[h], rps.at[h]))

    gg_all.wait_recv()
    grad_sum = jnp.sum(gg[:, 0:1, :], axis=0)
    gate_grad = jnp.sum(jnp.where(eye, grad_sum, 0.0), axis=1, keepdims=True)
    coef = sign * combine_first * combine_second * gate_grad
    coef_ref[...] = jnp.broadcast_to(coef, (total, LANES))
    logit_grad = coef * hot
    high = logit_grad.astype(BF16)
    low = (logit_grad - high.astype(F32)).astype(BF16)
    router_part = contract(
        jnp.concatenate([high, low], axis=0), jnp.concatenate([x_part, x_part], axis=0), 0, 0
    )
    for d in range(1, window):
        rg_send[d] = router_part[d * columns : (d + 1) * columns].astype(BF16)
    rg_all = along_z(lambda d: rg_send.at[d], rg_recv, rgs, z_down)

    diffs = []
    for part in range(groups):
        diff = gv_recv[part, :, :depth]
        for other in range(1, SPLIT):
            diff = diff + gv_recv[other * groups + part, :, :depth]
        diffs.append(diff)
    own_coef = coef_ref[pl.ds(pl.multiple_of(q * rows, rows), rows), 0:1]
    router_rows = own_coef * jnp.concatenate(diffs, axis=1)
    back = chunks * rows
    row = iota((back, back), 0)
    source = ((row >> 1) & (chunks - 1)) * rows + (row >> 4) * CAP + (row & 1)
    fold = one_hot(iota((back, back), 1) == source).astype(BF16)

    stores = []

    def weight_grad(left, right, staged, target):
        parts = 4
        step = staged.shape[0] // parts
        for p in range(parts):
            span = slice(p * step, (p + 1) * step)
            staged[span] = contract(left[:, span], right, 0, 0).astype(BF16)
            stores.append(
                pltpu.make_async_copy(
                    staged.at[span], target.at[span], store_sems.at[len(stores)]
                )
            )
            stores[-1].start()

    weight_grad(x_rows, pre_grad, g1, g1_out)
    for sent in (xp_all, dp_all, gv_all, gg_all):
        sent.wait_send()
    halves = []
    for h in range(2):
        rp_all[h].wait_recv()
        summed = jnp.sum(rp_recv[h].astype(F32), axis=0)
        halves += [summed[:rows], summed[rows:]]
    row_grad = jnp.concatenate(halves, axis=1)
    row_grad = row_grad + router_rows
    folded = jnp.concatenate(
        [row_grad[:, c * LANES : (c + 1) * LANES] for c in range(chunks)], axis=0
    ).astype(BF16)
    ret_send[...] = contract(fold, folded, 1, 0).astype(BF16).reshape(ret_send.shape)
    ret_recv[0] = ret_send[0]
    ret_all = along_z(lambda d: ret_send.at[d], ret_recv, rts, z_down)

    rg_all.wait_recv()
    router_grad_ref[...] = router_part[:columns] + jnp.sum(
        rg_recv[1:].astype(F32), axis=0
    )
    stores.append(
        pltpu.make_async_copy(router_grad_ref, router_grad_out, store_sems.at[len(stores)])
    )
    stores[-1].start()
    scaled_grad = (gate * dy_rows.astype(F32)).astype(BF16)
    weight_grad(gelu_value.astype(BF16), scaled_grad, g2, g2_out)
    for sent in (*rp_all, rg_all):
        sent.wait_send()
    ret_all.wait_recv()
    stores.append(
        pltpu.make_async_copy(ret_recv, returned_out, store_sems.at[len(stores)])
    )
    stores[-1].start()
    ret_all.wait_send()
    for store in stores:
        store.wait()


def fused(tokens, out_grad, w_router, w_in, w_out, expert_ids, slot_ids, keep_mask):
    window = lax.axis_size("expert") // SPLIT
    groups = lax.axis_size("group")
    plane = SPLIT * groups
    count, width = tokens.shape
    hidden = w_in.shape[2]
    depth, columns = w_router.shape
    rows = window * CAP
    message = -(-CAP * (2 * width // LANES + 1) // 16) * 16
    hbm = pl.BlockSpec(memory_space=pltpu.HBM)
    dma = pltpu.SemaphoreType.DMA
    routing = (expert_ids.T, slot_ids.T, keep_mask.T)
    g1, g2, returned, router_part = pl.pallas_call(
        functools.partial(fused_kernel, window, groups),
        out_shape=(
            jax.ShapeDtypeStruct((width, hidden), BF16),
            jax.ShapeDtypeStruct((hidden, width), BF16),
            jax.ShapeDtypeStruct((window, 16, LANES), BF16),
            jax.ShapeDtypeStruct((columns, depth), F32),
        ),
        in_specs=[hbm] * 8,
        out_specs=(hbm, hbm, hbm, hbm),
        scratch_shapes=[
            pltpu.VMEM(expert_ids.shape[::-1], jnp.int32),
            pltpu.VMEM(slot_ids.shape[::-1], jnp.int32),
            pltpu.VMEM(keep_mask.shape[::-1], jnp.int32),
            pltpu.VMEM((count, width), BF16),
            pltpu.VMEM((count, width), BF16),
            pltpu.VMEM((width, hidden), BF16),
            pltpu.VMEM((hidden, width), BF16),
            pltpu.VMEM((width, hidden), BF16),
            pltpu.VMEM((hidden, width), BF16),
            pltpu.VMEM((columns, depth), F32),
            pltpu.VMEM((window, message, LANES), BF16),
            pltpu.VMEM((window, message, LANES), BF16),
            pltpu.VMEM((window, columns, depth), BF16),
            pltpu.VMEM((plane, 16, width // 2 + LANES), BF16),
            pltpu.VMEM((plane, 16, width // 2), BF16),
            pltpu.VMEM((plane * rows, width), BF16),
            pltpu.VMEM((plane, rows, depth + LANES), F32),
            pltpu.VMEM((plane, rows, depth + LANES), F32),
            pltpu.VMEM((plane, rows, LANES), F32),
            pltpu.VMEM((2, plane, 16, width // 4), BF16),
            pltpu.VMEM((2, plane, 16, width // 4), BF16),
            pltpu.VMEM((plane * rows, LANES), F32),
            pltpu.VMEM((window, columns, depth), BF16),
            pltpu.VMEM((window, columns, depth), BF16),
            pltpu.VMEM((window, 16, LANES), BF16),
            pltpu.VMEM((window, 16, LANES), BF16),
            dma((8,)),
            dma((10,)),
        ]
        + [dma((2,))] * 6
        + [dma((2, 2))]
        + [dma((2,))] * 2,
        compiler_params=pltpu.CompilerParams(
            collective_id=0, has_side_effects=True, vmem_limit_bytes=60 * 1024 * 1024
        ),
    )(
        tokens,
        out_grad,
        w_router.T,
        w_in,
        w_out,
        *routing,
    )
    in_grad, w_in_grad, w_out_grad, router_grad = pl.pallas_call(
        functools.partial(finish_kernel, window),
        out_shape=(
            jax.ShapeDtypeStruct((count, width), BF16),
            jax.ShapeDtypeStruct(w_in.shape, BF16),
            jax.ShapeDtypeStruct(w_out.shape, BF16),
            jax.ShapeDtypeStruct((columns, depth), F32),
        ),
        in_specs=[hbm] * 7,
        out_specs=(hbm, hbm, hbm, hbm),
        scratch_shapes=[
            pltpu.VMEM((width, hidden), BF16),
            pltpu.VMEM((hidden, width), BF16),
            pltpu.VMEM((columns, depth), F32),
            pltpu.VMEM((count, width), BF16),
            pltpu.VMEM((window, 16, LANES), BF16),
            pltpu.VMEM(expert_ids.shape[::-1], jnp.int32),
            pltpu.VMEM(slot_ids.shape[::-1], jnp.int32),
            pltpu.VMEM(keep_mask.shape[::-1], jnp.int32),
            dma((10,)),
            dma((13,)),
        ],
        compiler_params=pltpu.CompilerParams(vmem_limit_bytes=60 * 1024 * 1024),
    )(g1, g2, returned, router_part, *routing)
    return (in_grad, w_in_grad, w_out_grad, router_grad.T)


def body(*args):
    tokens, _, w_router = args[:3]
    window = lax.axis_size("expert") // SPLIT
    fits = (
        window * CAP == 8
        and w_router.shape[1] % 16 == 0
        and w_router.shape[0] % LANES == 0
        and window * w_router.shape[1] == LANES
        and SPLIT * lax.axis_size("group") * window * CAP <= LANES
        and tokens.shape == (LANES, 8 * LANES)
    )
    return fused(*args) if fits else gathered_body(*args)


def solution(mesh):
    return jax.shard_map(
        body,
        mesh=mesh,
        in_specs=(
            P(("expert", "group"), None),
            P(("expert", "group"), None),
            P("group", "expert"),
            P("expert", None, "group"),
            P("expert", "group", None),
            P(("expert", "group"), None),
            P(("expert", "group"), None),
            P(("expert", "group"), None),
        ),
        out_specs=(
            P(("expert", "group"), None),
            P("expert", None, "group"),
            P("expert", "group", None),
            P("group", "expert"),
        ),
        check_vma=False,
    )
```

```python
import functools

import jax
import jax.numpy as jnp
from jax import lax
from jax.experimental import pallas as pl
from jax.experimental.pallas import tpu as pltpu
from jax.sharding import PartitionSpec as P

CAP = 2
SPLIT = 2
LANES = 128
F32 = jnp.float32
BF16 = jnp.bfloat16
MESH = pl.DeviceIdType.MESH


def gelu_parts(pre_act):
    cubic_term = 0.044715 * pre_act * pre_act * pre_act
    tanh_value = jnp.tanh(0.7978845608028654 * (pre_act + cubic_term))
    gelu_value = 0.5 * pre_act * (1.0 + tanh_value)
    gelu_slope = 0.5 * (1.0 + tanh_value) + 0.5 * pre_act * (
        1.0 - tanh_value * tanh_value
    ) * 0.7978845608028654 * (1.0 + 3.0 * 0.044715 * pre_act * pre_act)
    return (gelu_value, gelu_slope)


def expert_rows(w_in_local, w_out_local, pieces):
    x_piece, dy_piece, gate_piece = pieces
    gate_col = gate_piece.astype(jnp.float32)[:, None]
    pre_act = jnp.dot(x_piece, w_in_local, preferred_element_type=jnp.float32)
    gelu_value, gelu_slope = gelu_parts(pre_act)
    back_up = jnp.einsum("rd,hd->rh", dy_piece, w_out_local, preferred_element_type=jnp.float32)
    gate_piece_sum = jnp.sum(back_up * gelu_value, axis=1)
    pre_grad = (gate_col * back_up * gelu_slope).astype(jnp.bfloat16)
    scaled_grad = (gate_col * dy_piece.astype(jnp.float32)).astype(jnp.bfloat16)
    sum_in = jnp.einsum("rd,rh->dh", x_piece, pre_grad, preferred_element_type=jnp.float32)
    sum_out = jnp.einsum(
        "rh,rd->hd",
        gelu_value.astype(jnp.bfloat16),
        scaled_grad,
        preferred_element_type=jnp.float32,
    )
    part_rows = jnp.einsum("rh,dh->rd", pre_grad, w_in_local, preferred_element_type=jnp.float32)
    return (sum_in, sum_out, part_rows, gate_piece_sum)


def gathered_body(tokens, out_grad, w_router, w_in, w_out, expert_ids, slot_ids, keep_mask):
    expert_count = lax.axis_size("expert")
    window = expert_count // SPLIT
    slot_count = window * CAP
    model_width = tokens.shape[1]
    router_full = lax.all_gather(
        lax.all_gather(w_router, "expert", axis=1, tiled=True), "group", axis=0, tiled=True
    )
    logits = jnp.dot(tokens, router_full, preferred_element_type=jnp.float32)
    uniform_samples = jnp.arange(router_full.shape[1], dtype=jnp.int32)
    first_hot = (expert_ids[:, 0:1] == uniform_samples[None, :]).astype(jnp.float32)
    second_hot = (expert_ids[:, 1:2] == uniform_samples[None, :]).astype(jnp.float32)
    logit_gap = jnp.sum(logits * first_hot, axis=1) - jnp.sum(logits * second_hot, axis=1)
    combine = jnp.stack([jax.nn.sigmoid(logit_gap), jax.nn.sigmoid(-logit_gap)], axis=1)
    active = (keep_mask == 1) & (expert_ids < window)
    slot_code = jnp.where(active, expert_ids * CAP + slot_ids, -1)
    slot_axis = jnp.arange(slot_count, dtype=jnp.int32)
    place_first = (slot_code[:, 0:1] == slot_axis[None, :]).astype(jnp.float32)
    place_second = (slot_code[:, 1:2] == slot_axis[None, :]).astype(jnp.float32)
    placement = place_first + place_second
    place_round = placement.astype(jnp.bfloat16)
    token_slots = jnp.einsum(
        "ts,td->sd", place_round, tokens, preferred_element_type=jnp.float32
    ).astype(jnp.bfloat16)
    grad_slots = jnp.einsum(
        "ts,td->sd", place_round, out_grad, preferred_element_type=jnp.float32
    ).astype(jnp.bfloat16)
    gate_slots = jnp.sum(
        place_first * combine[:, 0:1] + place_second * combine[:, 1:2], axis=0
    ).astype(jnp.bfloat16)
    token_send = jnp.repeat(token_slots.reshape(window, CAP, model_width), SPLIT, axis=0)
    grad_send = jnp.repeat(grad_slots.reshape(window, CAP, model_width), SPLIT, axis=0)
    gate_send = jnp.repeat(gate_slots.reshape(window, CAP), SPLIT, axis=0)
    token_recv, grad_recv, gate_recv = (
        lax.all_to_all(token_send, "expert", split_axis=0, concat_axis=0, tiled=True),
        lax.all_to_all(grad_send, "expert", split_axis=0, concat_axis=0, tiled=True),
        lax.all_to_all(gate_send, "expert", split_axis=0, concat_axis=0, tiled=True),
    )
    row_count = expert_count * CAP
    token_rows = token_recv.reshape(row_count, model_width)
    grad_rows = grad_recv.reshape(row_count, model_width)
    gate_rows = gate_recv.reshape(row_count)
    w_in_local = w_in[0]
    w_out_local = w_out[0]
    sum_in, sum_out, row_parts, gate_parts = expert_rows(
        w_in_local,
        w_out_local,
        (
            lax.all_gather(token_rows, "group", axis=0, tiled=True),
            lax.all_gather(grad_rows, "group", axis=0, tiled=True),
            lax.all_gather(gate_rows, "group", axis=0, tiled=True),
        ),
    )
    w_in_grad = sum_in.astype(jnp.bfloat16)[None]
    w_out_grad = sum_out.astype(jnp.bfloat16)[None]
    row_sums = lax.psum_scatter(
        row_parts.astype(jnp.bfloat16), "group", scatter_dimension=0, tiled=True
    ).astype(jnp.float32)
    gate_sums = lax.psum_scatter(gate_parts, "group", scatter_dimension=0, tiled=True)
    rows_back, gates_back = (
        lax.all_to_all(
            row_sums.reshape(expert_count, CAP, model_width).astype(jnp.bfloat16),
            "expert",
            split_axis=0,
            concat_axis=0,
            tiled=True,
        ).astype(jnp.float32),
        lax.all_to_all(
            gate_sums.reshape(expert_count, CAP).astype(jnp.bfloat16),
            "expert",
            split_axis=0,
            concat_axis=0,
            tiled=True,
        ).astype(jnp.float32),
    )
    rows_back = jnp.sum(rows_back.reshape(window, SPLIT, CAP, model_width), axis=1).reshape(
        slot_count, model_width
    )
    gates_back = jnp.sum(gates_back.reshape(window, SPLIT, CAP), axis=1).reshape(slot_count)
    expert_part = jnp.dot(placement, rows_back, precision=lax.Precision.HIGHEST)
    gate_first = jnp.sum(place_first * gates_back[None, :], axis=1)
    gate_second = jnp.sum(place_second * gates_back[None, :], axis=1)
    gate_slope = combine[:, 0] * combine[:, 1] * (gate_first - gate_second)
    logit_grad = first_hot * gate_slope[:, None] - second_hot * gate_slope[:, None]
    router_part = jnp.dot(
        logit_grad, router_full.astype(jnp.float32).T, precision=lax.Precision.HIGHEST
    )
    in_grad = (expert_part + router_part).astype(jnp.bfloat16)
    router_sum = jnp.dot(tokens.astype(jnp.float32).T, logit_grad, precision=lax.Precision.HIGHEST)
    router_grad = lax.psum_scatter(
        lax.psum_scatter(router_sum, "expert", scatter_dimension=1, tiled=True),
        "group",
        scatter_dimension=0,
        tiled=True,
    )
    return (in_grad, w_in_grad, w_out_grad, router_grad)


def iota(shape, axis):
    return lax.broadcasted_iota(jnp.int32, shape, axis)


def one_hot(mask):
    return jnp.where(mask, 1.0, 0.0).astype(F32)


def contract(left, right, left_axis, right_axis):
    return lax.dot_general(
        left, right, (((left_axis,), (right_axis,)), ((), ())), preferred_element_type=F32
    )


def choice_places(count, z, window, ids_ref, slots_ref, keep_ref):
    places = []
    for k in range(2):
        ids = ids_ref[k : k + 1, :]
        relative = jnp.where(ids < z, ids - z + window, ids - z)
        active = (keep_ref[k : k + 1, :] == 1) & (ids < window)
        code = jnp.where(active, relative * CAP + slots_ref[k : k + 1, :], -1)
        places.append(one_hot(iota((count, LANES), 0) == code))
    return places


def finish_kernel(
    window,
    g1_hbm,
    g2_hbm,
    returned_hbm,
    router_hbm,
    ids_hbm,
    slots_hbm,
    keep_hbm,
    in_grad_hbm,
    w_in_grad_hbm,
    w_out_grad_hbm,
    router_grad_hbm,
    g1,
    g2,
    router_grad,
    in_grad,
    returned_ref,
    ids_ref,
    slots_ref,
    keep_ref,
    sems,
    load_sems,
):
    parts = 4
    loads, stores = [], []
    for src, staged, dst, pieces in (
        (ids_hbm, ids_ref, None, 1),
        (slots_hbm, slots_ref, None, 1),
        (keep_hbm, keep_ref, None, 1),
        (returned_hbm, returned_ref, None, 1),
        (router_hbm, router_grad, router_grad_hbm, 1),
        (g1_hbm, g1, w_in_grad_hbm.at[0], parts),
        (g2_hbm, g2, w_out_grad_hbm.at[0], parts),
    ):
        step = src.shape[0] // pieces
        for p in range(pieces):
            span = pl.ds(p * step, step)
            whole = pieces == 1
            loads.append(
                pltpu.make_async_copy(
                    src if whole else src.at[span],
                    staged if whole else staged.at[span],
                    load_sems.at[len(loads)],
                )
            )
            if dst is not None:
                stores.append(
                    pltpu.make_async_copy(
                        staged if whole else staged.at[span],
                        dst if whole else dst.at[span],
                        sems.at[len(stores)],
                    )
                )
    for load in loads:
        load.start()
    rows = window * CAP
    chunks = in_grad.shape[1] // LANES
    back = chunks * rows
    row = iota((back, back), 0)
    source = ((row >> 1) & (window - 1)) * 16 + (row >> 3) * CAP + (row & 1)
    unfold = one_hot(iota((back, back), 1) == source).astype(BF16)
    z = lax.axis_index("expert") // SPLIT
    for load in loads[:3]:
        load.wait()
    places = choice_places(LANES, z, window, ids_ref, slots_ref, keep_ref)
    spread_back = jnp.transpose(places[0] + places[1]).astype(BF16)
    loads[3].wait()
    flat = contract(unfold, returned_ref[...].reshape(back, LANES), 1, 0)
    returned = jnp.concatenate(
        [flat[c * rows : (c + 1) * rows] for c in range(chunks)], axis=1
    )
    returned = jnp.concatenate(
        [returned, jnp.zeros((LANES - rows, chunks * LANES), F32)], axis=0
    ).astype(BF16)
    for load, store in zip(loads[4:], stores):
        load.wait()
        store.start()
    in_grad[...] = contract(spread_back, returned, 1, 0).astype(BF16)
    stores.append(pltpu.make_async_copy(in_grad, in_grad_hbm, sems.at[len(stores)]))
    stores[-1].start()
    for store in stores:
        store.wait()


def fused_kernel(
    window,
    groups,
    tokens_hbm,
    out_grad_hbm,
    router_hbm,
    w_in_hbm,
    w_out_hbm,
    ids_hbm,
    slots_hbm,
    keep_hbm,
    g1_out,
    g2_out,
    returned_out,
    router_grad_out,
    ids_ref,
    slots_ref,
    keep_ref,
    tok,
    outg,
    w1,
    w2,
    g1,
    g2,
    router_grad_ref,
    z_send,
    z_recv,
    w_recv,
    x_pack,
    dy_pack,
    xs,
    gaps,
    diff_send,
    diff_recv,
    gg,
    rp_send,
    rp_recv,
    coef_ref,
    rg_send,
    rg_recv,
    ret_send,
    ret_recv,
    load_sems,
    store_sems,
    zs,
    ws,
    xps,
    dps,
    gps,
    dfs,
    ggs,
    rps,
    rgs,
    rts,
):
    plane = SPLIT * groups
    width = tok.shape[1]
    chunks = width // LANES
    rows = window * CAP
    message = z_send.shape[1]
    used = CAP * (2 * chunks + 1)
    columns, depth = router_hbm.shape
    ix = lax.axis_index("expert")
    g = lax.axis_index("group")
    z = ix // SPLIT
    y = lax.rem(ix, SPLIT)
    q = y * groups + g

    def z_up(d):
        return (lax.rem(z + d, window) * SPLIT + y, g)

    def z_down(d):
        return (lax.rem(z + window - d, window) * SPLIT + y, g)

    def in_plane(p):
        return (z * SPLIT + p // groups, lax.rem(p, groups))

    def q_up(d):
        return lax.rem(q + d, plane)

    def q_down(d):
        return lax.rem(q + plane - d, plane)

    def remote(src, dst, sems, target):
        return pltpu.make_async_remote_copy(
            src_ref=src,
            dst_ref=dst,
            send_sem=sems.at[0],
            recv_sem=sems.at[1],
            device_id=target,
            device_id_type=MESH,
        )

    def along_z(src, dst, sems, target_of):
        for d in range(1, window):
            remote(src(d), dst.at[d], sems, target_of(d)).start()
        every = dst.at[pl.ds(1, window - 1)]
        return remote(every, every, sems, target_of(1))

    def all_plane(src, dst, sems):
        for d in range(1, plane):
            target = q_up(d)
            remote(src(target), dst.at[q], sems, in_plane(target)).start()
        every = dst.at[pl.ds(0, plane - 1)]
        return remote(every, every, sems, in_plane(q_up(1)))

    loads = [
        pltpu.make_async_copy(src, dst, load_sems.at[i])
        for i, (src, dst) in enumerate(
            [
                (ids_hbm, ids_ref),
                (slots_hbm, slots_ref),
                (keep_hbm, keep_ref),
                (tokens_hbm, tok),
                (out_grad_hbm, outg),
                (router_hbm, w_recv.at[0]),
                (w_in_hbm.at[0], w1),
                (w_out_hbm.at[0], w2),
            ]
        )
    ]
    for load in loads[:5]:
        load.start()
    barrier = pltpu.get_barrier_semaphore()
    for d in range(1, window):
        pl.semaphore_signal(barrier, inc=1, device_id=z_up(d), device_id_type=MESH)
    for d in range(1, plane):
        pl.semaphore_signal(barrier, inc=1, device_id=in_plane(q_up(d)), device_id_type=MESH)

    for load in loads[5:]:
        load.start()

    depth_f = (2 * chunks + 2) * rows
    spread = []
    for d in range(window):
        row = iota((message, depth_f), 0)
        source = (row >> 1) * rows + d * CAP + (row & 1)
        spread.append(one_hot((iota((message, depth_f), 1) == source) & (row < used)))
    spread = jnp.concatenate(spread, axis=0).astype(BF16)
    half = width // 2
    side = chunks // 2
    wide = (chunks + 1) * 16
    row = iota((wide, window * message), 0)
    inner = row & 15
    column = row >> 4
    upper = jnp.where(inner < rows, 0, side)
    block = jnp.where(
        column < side,
        column + upper,
        jnp.where(column == side, 2 * chunks, chunks + column - side - 1 + upper),
    )
    source = ((inner & (rows - 1)) >> 1) * message + block * CAP + (inner & 1)
    gather = one_hot(iota((wide, window * message), 1) == source).astype(BF16)

    for load in loads[:3]:
        load.wait()
    places = choice_places(16, z, window, ids_ref, slots_ref, keep_ref)
    place = places[0] + places[1]
    place_rows = place.astype(BF16)
    short = place[:rows]
    first_id = jnp.sum(short * ids_ref[0:1, :].astype(F32), axis=1, keepdims=True)
    second_id = jnp.sum(short * ids_ref[1:2, :].astype(F32), axis=1, keepdims=True)
    which = jnp.sum(places[0][:rows] - places[1][:rows], axis=1, keepdims=True)
    lane = iota((rows, LANES), 1)
    meta = jnp.where(
        lane == 0, first_id, jnp.where(lane == 1, second_id, jnp.where(lane == 2, which, 0.0))
    )

    loads[3].wait()
    loads[4].wait()
    x_slots = contract(place_rows, tok[...], 1, 0)[:rows]
    dy_slots = contract(place_rows, outg[...], 1, 0)[:rows]
    pieces = [x_slots[:, c * LANES : (c + 1) * LANES] for c in range(chunks)]
    pieces += [dy_slots[:, c * LANES : (c + 1) * LANES] for c in range(chunks)]
    pieces += [meta, jnp.zeros((rows, LANES), F32)]
    folded = jnp.concatenate(pieces, axis=0).astype(BF16)
    messages = contract(spread, folded, 1, 0).astype(BF16)
    z_recv[0] = messages[:message]
    for d in range(1, window):
        z_send[d] = messages[d * message : (d + 1) * message]
    pl.semaphore_wait(barrier, window - 1 + plane - 1)

    z_all = along_z(lambda d: z_send.at[d], z_recv, zs, z_up)
    total = plane * rows
    eye = iota((total, LANES), 0) == iota((total, LANES), 1)
    column = iota((1, window * columns), 1)
    owner = lax.rem(z + window - column // columns, window)
    column_id = ((owner * SPLIT + y) * columns + lax.rem(column, columns)).astype(F32)
    loads[5].wait()
    w_all = along_z(lambda d: w_recv.at[0], w_recv, ws, z_up)
    z_all.wait_recv()
    arrived = z_recv[...].reshape(window * message, LANES)
    x_blocks = (side + 1) * 16
    gathered = contract(gather[:x_blocks], arrived, 1, 0).astype(BF16)
    for c in range(side + 1):
        x_pack[q, :, c * LANES : (c + 1) * LANES] = gathered[c * 16 : (c + 1) * 16]
    xp_all = all_plane(lambda p: x_pack.at[q], x_pack, xps)
    gathered = contract(gather[x_blocks:], arrived, 1, 0).astype(BF16)
    for c in range(side):
        dy_pack[q, :, c * LANES : (c + 1) * LANES] = gathered[c * 16 : (c + 1) * 16]
    dp_all = all_plane(lambda p: dy_pack.at[q], dy_pack, dps)

    def unfolded(block):
        return jnp.concatenate(
            [block[:, :rows, :half], block[:, rows:, :half]], axis=2
        ).reshape(plane * rows, width)

    z_all.wait_send()
    w_all.wait()
    router = w_recv[...].reshape(window * columns, depth)
    xp_all.wait_recv()

    packed = x_pack[...].astype(F32)
    x_rows = unfolded(packed).astype(BF16)
    info = packed[:, :rows, half:].reshape(total, LANES)
    xs[...] = x_rows
    x_part = xs[:, pl.ds(pl.multiple_of(g * depth, LANES), depth)]

    hot = one_hot(info[:, 0:1] == column_id) - one_hot(info[:, 1:2] == column_id)
    sign = info[:, 2:3]
    gap_part = jnp.sum(contract(x_part, router, 1, 1) * hot, axis=1, keepdims=True)
    gap_row = jnp.sum(jnp.where(eye, gap_part, 0.0), axis=0, keepdims=True)
    gaps[q] = jnp.broadcast_to(gap_row, (rows, LANES))
    gap_all = all_plane(lambda p: gaps.at[q], gaps, gps)
    row_diff = contract(hot.astype(BF16), router, 1, 0)
    diff_send[...] = row_diff.reshape(plane, rows, depth)
    diff_recv[q] = diff_send[q]
    diff_all = all_plane(lambda p: diff_send.at[p], diff_recv, dfs)

    loads[6].wait()
    pre_act = contract(x_rows, w1[...], 1, 0)
    loads[7].wait()
    dp_all.wait_recv()
    dy_rows = unfolded(dy_pack[...].astype(F32)).astype(BF16)
    back_up = contract(dy_rows, w2[...], 1, 1)
    gelu_value, gelu_slope = gelu_parts(pre_act)
    gate_part = jnp.sum(back_up * gelu_value, axis=1, keepdims=True)
    gate_row = jnp.sum(jnp.where(eye, gate_part, 0.0), axis=0, keepdims=True)
    gg[q] = jnp.broadcast_to(gate_row, (rows, LANES))
    gg_all = all_plane(lambda p: gg.at[q], gg, ggs)

    gap_all.wait_recv()
    gap_sum = jnp.sum(gaps[:, 0:1, :], axis=0)
    gap = jnp.sum(jnp.where(eye, gap_sum, 0.0), axis=1, keepdims=True)
    combine_first = jax.nn.sigmoid(gap)
    combine_second = jax.nn.sigmoid(-gap)
    gate = jnp.where(sign > 0.5, combine_first, jnp.where(sign < -0.5, combine_second, 0.0))
    gate = gate.astype(BF16).astype(F32)
    pre_grad = (gate * back_up * gelu_slope).astype(BF16)
    rp_all = []
    for h in range(2):
        part = contract(pre_grad, w1[h * half : (h + 1) * half, :], 1, 1)
        part = part.reshape(plane, rows, half)
        rp_send[h] = jnp.concatenate(
            [part[:, :, : half // 2], part[:, :, half // 2 :]], axis=1
        ).astype(BF16)
        rp_recv[h, q] = rp_send[h, q]
        rp_all.append(all_plane(lambda p, h=h: rp_send.at[h, p], rp_recv.at[h], rps.at[h]))

    gg_all.wait_recv()
    grad_sum = jnp.sum(gg[:, 0:1, :], axis=0)
    gate_grad = jnp.sum(jnp.where(eye, grad_sum, 0.0), axis=1, keepdims=True)
    coef = sign * combine_first * combine_second * gate_grad
    coef_ref[...] = jnp.broadcast_to(coef, (total, LANES))
    logit_grad = coef * hot
    high = logit_grad.astype(BF16)
    low = (logit_grad - high.astype(F32)).astype(BF16)
    router_part = contract(
        jnp.concatenate([high, low], axis=0), jnp.concatenate([x_part, x_part], axis=0), 0, 0
    )
    for d in range(1, window):
        rg_send[d] = router_part[d * columns : (d + 1) * columns].astype(BF16)
    rg_all = along_z(lambda d: rg_send.at[d], rg_recv, rgs, z_down)

    diff_all.wait_recv()
    diffs = []
    for part in range(groups):
        diff = diff_recv[part]
        for other in range(1, SPLIT):
            diff = diff + diff_recv[other * groups + part]
        diffs.append(diff)
    own_coef = coef_ref[pl.ds(pl.multiple_of(q * rows, rows), rows), 0:1]
    router_rows = own_coef * jnp.concatenate(diffs, axis=1)
    back = chunks * rows
    row = iota((back, back), 0)
    source = ((row >> 1) & (chunks - 1)) * rows + (row >> 4) * CAP + (row & 1)
    fold = one_hot(iota((back, back), 1) == source).astype(BF16)

    stores = []

    def weight_grad(left, right, staged, target):
        parts = 4
        step = staged.shape[0] // parts
        for p in range(parts):
            span = slice(p * step, (p + 1) * step)
            staged[span] = contract(left[:, span], right, 0, 0).astype(BF16)
            stores.append(
                pltpu.make_async_copy(
                    staged.at[span], target.at[span], store_sems.at[len(stores)]
                )
            )
            stores[-1].start()

    weight_grad(x_rows, pre_grad, g1, g1_out)
    for sent in (xp_all, dp_all, gap_all, diff_all, gg_all):
        sent.wait_send()
    halves = []
    for h in range(2):
        rp_all[h].wait_recv()
        summed = jnp.sum(rp_recv[h].astype(F32), axis=0)
        halves += [summed[:rows], summed[rows:]]
    row_grad = jnp.concatenate(halves, axis=1)
    row_grad = row_grad + router_rows
    folded = jnp.concatenate(
        [row_grad[:, c * LANES : (c + 1) * LANES] for c in range(chunks)], axis=0
    ).astype(BF16)
    ret_send[...] = contract(fold, folded, 1, 0).astype(BF16).reshape(ret_send.shape)
    ret_recv[0] = ret_send[0]
    ret_all = along_z(lambda d: ret_send.at[d], ret_recv, rts, z_down)

    rg_all.wait_recv()
    router_grad_ref[...] = router_part[:columns] + jnp.sum(
        rg_recv[1:].astype(F32), axis=0
    )
    stores.append(
        pltpu.make_async_copy(router_grad_ref, router_grad_out, store_sems.at[len(stores)])
    )
    stores[-1].start()
    scaled_grad = (gate * dy_rows.astype(F32)).astype(BF16)
    weight_grad(gelu_value.astype(BF16), scaled_grad, g2, g2_out)
    for sent in (*rp_all, rg_all):
        sent.wait_send()
    ret_all.wait_recv()
    stores.append(
        pltpu.make_async_copy(ret_recv, returned_out, store_sems.at[len(stores)])
    )
    stores[-1].start()
    ret_all.wait_send()
    for store in stores:
        store.wait()


def fused(tokens, out_grad, w_router, w_in, w_out, expert_ids, slot_ids, keep_mask):
    window = lax.axis_size("expert") // SPLIT
    groups = lax.axis_size("group")
    plane = SPLIT * groups
    count, width = tokens.shape
    hidden = w_in.shape[2]
    depth, columns = w_router.shape
    rows = window * CAP
    message = -(-CAP * (2 * width // LANES + 1) // 16) * 16
    hbm = pl.BlockSpec(memory_space=pltpu.HBM)
    dma = pltpu.SemaphoreType.DMA
    routing = (expert_ids.T, slot_ids.T, keep_mask.T)
    g1, g2, returned, router_part = pl.pallas_call(
        functools.partial(fused_kernel, window, groups),
        out_shape=(
            jax.ShapeDtypeStruct((width, hidden), BF16),
            jax.ShapeDtypeStruct((hidden, width), BF16),
            jax.ShapeDtypeStruct((window, 16, LANES), BF16),
            jax.ShapeDtypeStruct((columns, depth), F32),
        ),
        in_specs=[hbm] * 8,
        out_specs=(hbm, hbm, hbm, hbm),
        scratch_shapes=[
            pltpu.VMEM(expert_ids.shape[::-1], jnp.int32),
            pltpu.VMEM(slot_ids.shape[::-1], jnp.int32),
            pltpu.VMEM(keep_mask.shape[::-1], jnp.int32),
            pltpu.VMEM((count, width), BF16),
            pltpu.VMEM((count, width), BF16),
            pltpu.VMEM((width, hidden), BF16),
            pltpu.VMEM((hidden, width), BF16),
            pltpu.VMEM((width, hidden), BF16),
            pltpu.VMEM((hidden, width), BF16),
            pltpu.VMEM((columns, depth), F32),
            pltpu.VMEM((window, message, LANES), BF16),
            pltpu.VMEM((window, message, LANES), BF16),
            pltpu.VMEM((window, columns, depth), BF16),
            pltpu.VMEM((plane, 16, width // 2 + LANES), BF16),
            pltpu.VMEM((plane, 16, width // 2), BF16),
            pltpu.VMEM((plane * rows, width), BF16),
            pltpu.VMEM((plane, rows, LANES), F32),
            pltpu.VMEM((plane, rows, depth), F32),
            pltpu.VMEM((plane, rows, depth), F32),
            pltpu.VMEM((plane, rows, LANES), F32),
            pltpu.VMEM((2, plane, 16, width // 4), BF16),
            pltpu.VMEM((2, plane, 16, width // 4), BF16),
            pltpu.VMEM((plane * rows, LANES), F32),
            pltpu.VMEM((window, columns, depth), BF16),
            pltpu.VMEM((window, columns, depth), BF16),
            pltpu.VMEM((window, 16, LANES), BF16),
            pltpu.VMEM((window, 16, LANES), BF16),
            dma((8,)),
            dma((10,)),
        ]
        + [dma((2,))] * 7
        + [dma((2, 2))]
        + [dma((2,))] * 2,
        compiler_params=pltpu.CompilerParams(
            collective_id=0, has_side_effects=True, vmem_limit_bytes=60 * 1024 * 1024
        ),
    )(
        tokens,
        out_grad,
        w_router.T,
        w_in,
        w_out,
        *routing,
    )
    in_grad, w_in_grad, w_out_grad, router_grad = pl.pallas_call(
        functools.partial(finish_kernel, window),
        out_shape=(
            jax.ShapeDtypeStruct((count, width), BF16),
            jax.ShapeDtypeStruct(w_in.shape, BF16),
            jax.ShapeDtypeStruct(w_out.shape, BF16),
            jax.ShapeDtypeStruct((columns, depth), F32),
        ),
        in_specs=[hbm] * 7,
        out_specs=(hbm, hbm, hbm, hbm),
        scratch_shapes=[
            pltpu.VMEM((width, hidden), BF16),
            pltpu.VMEM((hidden, width), BF16),
            pltpu.VMEM((columns, depth), F32),
            pltpu.VMEM((count, width), BF16),
            pltpu.VMEM((window, 16, LANES), BF16),
            pltpu.VMEM(expert_ids.shape[::-1], jnp.int32),
            pltpu.VMEM(slot_ids.shape[::-1], jnp.int32),
            pltpu.VMEM(keep_mask.shape[::-1], jnp.int32),
            dma((10,)),
            dma((13,)),
        ],
        compiler_params=pltpu.CompilerParams(vmem_limit_bytes=60 * 1024 * 1024),
    )(g1, g2, returned, router_part, *routing)
    return (in_grad, w_in_grad, w_out_grad, router_grad.T)


def body(*args):
    tokens, _, w_router = args[:3]
    window = lax.axis_size("expert") // SPLIT
    fits = (
        window * CAP == 8
        and w_router.shape[1] % 16 == 0
        and w_router.shape[0] % LANES == 0
        and window * w_router.shape[1] == LANES
        and SPLIT * lax.axis_size("group") * window * CAP <= LANES
        and tokens.shape == (LANES, 8 * LANES)
    )
    return fused(*args) if fits else gathered_body(*args)


def solution(mesh):
    return jax.shard_map(
        body,
        mesh=mesh,
        in_specs=(
            P(("expert", "group"), None),
            P(("expert", "group"), None),
            P("group", "expert"),
            P("expert", None, "group"),
            P("expert", "group", None),
            P(("expert", "group"), None),
            P(("expert", "group"), None),
            P(("expert", "group"), None),
        ),
        out_specs=(
            P(("expert", "group"), None),
            P("expert", None, "group"),
            P("expert", "group", None),
            P("group", "expert"),
        ),
        check_vma=False,
    )
```

```python
import functools

import jax
import jax.numpy as jnp
from jax import lax
from jax.experimental import pallas as pl
from jax.experimental.pallas import tpu as pltpu
from jax.sharding import PartitionSpec as P

CAP = 2
SPLIT = 2
LANES = 128
F32 = jnp.float32
BF16 = jnp.bfloat16
MESH = pl.DeviceIdType.MESH


def gelu_parts(pre_act):
    cubic_term = 0.044715 * pre_act * pre_act * pre_act
    tanh_value = jnp.tanh(0.7978845608028654 * (pre_act + cubic_term))
    gelu_value = 0.5 * pre_act * (1.0 + tanh_value)
    gelu_slope = 0.5 * (1.0 + tanh_value) + 0.5 * pre_act * (
        1.0 - tanh_value * tanh_value
    ) * 0.7978845608028654 * (1.0 + 3.0 * 0.044715 * pre_act * pre_act)
    return (gelu_value, gelu_slope)


def expert_rows(w_in_local, w_out_local, pieces):
    x_piece, dy_piece, gate_piece = pieces
    gate_col = gate_piece.astype(jnp.float32)[:, None]
    pre_act = jnp.dot(x_piece, w_in_local, preferred_element_type=jnp.float32)
    gelu_value, gelu_slope = gelu_parts(pre_act)
    back_up = jnp.einsum("rd,hd->rh", dy_piece, w_out_local, preferred_element_type=jnp.float32)
    gate_piece_sum = jnp.sum(back_up * gelu_value, axis=1)
    pre_grad = (gate_col * back_up * gelu_slope).astype(jnp.bfloat16)
    scaled_grad = (gate_col * dy_piece.astype(jnp.float32)).astype(jnp.bfloat16)
    sum_in = jnp.einsum("rd,rh->dh", x_piece, pre_grad, preferred_element_type=jnp.float32)
    sum_out = jnp.einsum(
        "rh,rd->hd",
        gelu_value.astype(jnp.bfloat16),
        scaled_grad,
        preferred_element_type=jnp.float32,
    )
    part_rows = jnp.einsum("rh,dh->rd", pre_grad, w_in_local, preferred_element_type=jnp.float32)
    return (sum_in, sum_out, part_rows, gate_piece_sum)


def gathered_body(tokens, out_grad, w_router, w_in, w_out, expert_ids, slot_ids, keep_mask):
    expert_count = lax.axis_size("expert")
    window = expert_count // SPLIT
    slot_count = window * CAP
    model_width = tokens.shape[1]
    router_full = lax.all_gather(
        lax.all_gather(w_router, "expert", axis=1, tiled=True), "group", axis=0, tiled=True
    )
    logits = jnp.dot(tokens, router_full, preferred_element_type=jnp.float32)
    uniform_samples = jnp.arange(router_full.shape[1], dtype=jnp.int32)
    first_hot = (expert_ids[:, 0:1] == uniform_samples[None, :]).astype(jnp.float32)
    second_hot = (expert_ids[:, 1:2] == uniform_samples[None, :]).astype(jnp.float32)
    logit_gap = jnp.sum(logits * first_hot, axis=1) - jnp.sum(logits * second_hot, axis=1)
    combine = jnp.stack([jax.nn.sigmoid(logit_gap), jax.nn.sigmoid(-logit_gap)], axis=1)
    active = (keep_mask == 1) & (expert_ids < window)
    slot_code = jnp.where(active, expert_ids * CAP + slot_ids, -1)
    slot_axis = jnp.arange(slot_count, dtype=jnp.int32)
    place_first = (slot_code[:, 0:1] == slot_axis[None, :]).astype(jnp.float32)
    place_second = (slot_code[:, 1:2] == slot_axis[None, :]).astype(jnp.float32)
    placement = place_first + place_second
    place_round = placement.astype(jnp.bfloat16)
    token_slots = jnp.einsum(
        "ts,td->sd", place_round, tokens, preferred_element_type=jnp.float32
    ).astype(jnp.bfloat16)
    grad_slots = jnp.einsum(
        "ts,td->sd", place_round, out_grad, preferred_element_type=jnp.float32
    ).astype(jnp.bfloat16)
    gate_slots = jnp.sum(
        place_first * combine[:, 0:1] + place_second * combine[:, 1:2], axis=0
    ).astype(jnp.bfloat16)
    token_send = jnp.repeat(token_slots.reshape(window, CAP, model_width), SPLIT, axis=0)
    grad_send = jnp.repeat(grad_slots.reshape(window, CAP, model_width), SPLIT, axis=0)
    gate_send = jnp.repeat(gate_slots.reshape(window, CAP), SPLIT, axis=0)
    token_recv, grad_recv, gate_recv = (
        lax.all_to_all(token_send, "expert", split_axis=0, concat_axis=0, tiled=True),
        lax.all_to_all(grad_send, "expert", split_axis=0, concat_axis=0, tiled=True),
        lax.all_to_all(gate_send, "expert", split_axis=0, concat_axis=0, tiled=True),
    )
    row_count = expert_count * CAP
    token_rows = token_recv.reshape(row_count, model_width)
    grad_rows = grad_recv.reshape(row_count, model_width)
    gate_rows = gate_recv.reshape(row_count)
    w_in_local = w_in[0]
    w_out_local = w_out[0]
    sum_in, sum_out, row_parts, gate_parts = expert_rows(
        w_in_local,
        w_out_local,
        (
            lax.all_gather(token_rows, "group", axis=0, tiled=True),
            lax.all_gather(grad_rows, "group", axis=0, tiled=True),
            lax.all_gather(gate_rows, "group", axis=0, tiled=True),
        ),
    )
    w_in_grad = sum_in.astype(jnp.bfloat16)[None]
    w_out_grad = sum_out.astype(jnp.bfloat16)[None]
    row_sums = lax.psum_scatter(
        row_parts.astype(jnp.bfloat16), "group", scatter_dimension=0, tiled=True
    ).astype(jnp.float32)
    gate_sums = lax.psum_scatter(gate_parts, "group", scatter_dimension=0, tiled=True)
    rows_back, gates_back = (
        lax.all_to_all(
            row_sums.reshape(expert_count, CAP, model_width).astype(jnp.bfloat16),
            "expert",
            split_axis=0,
            concat_axis=0,
            tiled=True,
        ).astype(jnp.float32),
        lax.all_to_all(
            gate_sums.reshape(expert_count, CAP).astype(jnp.bfloat16),
            "expert",
            split_axis=0,
            concat_axis=0,
            tiled=True,
        ).astype(jnp.float32),
    )
    rows_back = jnp.sum(rows_back.reshape(window, SPLIT, CAP, model_width), axis=1).reshape(
        slot_count, model_width
    )
    gates_back = jnp.sum(gates_back.reshape(window, SPLIT, CAP), axis=1).reshape(slot_count)
    expert_part = jnp.dot(placement, rows_back, precision=lax.Precision.HIGHEST)
    gate_first = jnp.sum(place_first * gates_back[None, :], axis=1)
    gate_second = jnp.sum(place_second * gates_back[None, :], axis=1)
    gate_slope = combine[:, 0] * combine[:, 1] * (gate_first - gate_second)
    logit_grad = first_hot * gate_slope[:, None] - second_hot * gate_slope[:, None]
    router_part = jnp.dot(
        logit_grad, router_full.astype(jnp.float32).T, precision=lax.Precision.HIGHEST
    )
    in_grad = (expert_part + router_part).astype(jnp.bfloat16)
    router_sum = jnp.dot(tokens.astype(jnp.float32).T, logit_grad, precision=lax.Precision.HIGHEST)
    router_grad = lax.psum_scatter(
        lax.psum_scatter(router_sum, "expert", scatter_dimension=1, tiled=True),
        "group",
        scatter_dimension=0,
        tiled=True,
    )
    return (in_grad, w_in_grad, w_out_grad, router_grad)


def iota(shape, axis):
    return lax.broadcasted_iota(jnp.int32, shape, axis)


def one_hot(mask):
    return jnp.where(mask, 1.0, 0.0).astype(F32)


def contract(left, right, left_axis, right_axis):
    return lax.dot_general(
        left, right, (((left_axis,), (right_axis,)), ((), ())), preferred_element_type=F32
    )


def choice_places(count, z, window, ids_ref, slots_ref, keep_ref):
    places = []
    for k in range(2):
        ids = ids_ref[k : k + 1, :]
        relative = jnp.where(ids < z, ids - z + window, ids - z)
        active = (keep_ref[k : k + 1, :] == 1) & (ids < window)
        code = jnp.where(active, relative * CAP + slots_ref[k : k + 1, :], -1)
        places.append(one_hot(iota((count, LANES), 0) == code))
    return places


def finish_kernel(
    window,
    g1_hbm,
    g2_hbm,
    returned_hbm,
    router_hbm,
    ids_hbm,
    slots_hbm,
    keep_hbm,
    in_grad_hbm,
    w_in_grad_hbm,
    w_out_grad_hbm,
    router_grad_hbm,
    g1,
    g2,
    router_grad,
    in_grad,
    returned_ref,
    ids_ref,
    slots_ref,
    keep_ref,
    sems,
    load_sems,
):
    parts = 4
    loads, stores = [], []
    for src, staged, dst, pieces in (
        (g1_hbm, g1, w_in_grad_hbm.at[0], parts),
        (ids_hbm, ids_ref, None, 1),
        (slots_hbm, slots_ref, None, 1),
        (keep_hbm, keep_ref, None, 1),
        (returned_hbm, returned_ref, None, 1),
        (router_hbm, router_grad, router_grad_hbm, 1),
        (g2_hbm, g2, w_out_grad_hbm.at[0], parts),
    ):
        step = src.shape[0] // pieces
        for p in range(pieces):
            span = pl.ds(p * step, step)
            whole = pieces == 1
            loads.append(
                pltpu.make_async_copy(
                    src if whole else src.at[span],
                    staged if whole else staged.at[span],
                    load_sems.at[len(loads)],
                )
            )
            if dst is not None:
                stores.append(
                    pltpu.make_async_copy(
                        staged if whole else staged.at[span],
                        dst if whole else dst.at[span],
                        sems.at[len(stores)],
                    )
                )
    for load in loads:
        load.start()
    rows = window * CAP
    chunks = in_grad.shape[1] // LANES
    back = chunks * rows
    row = iota((back, back), 0)
    source = ((row >> 1) & (window - 1)) * 16 + (row >> 3) * CAP + (row & 1)
    unfold = one_hot(iota((back, back), 1) == source).astype(BF16)
    z = lax.axis_index("expert") // SPLIT
    for load, store in zip(loads[:parts], stores):
        load.wait()
        store.start()
    for load in loads[parts : parts + 3]:
        load.wait()
    places = choice_places(LANES, z, window, ids_ref, slots_ref, keep_ref)
    spread_back = jnp.transpose(places[0] + places[1]).astype(BF16)
    loads[parts + 3].wait()
    flat = contract(unfold, returned_ref[...].reshape(back, LANES), 1, 0)
    returned = jnp.concatenate(
        [flat[c * rows : (c + 1) * rows] for c in range(chunks)], axis=1
    )
    returned = jnp.concatenate(
        [returned, jnp.zeros((LANES - rows, chunks * LANES), F32)], axis=0
    ).astype(BF16)
    for load, store in zip(loads[parts + 4 :], stores[parts:]):
        load.wait()
        store.start()
    in_grad[...] = contract(spread_back, returned, 1, 0).astype(BF16)
    stores.append(pltpu.make_async_copy(in_grad, in_grad_hbm, sems.at[len(stores)]))
    stores[-1].start()
    for store in stores:
        store.wait()


def fused_kernel(
    window,
    groups,
    tokens_hbm,
    out_grad_hbm,
    router_hbm,
    w_in_hbm,
    w_out_hbm,
    ids_hbm,
    slots_hbm,
    keep_hbm,
    g1_out,
    g2_out,
    returned_out,
    router_grad_out,
    ids_ref,
    slots_ref,
    keep_ref,
    tok,
    outg,
    w1,
    w2,
    g1,
    g2,
    router_grad_ref,
    z_send,
    z_recv,
    w_recv,
    x_pack,
    dy_pack,
    xs,
    gaps,
    diff_send,
    diff_recv,
    gg,
    rp_send,
    rp_recv,
    coef_ref,
    rg_send,
    rg_recv,
    ret_send,
    ret_recv,
    load_sems,
    store_sems,
    zs,
    ws,
    xps,
    dps,
    gps,
    dfs,
    ggs,
    rps,
    rgs,
    rts,
):
    plane = SPLIT * groups
    width = tok.shape[1]
    chunks = width // LANES
    rows = window * CAP
    message = z_send.shape[1]
    used = CAP * (2 * chunks + 1)
    columns, depth = router_hbm.shape
    ix = lax.axis_index("expert")
    g = lax.axis_index("group")
    z = ix // SPLIT
    y = lax.rem(ix, SPLIT)
    q = y * groups + g

    def z_up(d):
        return (lax.rem(z + d, window) * SPLIT + y, g)

    def z_down(d):
        return (lax.rem(z + window - d, window) * SPLIT + y, g)

    def in_plane(p):
        return (z * SPLIT + p // groups, lax.rem(p, groups))

    def q_up(d):
        return lax.rem(q + d, plane)

    def q_down(d):
        return lax.rem(q + plane - d, plane)

    def remote(src, dst, sems, target):
        return pltpu.make_async_remote_copy(
            src_ref=src,
            dst_ref=dst,
            send_sem=sems.at[0],
            recv_sem=sems.at[1],
            device_id=target,
            device_id_type=MESH,
        )

    def along_z(src, dst, sems, target_of):
        for d in range(1, window):
            remote(src(d), dst.at[d], sems, target_of(d)).start()
        every = dst.at[pl.ds(1, window - 1)]
        return remote(every, every, sems, target_of(1))

    def all_plane(src, dst, sems):
        for d in range(1, plane):
            target = q_up(d)
            remote(src(target), dst.at[q], sems, in_plane(target)).start()
        every = dst.at[pl.ds(0, plane - 1)]
        return remote(every, every, sems, in_plane(q_up(1)))

    loads = [
        pltpu.make_async_copy(src, dst, load_sems.at[i])
        for i, (src, dst) in enumerate(
            [
                (ids_hbm, ids_ref),
                (slots_hbm, slots_ref),
                (keep_hbm, keep_ref),
                (tokens_hbm, tok),
                (out_grad_hbm, outg),
                (router_hbm, w_recv.at[0]),
                (w_in_hbm.at[0], w1),
                (w_out_hbm.at[0], w2),
            ]
        )
    ]
    for load in loads[:5]:
        load.start()
    barrier = pltpu.get_barrier_semaphore()
    for d in range(1, window):
        pl.semaphore_signal(barrier, inc=1, device_id=z_up(d), device_id_type=MESH)
    for d in range(1, plane):
        pl.semaphore_signal(barrier, inc=1, device_id=in_plane(q_up(d)), device_id_type=MESH)

    for load in loads[5:]:
        load.start()

    depth_f = (2 * chunks + 2) * rows
    spread = []
    for d in range(window):
        row = iota((message, depth_f), 0)
        source = (row >> 1) * rows + d * CAP + (row & 1)
        spread.append(one_hot((iota((message, depth_f), 1) == source) & (row < used)))
    spread = jnp.concatenate(spread, axis=0).astype(BF16)
    half = width // 2
    side = chunks // 2
    wide = (chunks + 1) * 16
    row = iota((wide, window * message), 0)
    inner = row & 15
    column = row >> 4
    upper = jnp.where(inner < rows, 0, side)
    block = jnp.where(
        column < side,
        column + upper,
        jnp.where(column == side, 2 * chunks, chunks + column - side - 1 + upper),
    )
    source = ((inner & (rows - 1)) >> 1) * message + block * CAP + (inner & 1)
    gather = one_hot(iota((wide, window * message), 1) == source).astype(BF16)

    for load in loads[:3]:
        load.wait()
    places = choice_places(16, z, window, ids_ref, slots_ref, keep_ref)
    place = places[0] + places[1]
    place_rows = place.astype(BF16)
    short = place[:rows]
    first_id = jnp.sum(short * ids_ref[0:1, :].astype(F32), axis=1, keepdims=True)
    second_id = jnp.sum(short * ids_ref[1:2, :].astype(F32), axis=1, keepdims=True)
    which = jnp.sum(places[0][:rows] - places[1][:rows], axis=1, keepdims=True)
    lane = iota((rows, LANES), 1)
    meta = jnp.where(
        lane == 0, first_id, jnp.where(lane == 1, second_id, jnp.where(lane == 2, which, 0.0))
    )

    loads[3].wait()
    loads[4].wait()
    x_slots = contract(place_rows, tok[...], 1, 0)[:rows]
    dy_slots = contract(place_rows, outg[...], 1, 0)[:rows]
    pieces = [x_slots[:, c * LANES : (c + 1) * LANES] for c in range(chunks)]
    pieces += [dy_slots[:, c * LANES : (c + 1) * LANES] for c in range(chunks)]
    pieces += [meta, jnp.zeros((rows, LANES), F32)]
    folded = jnp.concatenate(pieces, axis=0).astype(BF16)
    messages = contract(spread, folded, 1, 0).astype(BF16)
    z_recv[0] = messages[:message]
    for d in range(1, window):
        z_send[d] = messages[d * message : (d + 1) * message]
    pl.semaphore_wait(barrier, window - 1 + plane - 1)

    z_all = along_z(lambda d: z_send.at[d], z_recv, zs, z_up)
    total = plane * rows
    eye = iota((total, LANES), 0) == iota((total, LANES), 1)
    column = iota((1, window * columns), 1)
    owner = lax.rem(z + window - column // columns, window)
    column_id = ((owner * SPLIT + y) * columns + lax.rem(column, columns)).astype(F32)
    loads[5].wait()
    w_all = along_z(lambda d: w_recv.at[0], w_recv, ws, z_up)
    z_all.wait_recv()
    arrived = z_recv[...].reshape(window * message, LANES)
    x_blocks = (side + 1) * 16
    gathered = contract(gather[:x_blocks], arrived, 1, 0).astype(BF16)
    for c in range(side + 1):
        x_pack[q, :, c * LANES : (c + 1) * LANES] = gathered[c * 16 : (c + 1) * 16]
    xp_all = all_plane(lambda p: x_pack.at[q], x_pack, xps)
    gathered = contract(gather[x_blocks:], arrived, 1, 0).astype(BF16)
    for c in range(side):
        dy_pack[q, :, c * LANES : (c + 1) * LANES] = gathered[c * 16 : (c + 1) * 16]
    dp_all = all_plane(lambda p: dy_pack.at[q], dy_pack, dps)

    def unfolded(block):
        return jnp.concatenate(
            [block[:, :rows, :half], block[:, rows:, :half]], axis=2
        ).reshape(plane * rows, width)

    z_all.wait_send()
    w_all.wait()
    router = w_recv[...].reshape(window * columns, depth)
    xp_all.wait_recv()

    packed = x_pack[...].astype(F32)
    x_rows = unfolded(packed).astype(BF16)
    info = packed[:, :rows, half:].reshape(total, LANES)
    xs[...] = x_rows
    x_part = xs[:, pl.ds(pl.multiple_of(g * depth, LANES), depth)]

    hot = one_hot(info[:, 0:1] == column_id) - one_hot(info[:, 1:2] == column_id)
    sign = info[:, 2:3]
    gap_part = jnp.sum(contract(x_part, router, 1, 1) * hot, axis=1, keepdims=True)
    gap_row = jnp.sum(jnp.where(eye, gap_part, 0.0), axis=0, keepdims=True)
    gaps[q] = jnp.broadcast_to(gap_row, (rows, LANES))
    gap_all = all_plane(lambda p: gaps.at[q], gaps, gps)
    row_diff = contract(hot.astype(BF16), router, 1, 0)
    diff_send[...] = row_diff.reshape(plane, rows, depth)
    diff_recv[q] = diff_send[q]
    diff_all = all_plane(lambda p: diff_send.at[p], diff_recv, dfs)

    loads[6].wait()
    pre_act = contract(x_rows, w1[...], 1, 0)
    loads[7].wait()
    dp_all.wait_recv()
    dy_rows = unfolded(dy_pack[...].astype(F32)).astype(BF16)
    back_up = contract(dy_rows, w2[...], 1, 1)
    gelu_value, gelu_slope = gelu_parts(pre_act)
    gate_part = jnp.sum(back_up * gelu_value, axis=1, keepdims=True)
    gate_row = jnp.sum(jnp.where(eye, gate_part, 0.0), axis=0, keepdims=True)
    gg[q] = jnp.broadcast_to(gate_row, (rows, LANES))
    gg_all = all_plane(lambda p: gg.at[q], gg, ggs)

    gap_all.wait_recv()
    gap_sum = jnp.sum(gaps[:, 0:1, :], axis=0)
    gap = jnp.sum(jnp.where(eye, gap_sum, 0.0), axis=1, keepdims=True)
    combine_first = jax.nn.sigmoid(gap)
    combine_second = jax.nn.sigmoid(-gap)
    gate = jnp.where(sign > 0.5, combine_first, jnp.where(sign < -0.5, combine_second, 0.0))
    gate = gate.astype(BF16).astype(F32)
    pre_grad = (gate * back_up * gelu_slope).astype(BF16)
    rp_all = []
    for h in range(2):
        part = contract(pre_grad, w1[h * half : (h + 1) * half, :], 1, 1)
        part = part.reshape(plane, rows, half)
        rp_send[h] = jnp.concatenate(
            [part[:, :, : half // 2], part[:, :, half // 2 :]], axis=1
        ).astype(BF16)
        rp_recv[h, q] = rp_send[h, q]
        rp_all.append(all_plane(lambda p, h=h: rp_send.at[h, p], rp_recv.at[h], rps.at[h]))

    gg_all.wait_recv()
    grad_sum = jnp.sum(gg[:, 0:1, :], axis=0)
    gate_grad = jnp.sum(jnp.where(eye, grad_sum, 0.0), axis=1, keepdims=True)
    coef = sign * combine_first * combine_second * gate_grad
    coef_ref[...] = jnp.broadcast_to(coef, (total, LANES))
    logit_grad = coef * hot
    high = logit_grad.astype(BF16)
    low = (logit_grad - high.astype(F32)).astype(BF16)
    router_part = contract(
        jnp.concatenate([high, low], axis=0), jnp.concatenate([x_part, x_part], axis=0), 0, 0
    )
    for d in range(1, window):
        rg_send[d] = router_part[d * columns : (d + 1) * columns].astype(BF16)
    rg_all = along_z(lambda d: rg_send.at[d], rg_recv, rgs, z_down)

    diff_all.wait_recv()
    diffs = []
    for part in range(groups):
        diff = diff_recv[part]
        for other in range(1, SPLIT):
            diff = diff + diff_recv[other * groups + part]
        diffs.append(diff)
    own_coef = coef_ref[pl.ds(pl.multiple_of(q * rows, rows), rows), 0:1]
    router_rows = own_coef * jnp.concatenate(diffs, axis=1)
    back = chunks * rows
    row = iota((back, back), 0)
    source = ((row >> 1) & (chunks - 1)) * rows + (row >> 4) * CAP + (row & 1)
    fold = one_hot(iota((back, back), 1) == source).astype(BF16)

    stores = []

    def weight_grad(left, right, staged, target):
        parts = 4
        step = staged.shape[0] // parts
        for p in range(parts):
            span = slice(p * step, (p + 1) * step)
            staged[span] = contract(left[:, span], right, 0, 0).astype(BF16)
            stores.append(
                pltpu.make_async_copy(
                    staged.at[span], target.at[span], store_sems.at[len(stores)]
                )
            )
            stores[-1].start()

    weight_grad(x_rows, pre_grad, g1, g1_out)
    for sent in (xp_all, dp_all, gap_all, diff_all, gg_all):
        sent.wait_send()
    halves = []
    for h in range(2):
        rp_all[h].wait_recv()
        summed = jnp.sum(rp_recv[h].astype(F32), axis=0)
        halves += [summed[:rows], summed[rows:]]
    row_grad = jnp.concatenate(halves, axis=1)
    row_grad = row_grad + router_rows
    folded = jnp.concatenate(
        [row_grad[:, c * LANES : (c + 1) * LANES] for c in range(chunks)], axis=0
    ).astype(BF16)
    ret_send[...] = contract(fold, folded, 1, 0).astype(BF16).reshape(ret_send.shape)
    ret_recv[0] = ret_send[0]
    ret_all = along_z(lambda d: ret_send.at[d], ret_recv, rts, z_down)

    rg_all.wait_recv()
    router_grad_ref[...] = router_part[:columns] + jnp.sum(
        rg_recv[1:].astype(F32), axis=0
    )
    stores.append(
        pltpu.make_async_copy(router_grad_ref, router_grad_out, store_sems.at[len(stores)])
    )
    stores[-1].start()
    scaled_grad = (gate * dy_rows.astype(F32)).astype(BF16)
    weight_grad(gelu_value.astype(BF16), scaled_grad, g2, g2_out)
    for sent in (*rp_all, rg_all):
        sent.wait_send()
    ret_all.wait_recv()
    stores.append(
        pltpu.make_async_copy(ret_recv, returned_out, store_sems.at[len(stores)])
    )
    stores[-1].start()
    ret_all.wait_send()
    for store in stores:
        store.wait()


def fused(tokens, out_grad, w_router, w_in, w_out, expert_ids, slot_ids, keep_mask):
    window = lax.axis_size("expert") // SPLIT
    groups = lax.axis_size("group")
    plane = SPLIT * groups
    count, width = tokens.shape
    hidden = w_in.shape[2]
    depth, columns = w_router.shape
    rows = window * CAP
    message = -(-CAP * (2 * width // LANES + 1) // 16) * 16
    hbm = pl.BlockSpec(memory_space=pltpu.HBM)
    dma = pltpu.SemaphoreType.DMA
    routing = (expert_ids.T, slot_ids.T, keep_mask.T)
    g1, g2, returned, router_part = pl.pallas_call(
        functools.partial(fused_kernel, window, groups),
        out_shape=(
            jax.ShapeDtypeStruct((width, hidden), BF16),
            jax.ShapeDtypeStruct((hidden, width), BF16),
            jax.ShapeDtypeStruct((window, 16, LANES), BF16),
            jax.ShapeDtypeStruct((columns, depth), F32),
        ),
        in_specs=[hbm] * 8,
        out_specs=(hbm, hbm, hbm, hbm),
        scratch_shapes=[
            pltpu.VMEM(expert_ids.shape[::-1], jnp.int32),
            pltpu.VMEM(slot_ids.shape[::-1], jnp.int32),
            pltpu.VMEM(keep_mask.shape[::-1], jnp.int32),
            pltpu.VMEM((count, width), BF16),
            pltpu.VMEM((count, width), BF16),
            pltpu.VMEM((width, hidden), BF16),
            pltpu.VMEM((hidden, width), BF16),
            pltpu.VMEM((width, hidden), BF16),
            pltpu.VMEM((hidden, width), BF16),
            pltpu.VMEM((columns, depth), F32),
            pltpu.VMEM((window, message, LANES), BF16),
            pltpu.VMEM((window, message, LANES), BF16),
            pltpu.VMEM((window, columns, depth), BF16),
            pltpu.VMEM((plane, 16, width // 2 + LANES), BF16),
            pltpu.VMEM((plane, 16, width // 2), BF16),
            pltpu.VMEM((plane * rows, width), BF16),
            pltpu.VMEM((plane, rows, LANES), F32),
            pltpu.VMEM((plane, rows, depth), F32),
            pltpu.VMEM((plane, rows, depth), F32),
            pltpu.VMEM((plane, rows, LANES), F32),
            pltpu.VMEM((2, plane, 16, width // 4), BF16),
            pltpu.VMEM((2, plane, 16, width // 4), BF16),
            pltpu.VMEM((plane * rows, LANES), F32),
            pltpu.VMEM((window, columns, depth), BF16),
            pltpu.VMEM((window, columns, depth), BF16),
            pltpu.VMEM((window, 16, LANES), BF16),
            pltpu.VMEM((window, 16, LANES), BF16),
            dma((8,)),
            dma((10,)),
        ]
        + [dma((2,))] * 7
        + [dma((2, 2))]
        + [dma((2,))] * 2,
        compiler_params=pltpu.CompilerParams(
            collective_id=0, has_side_effects=True, vmem_limit_bytes=60 * 1024 * 1024
        ),
    )(
        tokens,
        out_grad,
        w_router.T,
        w_in,
        w_out,
        *routing,
    )
    in_grad, w_in_grad, w_out_grad, router_grad = pl.pallas_call(
        functools.partial(finish_kernel, window),
        out_shape=(
            jax.ShapeDtypeStruct((count, width), BF16),
            jax.ShapeDtypeStruct(w_in.shape, BF16),
            jax.ShapeDtypeStruct(w_out.shape, BF16),
            jax.ShapeDtypeStruct((columns, depth), F32),
        ),
        in_specs=[hbm] * 7,
        out_specs=(hbm, hbm, hbm, hbm),
        scratch_shapes=[
            pltpu.VMEM((width, hidden), BF16),
            pltpu.VMEM((hidden, width), BF16),
            pltpu.VMEM((columns, depth), F32),
            pltpu.VMEM((count, width), BF16),
            pltpu.VMEM((window, 16, LANES), BF16),
            pltpu.VMEM(expert_ids.shape[::-1], jnp.int32),
            pltpu.VMEM(slot_ids.shape[::-1], jnp.int32),
            pltpu.VMEM(keep_mask.shape[::-1], jnp.int32),
            dma((10,)),
            dma((13,)),
        ],
        compiler_params=pltpu.CompilerParams(vmem_limit_bytes=60 * 1024 * 1024),
    )(g1, g2, returned, router_part, *routing)
    return (in_grad, w_in_grad, w_out_grad, router_grad.T)


def body(*args):
    tokens, _, w_router = args[:3]
    window = lax.axis_size("expert") // SPLIT
    fits = (
        window * CAP == 8
        and w_router.shape[1] % 16 == 0
        and w_router.shape[0] % LANES == 0
        and window * w_router.shape[1] == LANES
        and SPLIT * lax.axis_size("group") * window * CAP <= LANES
        and tokens.shape == (LANES, 8 * LANES)
    )
    return fused(*args) if fits else gathered_body(*args)


def solution(mesh):
    return jax.shard_map(
        body,
        mesh=mesh,
        in_specs=(
            P(("expert", "group"), None),
            P(("expert", "group"), None),
            P("group", "expert"),
            P("expert", None, "group"),
            P("expert", "group", None),
            P(("expert", "group"), None),
            P(("expert", "group"), None),
            P(("expert", "group"), None),
        ),
        out_specs=(
            P(("expert", "group"), None),
            P("expert", None, "group"),
            P("expert", "group", None),
            P("group", "expert"),
        ),
        check_vma=False,
    )
```
